32 devices in a mesh: slab: 16 (over z, x, core), view: 2 (over y).
Axes of the slice: x: 2, y: 2, z: 4, core: 2. Of those that a mesh axis runs over, the one named last changes fastest.
Arguments:
- fine_volume: float32 [64, 4096], P('slab'), may hold values from 0 to 1
- coarse_volume: float32 [256, 4096], P('slab'), may hold values from 0 to 1
- fine_rays: bfloat16 [4, 4096, 128], P('view'), may hold values from -0.09375 to 0.09375
- coarse_rays: bfloat16 [4, 4096, 128], P('view'), may hold values from -0.09375 to 0.09375
- fine_axial: bfloat16 [4, 64, 128], P('view', 'slab'), may hold values from -0.4375 to 0.4375
- coarse_axial: bfloat16 [4, 256, 128], P('view', 'slab'), may hold values from -0.3125 to 0.3125
- measured: float32 [128, 4, 128], P('slab', 'view'), may hold values from 0 to 2
- ray_weight: float32 [128, 4, 128], P('slab', 'view'), may hold values from 0.25 to 0.5
- fine_cell_weight: float32 [64, 4096], P('slab'), may hold values from 0.3 to 0.6
- coarse_cell_weight: float32 [256, 4096], P('slab'), may hold values from 0.3 to 0.6
- margin_blocks: int32 [16, 8], P('slab'), may hold values from 0 to 31, as said below
- ray_hits: int32 [4, 16, 8], P('view', 'slab'), may hold values 0 or 1
Outputs:
- fine_result: float32 [64, 4096], P('slab')
- coarse_result: float32 [256, 4096], P('slab')
The draws below stay inside these ranges and needn't reach their ends.
Inputs may be any that keep to these rules, and one draw needn't show every extreme that they name: `margin_blocks`: each row lists 8 different block numbers.
All inputs are finite; a program needn't handle non-finite values. No bound on the sum of `ray_hits` on one device may be relied on, other than what follows from the above.
Results may differ from the reference program's by a relative error of at most 0.005.
Values may be sent and summed in bfloat16 or wider, within the bound.
No kernel may reach another device: no remote copies, remote signals or barrier semaphores. Data moves between devices by JAX's collectives and lax.ppermute only.
A program may use at most 64 MiB of HBM per device.

```python
import math
import jax
import jax.numpy as jnp

FXY = 4096
CXY = 4096
DET_U = 128
FZ_DEV = 4
VD = 2
ITERS = 3
TILES = 8
BLOCK = 128
OB = 8
CZ_DEV = 16
FZ = 64
CZ = 256
DET_W = 128
VIEWS = 4
N_SLAB = 16
N_VIEW = 2


def draw_margin_blocks(key, part):
    block_count = CXY // BLOCK
    scores = jax.random.randint(jax.random.fold_in(key, 17), (N_SLAB, block_count), 0, 1 << 20, dtype=jnp.int32)
    scores = scores * block_count + jnp.arange(block_count, dtype=jnp.int32)[None, :]
    order = jnp.argsort(scores, axis=1, stable=True).astype(jnp.int32)
    return order[:, :OB]


def with_ends(entries, key, low, top_value):
    shape = entries.shape
    place = [jax.random.randint(jax.random.fold_in(key, axis), (), 0, shape[axis]) for axis in range(len(shape))]
    entries = entries.at[tuple(place)].set(low)
    longest = shape.index(max(shape))
    place[longest] = (place[longest] + 1) % shape[longest]
    return entries.at[tuple(place)].set(top_value)


def block_scale(rng, dims, cuts, smallest, top_value):
    def one(dim, parts):
        steps = jax.random.uniform(jax.random.fold_in(jax.random.fold_in(rng, 6), dim), (parts,), jnp.float32, smallest / len(cuts), top_value / len(cuts))
        return jnp.repeat(jnp.exp(steps), dims[dim] // parts).reshape((-1,) + (1,) * (len(dims) - dim - 1))

    gain = one(*cuts[0])
    for cut in cuts[1:]:
        gain = gain * one(*cut)
    return gain


def bell_draw(stream_key, dims, spread, limit, split=(), held_as=jnp.bfloat16):
    array = jax.random.normal(stream_key, dims, jnp.float32) * spread
    if len(split) > 0:
        array = block_scale(stream_key, dims, split, -0.22, 0.18) * array
    return jnp.clip(array, min=-limit, max=limit).astype(held_as)


def setup_inputs(seed: int = 0) -> dict:
    key_of = jax.random.split(jax.random.key(seed), 13)
    fine_volume = jnp.clip(1.0 * jax.random.uniform(key_of[0], (FZ, FXY), jnp.float32) ** block_scale(key_of[0], (FZ, FXY), ((0, 16),), -0.2, 0.2), 0.0, 1.0)
    coarse_volume = jnp.clip(1.0 * jax.random.uniform(key_of[1], (CZ, CXY), jnp.float32) ** block_scale(key_of[1], (CZ, CXY), ((0, 16),), -0.2, 0.2), 0.0, 1.0)
    fine_rays = bell_draw(key_of[2], (VIEWS, FXY, DET_U), (FXY + DET_U) ** -0.5, 0.09375, ((0, 2),))
    coarse_rays = bell_draw(key_of[3], (VIEWS, CXY, DET_U), (CXY + DET_U) ** -0.5, 0.09375, ((0, 2),))
    fine_axial = bell_draw(key_of[4], (VIEWS, FZ, DET_W), (FZ + DET_W) ** -0.5, 0.4375, ((0, 2), (1, 16)))
    coarse_axial = bell_draw(key_of[5], (VIEWS, CZ, DET_W), (CZ + DET_W) ** -0.5, 0.3125, ((0, 2), (1, 16)))
    measured = jnp.clip(2.0 * jax.random.uniform(key_of[6], (DET_W, VIEWS, DET_U), jnp.float32) ** block_scale(key_of[6], (DET_W, VIEWS, DET_U), ((0, 16), (1, 2)), -0.2, 0.2), 0.0, 2.0)
    ray_weight = jnp.clip(jnp.exp(math.log(0.5) - 0.6931472 * jax.random.uniform(key_of[7], (DET_W, VIEWS, DET_U), jnp.float32) ** block_scale(key_of[7], (DET_W, VIEWS, DET_U), ((0, 16), (1, 2)), -0.2, 0.2)), 0.25, 0.5)
    fine_cell_weight = jnp.clip(jnp.exp(math.log(0.6) - 0.6931472 * jax.random.uniform(key_of[8], (FZ, FXY), jnp.float32) ** block_scale(key_of[8], (FZ, FXY), ((0, 16),), -0.2, 0.2)), 0.3, 0.6)
    coarse_cell_weight = jnp.clip(jnp.exp(math.log(0.6) - 0.6931472 * jax.random.uniform(key_of[9], (CZ, CXY), jnp.float32) ** block_scale(key_of[9], (CZ, CXY), ((0, 16),), -0.2, 0.2)), 0.3, 0.6)
    margin_blocks = draw_margin_blocks(jax.random.fold_in(key_of[12], 71), 0)
    ray_hits = with_ends((jax.random.randint(key_of[11], (VIEWS, N_SLAB, TILES), 0, 4) < 3).astype(jnp.int32), jax.random.fold_in(key_of[11], 1), 0, 1)
    return {"fine_volume": fine_volume, "coarse_volume": coarse_volume, "fine_rays": fine_rays, "coarse_rays": coarse_rays, "fine_axial": fine_axial, "coarse_axial": coarse_axial, "measured": measured, "ray_weight": ray_weight, "fine_cell_weight": fine_cell_weight, "coarse_cell_weight": coarse_cell_weight, "margin_blocks": margin_blocks, "ray_hits": ray_hits}


def reference(fine_volume, coarse_volume, fine_rays, coarse_rays, fine_axial, coarse_axial, measured, ray_weight, fine_cell_weight, coarse_cell_weight, margin_blocks, ray_hits):
    block_ids = jnp.arange(CXY, dtype=jnp.int32) // BLOCK
    listed = jnp.any(margin_blocks[:, :, None] == block_ids[None, None, :], axis=1)
    keep_mask = jnp.repeat(jnp.where(listed, 0.0, 1.0).astype(jnp.float32), CZ_DEV, axis=0)
    hit_rows = jnp.repeat(ray_hits, DET_W // TILES, axis=2)
    fine_hit = jnp.repeat(hit_rows, FZ_DEV, axis=1).astype(jnp.bfloat16)
    coarse_hit = jnp.repeat(hit_rows, CZ_DEV, axis=1).astype(jnp.bfloat16)
    fine_depth = (fine_axial * fine_hit).astype(jnp.float32)
    coarse_depth = (coarse_axial * coarse_hit).astype(jnp.float32)
    fine_footprint = fine_rays.astype(jnp.float32)
    coarse_footprint = coarse_rays.astype(jnp.float32)
    fine = fine_volume
    coarse = coarse_volume * keep_mask
    for iteration in range(ITERS):
        fine_moment = jnp.einsum('zx,vxu->vzu', fine.astype(jnp.bfloat16).astype(jnp.float32), fine_footprint).astype(jnp.bfloat16).astype(jnp.float32)
        coarse_moment = jnp.einsum('zx,vxu->vzu', coarse.astype(jnp.bfloat16).astype(jnp.float32), coarse_footprint).astype(jnp.bfloat16).astype(jnp.float32)
        projection = jnp.einsum('vzw,vzu->wvu', fine_depth, fine_moment) + jnp.einsum('vzw,vzu->wvu', coarse_depth, coarse_moment)
        residual = (ray_weight * (measured - projection)).astype(jnp.bfloat16).astype(jnp.float32)
        fine_spread = jnp.einsum('vzw,wvu->vzu', fine_depth, residual).astype(jnp.bfloat16).astype(jnp.float32)
        coarse_spread = jnp.einsum('vzw,wvu->vzu', coarse_depth, residual).astype(jnp.bfloat16).astype(jnp.float32)
        fine_group = jnp.einsum('gvzu,gvxu->gzx', fine_spread.reshape(N_VIEW, VD, FZ, DET_U), fine_footprint.reshape(N_VIEW, VD, FXY, DET_U))
        coarse_group = jnp.einsum('gvzu,gvxu->gzx', coarse_spread.reshape(N_VIEW, VD, CZ, DET_U), coarse_footprint.reshape(N_VIEW, VD, CXY, DET_U))
        fine_back = jnp.sum(fine_group.astype(jnp.bfloat16).astype(jnp.float32), axis=0)
        coarse_back = jnp.sum(coarse_group.astype(jnp.bfloat16).astype(jnp.float32), axis=0)
        fine = fine + fine_cell_weight * fine_back
        coarse = (coarse + coarse_cell_weight * coarse_back) * keep_mask
    return fine, coarse
```

```python
import jax
import jax.numpy as jnp
from jax import lax
from jax.sharding import PartitionSpec as P

ITERS = 3
BLOCK = 128


def swap(value, axis, size, bit):
    return lax.ppermute(value, axis, [(i, i ^ bit) for i in range(size)])


def bits_of(size):
    return [1 << k for k in range(size.bit_length() - 1)]


def pair_sum(value, axis, size):
    for bit in bits_of(size):
        value = value + swap(value, axis, size, bit)
    return value


def pair_gather(value, axis, size):
    me = lax.axis_index(axis)
    for bit in bits_of(size):
        other = swap(value, axis, size, bit)
        upper = (me & bit) != 0
        value = jnp.where(
            upper, jnp.concatenate([other, value]), jnp.concatenate([value, other])
        )
    return value


def make_body(slabs, groups):
    def body(
        fine_volume,
        coarse_volume,
        fine_rays,
        coarse_rays,
        fine_axial,
        coarse_axial,
        measured,
        ray_weight,
        fine_cell_weight,
        coarse_cell_weight,
        margin_blocks,
        ray_hits,
    ):
        view_count = fine_rays.shape[0]
        detector_rows = fine_axial.shape[2]
        tile_count = ray_hits.shape[2]
        coarse_cells = coarse_volume.shape[1]
        block_ids = jnp.arange(coarse_cells, dtype=jnp.int32) // BLOCK
        listed = jnp.any(margin_blocks[0][:, None] == block_ids[None, :], axis=0)
        keep_mask = jnp.where(listed, 0.0, 1.0).astype(jnp.float32)[None, :]
        hit_rows = jnp.broadcast_to(
            ray_hits[:, 0, :, None], (view_count, tile_count, detector_rows // tile_count)
        )
        hit_rows = hit_rows.reshape(view_count, detector_rows).astype(jnp.bfloat16)
        fine_depth = fine_axial * hit_rows[:, None, :]
        coarse_depth = coarse_axial * hit_rows[:, None, :]
        fine_rows = fine_volume.shape[0]
        fine = fine_volume
        coarse = coarse_volume * keep_mask
        gathered = pair_gather(jnp.stack([measured, ray_weight], axis=1), "slab", slabs)
        whole_measured, whole_weight = gathered[:, 0], gathered[:, 1]
        for iteration in range(ITERS):
            fine_moment = jnp.einsum(
                "zx,vxu->vzu",
                fine.astype(jnp.bfloat16),
                fine_rays,
                preferred_element_type=jnp.float32,
            ).astype(jnp.bfloat16)
            coarse_moment = jnp.einsum(
                "zx,vxu->vzu",
                coarse.astype(jnp.bfloat16),
                coarse_rays,
                preferred_element_type=jnp.float32,
            ).astype(jnp.bfloat16)
            total = jnp.einsum(
                "vzw,vzu->wvu", fine_depth, fine_moment, preferred_element_type=jnp.float32
            ) + jnp.einsum(
                "vzw,vzu->wvu", coarse_depth, coarse_moment, preferred_element_type=jnp.float32
            )
            projection = pair_sum(total.astype(jnp.bfloat16), "slab", slabs).astype(jnp.float32)
            residual = (whole_weight * (whole_measured - projection)).astype(jnp.bfloat16)
            fine_spread = jnp.einsum(
                "vzw,wvu->vzu", fine_depth, residual, preferred_element_type=jnp.float32
            ).astype(jnp.bfloat16)
            coarse_spread = jnp.einsum(
                "vzw,wvu->vzu", coarse_depth, residual, preferred_element_type=jnp.float32
            ).astype(jnp.bfloat16)
            fine_term = jnp.einsum(
                "vzu,vxu->zx", fine_spread, fine_rays, preferred_element_type=jnp.float32
            ).astype(jnp.bfloat16)
            coarse_term = jnp.einsum(
                "vzu,vxu->zx", coarse_spread, coarse_rays, preferred_element_type=jnp.float32
            ).astype(jnp.bfloat16)
            term = jnp.concatenate([fine_term, coarse_term])
            back = pair_sum(term, "view", groups).astype(jnp.float32)
            fine = fine + fine_cell_weight * back[:fine_rows]
            coarse = (coarse + coarse_cell_weight * back[fine_rows:]) * keep_mask
        return (fine, coarse)

    return body


def solution(mesh):
    return jax.shard_map(
        make_body(mesh.shape["slab"], mesh.shape["view"]),
        mesh=mesh,
        in_specs=(
            P("slab", None),
            P("slab", None),
            P("view", None, None),
            P("view", None, None),
            P("view", "slab", None),
            P("view", "slab", None),
            P("slab", "view", None),
            P("slab", "view", None),
            P("slab", None),
            P("slab", None),
            P("slab", None),
            P("view", "slab", None),
        ),
        out_specs=(P("slab", None), P("slab", None)),
        check_vma=False,
    )
```

```python
import functools
import jax
import jax.numpy as jnp
from jax import lax
from jax.experimental import pallas as pl
from jax.experimental.pallas import tpu as pltpu
from jax.sharding import PartitionSpec as P

BLOCK = 128
PACK = 16
F32 = jnp.float32
BF16 = jnp.bfloat16
PARAMS = pltpu.CompilerParams(vmem_limit_bytes=24 * 1024 * 1024)
VMEM = pl.BlockSpec(memory_space=pltpu.VMEM)
SMEM = pl.BlockSpec(memory_space=pltpu.SMEM)
HBM = pl.BlockSpec(memory_space=pltpu.HBM)
QUICK = pl.CostEstimate(flops=1, bytes_accessed=1, transcendentals=0)


def fetch(source, target, sem):
    copy = pltpu.make_async_copy(source, target, sem)
    copy.start()
    return copy


def swap(value, axis, size, bits):
    return lax.ppermute(value, axis, [(i, i ^ bits) for i in range(size)])


def dot(a, b, dims):
    return lax.dot_general(a, b, (dims, ((), ())), preferred_element_type=F32)


def keep_row(blocks_ref, start, width):
    ids = (lax.broadcasted_iota(jnp.int32, (1, width), 1) + start) // BLOCK
    keep = jnp.ones((1, width), F32)
    for k in range(blocks_ref.shape[1]):
        keep = jnp.where(ids == blocks_ref[0, k], 0.0, keep)
    return keep


def prepare_kernel(
    fine_rays,
    coarse_rays,
    fine_weight_in,
    coarse_weight_in,
    fine_axial_in,
    coarse_axial_in,
    ray_weight_in,
    blocks,
    hits,
    rays,
    mine,
    theirs,
    rows,
    fine_weight,
    coarse_weight,
    fine_axial,
    coarse_axial,
    ray_weight,
    sems,
):
    core = lax.axis_index("slab") % 2
    half = coarse_weight.shape[1] // 2
    cut = pl.ds(pl.multiple_of(core * half, half), half)
    copies = [
        fetch(source, target, sems.at[i])
        for i, (source, target) in enumerate(
            (
                (fine_weight_in, fine_weight),
                (coarse_weight_in, coarse_weight),
                (fine_axial_in, fine_axial),
                (coarse_axial_in, coarse_axial),
                (ray_weight_in, ray_weight),
                (fine_rays.at[:, cut, :], rays.at[0]),
                (coarse_rays.at[:, cut, :], rays.at[1]),
            )
        )
    ]
    for copy in copies[:5]:
        copy.wait()
    fz = fine_weight.shape[0]
    parts = PACK // fz
    width = half // parts
    for out, side in ((mine, core), (theirs, 1 - core)):
        start = pl.multiple_of(side * half, half)
        keep = keep_row(blocks, start, half)
        out[:, :half] = (coarse_weight[:, pl.ds(start, half)] * keep).astype(BF16)
        fine = fine_weight[:, pl.ds(start, half)]
        pieces = [
            fine[i : i + 1, k * width : (k + 1) * width] for i in range(fz) for k in range(parts)
        ]
        out[:, half:] = jnp.concatenate(pieces, axis=0).astype(BF16)
    views, _, det = fine_axial.shape
    columns = ray_weight.shape[2]
    tiles = hits.shape[2]
    tile = lax.broadcasted_iota(jnp.int32, (1, det), 1) // (det // tiles)
    span = views * det
    own = ray_weight.shape[0]
    rows[...] = jnp.zeros(rows.shape, BF16)
    side = []
    for v in range(views):
        hit = jnp.zeros((1, det), F32)
        for t in range(tiles):
            hit = jnp.where(tile == t, hits[v, 0, t].astype(F32), hit)
        rows[:, v * det : (v + 1) * det] = (coarse_axial[v].astype(F32) * hit).astype(BF16)
        side.append(fine_axial[v].astype(F32) * hit)
    wide = rows.shape[1] - span
    weight = jnp.concatenate([ray_weight[:, v, :] for v in range(views)], axis=1)
    fine = jnp.concatenate(side, axis=1)
    if wide > weight.shape[1]:
        weight = jnp.concatenate([weight, jnp.zeros((own, wide - weight.shape[1]), F32)], axis=1)
    if wide > span:
        fine = jnp.concatenate([fine, jnp.zeros((fz, wide - span), F32)], axis=1)
    stack = [weight, fine]
    if own + fz < PACK:
        stack.append(jnp.zeros((PACK - own - fz, wide), F32))
    rows[:, span:] = jnp.concatenate(stack, axis=0).astype(BF16)
    for copy in copies[5:]:
        copy.wait()


def forward_kernel(
    fine_in,
    coarse_in,
    fine_rays_in,
    coarse_rays_in,
    measured_in,
    rows,
    blocks,
    out,
    fine,
    coarse,
    fine_rays,
    coarse_rays,
    measured,
    sems,
):
    steps = sems.shape[0] - 1
    fz, cells = fine.shape
    chunk = cells // steps
    views, _, columns = fine_rays.shape
    given_copy = fetch(measured_in, measured, sems.at[steps, 0])
    copies = []
    for i in range(steps):
        cut = pl.ds(i * chunk, chunk)
        copies.append(
            [
                fetch(fine_in.at[:, cut], fine.at[:, cut], sems.at[i, 0]),
                fetch(fine_rays_in.at[:, cut, :], fine_rays.at[:, cut, :], sems.at[i, 1]),
                fetch(coarse_in.at[:, cut], coarse.at[:, cut], sems.at[i, 2]),
                fetch(coarse_rays_in.at[:, cut, :], coarse_rays.at[:, cut, :], sems.at[i, 3]),
            ]
        )
    fine_sum = coarse_sum = None
    for i in range(steps):
        cut = slice(i * chunk, (i + 1) * chunk)
        for copy in copies[i]:
            copy.wait()
        keep = keep_row(blocks, i * chunk, chunk)
        fine_rows = fine[:, cut].astype(BF16)
        coarse_rows = (coarse[:, cut] * keep).astype(BF16)
        fine_wide = jnp.concatenate([fine_rays[v, cut, :] for v in range(views)], axis=1)
        coarse_wide = jnp.concatenate([coarse_rays[v, cut, :] for v in range(views)], axis=1)
        fine_part = dot(fine_rows, fine_wide, ((1,), (0,)))
        coarse_part = dot(coarse_rows, coarse_wide, ((1,), (0,)))
        fine_sum = fine_part if fine_sum is None else fine_sum + fine_part
        coarse_sum = coarse_part if coarse_sum is None else coarse_sum + coarse_part
    given_copy.wait()
    own = measured.shape[0]
    det = out.shape[0]
    span = views * det
    total = views * columns
    stack = [jnp.zeros((own, total), F32), fine_sum]
    if own + fz < PACK:
        stack.append(jnp.zeros((PACK - own - fz, total), F32))
    moment = jnp.concatenate([coarse_sum] + stack, axis=0).astype(BF16)
    start = lax.axis_index("slab") * own
    row = lax.broadcasted_iota(jnp.int32, (det, columns), 0) - start
    for v in range(views):
        depth = jnp.concatenate(
            [
                rows[:, v * det : (v + 1) * det],
                rows[:, span + v * det : span + (v + 1) * det],
            ],
            axis=0,
        )
        cut = slice(v * columns, (v + 1) * columns)
        projection = dot(depth, moment[:, cut], ((0,), (0,)))
        given = jnp.zeros((det, columns), F32)
        for i in range(own):
            given = jnp.where(row == i, measured[i : i + 1, v, :], given)
        out[:, cut] = given - projection


def unpack_rays(rows, groups, slabs, own, fz, det, total):
    core = lax.axis_index("slab") % 2
    me = lax.axis_index("slab")
    count = slabs * PACK
    half_groups = rows.shape[1]
    span = rows.shape[4] // 2
    shape = (slabs * own, count)
    w = lax.broadcasted_iota(jnp.int32, shape, 0)
    column = lax.broadcasted_iota(jnp.int32, shape, 1)
    block, row = column // PACK, column % PACK
    across, along = (block // 2) // (slabs // 4), (block // 2) % (slabs // 4)
    slab = ((me - core) ^ (across * 2 + along * 4)) + block % 2
    to_weight = jnp.where((row < own) & (w == slab * own + row), 1.0, 0.0).astype(BF16)
    shape = (slabs * fz, count)
    z = lax.broadcasted_iota(jnp.int32, shape, 0)
    column = lax.broadcasted_iota(jnp.int32, shape, 1)
    to_fine = jnp.where(column == (z // fz) * PACK + own + z % fz, 1.0, 0.0).astype(BF16)
    result = []
    for g in range(groups):
        one = rows[(g // half_groups) ^ core, g % half_groups]
        coarse = one[:, :, :span].reshape(count, span)
        side = one[:, :, span:].reshape(count, span)
        fine = dot(to_fine, side, ((1,), (0,))).astype(BF16)
        weight = dot(to_weight, side, ((1,), (0,)))[:, :total]
        result.append((coarse, fine, weight))
    return result


def residuals(q, deltas, weights, groups):
    current = [q[g] for g in range(groups)]
    results = [[weights[g] * current[g] for g in range(groups)]]
    for pair in deltas:
        current = [
            current[g] - (pair[0][g].astype(F32) + pair[1][g].astype(F32)) for g in range(groups)
        ]
        results.append([weights[g] * current[g] for g in range(groups)])
    return results


def in_two(value):
    high = value.astype(BF16)
    return high, (value - high.astype(F32)).astype(BF16)


def loop_kernel(slabs, groups, views, own, fz, rounds, q, *refs):
    deltas = [(refs[2 * i], refs[2 * i + 1]) for i in range(rounds)]
    refs = refs[2 * rounds :]
    weights, rows = refs[0], refs[1]
    held = refs[2 : 2 + groups]
    out = refs[2 + groups]
    det = q.shape[1]
    total = q.shape[2]
    columns = total // views
    half = held[0].shape[2]
    chunk = min(half, 512)
    unpacked = unpack_rays(rows, groups, slabs, own, fz, det, total)
    residual = residuals(q, deltas, [u[2] for u in unpacked], groups)[-1]
    residual = [r.astype(BF16) for r in residual]
    count = slabs * PACK
    parts = PACK // fz
    width = half // parts
    shape = (slabs * fz, count)
    z = lax.broadcasted_iota(jnp.int32, shape, 0)
    column = lax.broadcasted_iota(jnp.int32, shape, 1)
    projections = [None] * groups
    for part in range(2):
        depths = [unpacked[g][1 - part] for g in range(groups)]
        spreads = []
        for g in range(groups):
            pieces = [
                dot(
                    depths[g][:, v * det : (v + 1) * det],
                    residual[g][:, v * columns : (v + 1) * columns],
                    ((1,), (0,)),
                ).astype(BF16)
                for v in range(views)
            ]
            spreads.append(jnp.concatenate(pieces, axis=1))
        moments = [None] * groups
        for c in range(half // chunk):
            cut = slice(c * chunk, (c + 1) * chunk)
            if part == 1:
                weight = weights[:, :, cut].reshape(count, chunk).astype(F32)
            else:
                which = (c * chunk) // width
                low = c * chunk - which * width
                source = weights[:, :, half + low : half + low + chunk].reshape(count, chunk)
                choose = jnp.where(
                    column == (z // fz) * PACK + (z % fz) * parts + which, 1.0, 0.0
                ).astype(BF16)
                weight = dot(choose, source, ((1,), (0,)))
            rays = [
                jnp.concatenate([held[g][part, v, cut, :] for v in range(views)], axis=1)
                for g in range(groups)
            ]
            back = dot(spreads[0], rays[0], ((1,), (1,)))
            for g in range(1, groups):
                back = back + dot(spreads[g], rays[g], ((1,), (1,)))
            change = (weight * back).astype(BF16)
            for g in range(groups):
                moment = dot(change, rays[g], ((1,), (0,)))
                moments[g] = moment if moments[g] is None else moments[g] + moment
        for g in range(groups):
            moment = moments[g].astype(BF16)
            pieces = [
                dot(
                    depths[g][:, v * det : (v + 1) * det],
                    moment[:, v * columns : (v + 1) * columns],
                    ((0,), (0,)),
                )
                for v in range(views)
            ]
            value = jnp.concatenate(pieces, axis=1)
            projections[g] = value if projections[g] is None else projections[g] + value
    for g in range(groups):
        out[g] = projections[g].astype(BF16)


def tail_kernel(slabs, groups, views, own, fz, rounds, q, *refs):
    deltas = [(refs[2 * i], refs[2 * i + 1]) for i in range(rounds)]
    refs = refs[2 * rounds :]
    rows = refs[0]
    held = refs[1 : 1 + groups]
    mine, theirs = refs[1 + groups : 3 + groups]
    det = q.shape[1]
    total = q.shape[2]
    columns = total // views
    half = held[0].shape[2]
    chunk = min(half, 512)
    core = lax.axis_index("slab") % 2
    unpacked = unpack_rays(rows, groups, slabs, own, fz, det, total)
    history = residuals(q, deltas, [u[2] for u in unpacked], groups)
    half_groups = rows.shape[1]
    span = rows.shape[4] // 2
    spreads = []
    for g in range(groups):
        value = history[0][g]
        for other in history[1:]:
            value = value + other[g]
        high, low = in_two(value)
        pieces = []
        for v in range(views):
            depth = jnp.concatenate(
                [
                    rows[(g // half_groups) ^ core, g % half_groups, side ^ core, :, cut]
                    for side in range(2)
                    for cut in (
                        slice(v * det, (v + 1) * det),
                        slice(span + v * det, span + (v + 1) * det),
                    )
                ],
                axis=0,
            )
            cut = slice(v * columns, (v + 1) * columns)
            pieces.append(
                dot(depth, high[:, cut], ((1,), (0,))) + dot(depth, low[:, cut], ((1,), (0,)))
            )
        spreads.append(in_two(jnp.concatenate(pieces, axis=1)))
    for part in range(2):
        first = slice(PACK * (1 - part), PACK * (2 - part))
        second = slice(PACK * (3 - part), PACK * (4 - part))
        chosen = [
            jnp.concatenate([s[first] for s in pair] + [s[second] for s in pair], axis=0)
            for pair in spreads
        ]
        for c in range(half // chunk):
            cut = slice(c * chunk, (c + 1) * chunk)
            back = None
            for g in range(groups):
                rays = jnp.concatenate([held[g][part, v, cut, :] for v in range(views)], axis=1)
                value = dot(chosen[g], rays, ((1,), (1,)))
                back = value if back is None else back + value
            mine[part, :, cut] = back[:PACK] + back[PACK : 2 * PACK]
            theirs[part, :, cut] = back[2 * PACK : 3 * PACK] + back[3 * PACK :]


def final_kernel(own, mine, received, fine, coarse, fw, cw, blocks, fine_out, coarse_out):
    core = lax.axis_index("slab") % 2
    half = mine.shape[2]
    fz = fine.shape[0]
    for source, side in ((mine, core), (received, 1 - core)):
        start = pl.multiple_of(side * half, half)
        where = pl.ds(start, half)
        keep = keep_row(blocks, start, half)
        change = source[0, own : own + fz]
        fine_out[:, where] = fine[:, where] + fw[:, where] * change
        coarse_out[:, where] = (
            coarse[:, where] + cw[:, where] * source[1]
        ) * keep


def make_body(slabs, groups):
    def body(
        fine_volume,
        coarse_volume,
        fine_rays,
        coarse_rays,
        fine_axial,
        coarse_axial,
        measured,
        ray_weight,
        fine_cell_weight,
        coarse_cell_weight,
        margin_blocks,
        ray_hits,
    ):
        views, cells, columns = fine_rays.shape
        det = fine_axial.shape[2]
        fz, cz = fine_volume.shape[0], coarse_volume.shape[0]
        own = measured.shape[0]
        total = views * columns
        span = max(views * det, total)
        half = cells // 2
        core = lax.axis_index("slab") % 2
        width = half + half * fz // PACK

        own_rays, weights_mine, weights_theirs, rows = pl.pallas_call(
            prepare_kernel,
            out_shape=(
                jax.ShapeDtypeStruct((2, views, half, columns), BF16),
                jax.ShapeDtypeStruct((PACK, width), BF16),
                jax.ShapeDtypeStruct((PACK, width), BF16),
                jax.ShapeDtypeStruct((PACK, views * det + span), BF16),
            ),
            in_specs=[HBM] * 7 + [SMEM] * 2,
            out_specs=(VMEM,) * 4,
            scratch_shapes=[
                pltpu.VMEM(a.shape, a.dtype)
                for a in (
                    fine_cell_weight,
                    coarse_cell_weight,
                    fine_axial,
                    coarse_axial,
                    ray_weight,
                )
            ]
            + [pltpu.SemaphoreType.DMA((7,))],
            compiler_params=PARAMS,
            cost_estimate=QUICK,
            name="prepare",
        )(
            fine_rays,
            coarse_rays,
            fine_cell_weight,
            coarse_cell_weight,
            fine_axial,
            coarse_axial,
            ray_weight,
            margin_blocks,
            ray_hits,
        )

        ray_list = [own_rays]
        all_rows = rows[None]
        bit = 1
        while bit < groups:
            all_rows = jnp.concatenate([all_rows, swap(all_rows, "view", groups, bit)])
            ray_list += [swap(value, "view", groups, bit) for value in ray_list]
            bit *= 2

        half_groups = groups // 2
        first, second = all_rows[:half_groups], all_rows[half_groups:]
        lead = core == 0
        rows_mine = jnp.where(lead, first, second)
        rows_theirs = jnp.where(lead, second, first)
        weights_other = swap(weights_theirs, "slab", slabs, 1)
        rows_other = swap(rows_theirs, "slab", slabs, 1)

        def pair(a, b):
            return jnp.where(lead, jnp.stack([a, b]), jnp.stack([b, a]))

        held_weights = pair(weights_mine, weights_other)
        held_rows = pair(rows_mine, rows_other)
        far = [4 * k for k in range(1, slabs // 4)]
        held_weights = jnp.concatenate(
            [held_weights] + [swap(held_weights, "slab", slabs, k) for k in far]
        )
        held_rows = jnp.concatenate(
            [held_rows] + [swap(held_rows, "slab", slabs, k) for k in far]
        )
        held_weights = jnp.concatenate([held_weights, swap(held_weights, "slab", slabs, 2)])
        held_rows = jnp.concatenate([held_rows, swap(held_rows, "slab", slabs, 2)])
        held_rows = jnp.swapaxes(held_rows, 0, 1)
        held_rows = jnp.stack([held_rows, swap(held_rows, "slab", slabs, 1)])

        steps = 4
        q = pl.pallas_call(
            forward_kernel,
            out_shape=jax.ShapeDtypeStruct((det, total), F32),
            in_specs=[HBM] * 5 + [VMEM, SMEM],
            out_specs=VMEM,
            scratch_shapes=[
                pltpu.VMEM(a.shape, a.dtype)
                for a in (fine_volume, coarse_volume, fine_rays, coarse_rays, measured)
            ]
            + [pltpu.SemaphoreType.DMA((steps + 1, 4))],
            compiler_params=PARAMS,
            cost_estimate=QUICK,
            name="forward",
        )(fine_volume, coarse_volume, fine_rays, coarse_rays, measured, rows, margin_blocks)
        bit = 1
        while bit < slabs:
            q = q + swap(q.astype(BF16), "slab", slabs, bit).astype(F32)
            bit *= 2
        q = q[None]
        bit = 1
        while bit < groups:
            q = jnp.concatenate([q, swap(q, "view", groups, bit)])
            bit *= 2

        deltas = []
        for rounds in range(2):
            delta = pl.pallas_call(
                functools.partial(loop_kernel, slabs, groups, views, own, fz, rounds),
                out_shape=jax.ShapeDtypeStruct((groups, det, total), BF16),
                in_specs=[VMEM] * (3 + 2 * rounds + groups),
                out_specs=VMEM,
                compiler_params=PARAMS,
                name="ray_space_step",
            )(q, *deltas, held_weights, held_rows, *ray_list)
            deltas += [delta, swap(delta, "slab", slabs, 1)]
        mine, theirs = pl.pallas_call(
            functools.partial(tail_kernel, slabs, groups, views, own, fz, 2),
            out_shape=(jax.ShapeDtypeStruct((2, PACK, half), F32),) * 2,
            in_specs=[VMEM] * (2 + len(deltas) + groups),
            out_specs=(VMEM, VMEM),
            compiler_params=PARAMS,
            name="back_projection",
        )(q, *deltas, held_rows, *ray_list)
        received = swap(theirs, "slab", slabs, 1)
        return pl.pallas_call(
            functools.partial(final_kernel, own),
            out_shape=(
                jax.ShapeDtypeStruct(fine_volume.shape, F32),
                jax.ShapeDtypeStruct(coarse_volume.shape, F32),
            ),
            in_specs=[VMEM] * 6 + [SMEM],
            out_specs=(VMEM, VMEM),
            compiler_params=PARAMS,
            name="update",
        )(
            mine,
            received,
            fine_volume,
            coarse_volume,
            fine_cell_weight,
            coarse_cell_weight,
            margin_blocks,
        )

    return body


def solution(mesh):
    return jax.shard_map(
        make_body(mesh.shape["slab"], mesh.shape["view"]),
        mesh=mesh,
        in_specs=(
            P("slab", None),
            P("slab", None),
            P("view", None, None),
            P("view", None, None),
            P("view", "slab", None),
            P("view", "slab", None),
            P("slab", "view", None),
            P("slab", "view", None),
            P("slab", None),
            P("slab", None),
            P("slab", None),
            P("view", "slab", None),
        ),
        out_specs=(P("slab", None), P("slab", None)),
        check_vma=False,
    )
```

```python
import functools
import jax
import jax.numpy as jnp
from jax import lax
from jax.experimental import pallas as pl
from jax.experimental.pallas import tpu as pltpu
from jax.sharding import PartitionSpec as P

BLOCK = 128
LANES = 128
PACK = 16
F32 = jnp.float32
BF16 = jnp.bfloat16
PARAMS = pltpu.CompilerParams(vmem_limit_bytes=24 * 1024 * 1024)
VMEM = pl.BlockSpec(memory_space=pltpu.VMEM)
SMEM = pl.BlockSpec(memory_space=pltpu.SMEM)
HBM = pl.BlockSpec(memory_space=pltpu.HBM)
QUICK = pl.CostEstimate(flops=1, bytes_accessed=1, transcendentals=0)


def fetch(source, target, sem):
    copy = pltpu.make_async_copy(source, target, sem)
    copy.start()
    return copy


def in_hbm(*arrays):
    return [pltpu.with_memory_space_constraint(a, pltpu.HBM) for a in arrays]


def scratch_like(*arrays):
    return [pltpu.VMEM(a.shape, a.dtype) for a in arrays]


def shaped(shape, dtype):
    return jax.ShapeDtypeStruct(shape, dtype)


def call(kernel, name, out_shape, in_specs, scratch=()):
    many = isinstance(out_shape, tuple)
    return pl.pallas_call(
        kernel,
        out_shape=out_shape,
        in_specs=in_specs,
        out_specs=(VMEM,) * len(out_shape) if many else VMEM,
        scratch_shapes=list(scratch),
        compiler_params=PARAMS,
        cost_estimate=QUICK,
        name=name,
    )


def swap(value, axis, size, bits):
    return lax.ppermute(value, axis, [(i, i ^ bits) for i in range(size)])


def dot(a, b, dims):
    return lax.dot_general(a, b, (dims, ((), ())), preferred_element_type=F32)


def in_two(value):
    high = value.astype(BF16)
    return high, (value - high.astype(F32)).astype(BF16)


def keep_row(blocks_ref, start, width):
    ids = (lax.broadcasted_iota(jnp.int32, (1, width), 1) + start) // BLOCK
    keep = jnp.ones((1, width), F32)
    for k in range(blocks_ref.shape[1]):
        keep = jnp.where(ids == blocks_ref[0, k], 0.0, keep)
    return keep


def packed_tiles(cells, fz):
    parts = PACK // fz
    return -(-(cells // LANES) // parts)


def hit_depths(axial, hits):
    views, _, det = axial.shape
    tiles = hits.shape[2]
    tile = lax.broadcasted_iota(jnp.int32, (1, det), 1) // (det // tiles)
    result = []
    for v in range(views):
        hit = jnp.zeros((1, det), F32)
        for t in range(tiles):
            hit = jnp.where(tile == t, hits[v, 0, t].astype(F32), hit)
        result.append(axial[v].astype(F32) * hit)
    return result


def prepare_kernel(
    cut,
    fine_rays,
    coarse_rays,
    fine_weight_in,
    coarse_weight_in,
    fine_axial_in,
    coarse_axial_in,
    ray_weight_in,
    blocks,
    hits,
    near,
    rest,
    mine,
    theirs,
    rows,
    fine_weight,
    coarse_weight,
    fine_axial,
    coarse_axial,
    ray_weight,
    sems,
):
    me = lax.axis_index("slab")
    core, across = me % 2, (me // 2) % 2
    fz, cells = fine_weight.shape
    half = cells // 2
    base = pl.multiple_of(core * half, half)
    here = pl.ds(pl.multiple_of(base + across * cut, LANES), cut)
    tail = pl.ds(pl.multiple_of(base + 2 * cut, LANES), half - 2 * cut)
    sources = (
        (fine_axial_in, fine_axial),
        (coarse_axial_in, coarse_axial),
        (ray_weight_in, ray_weight),
        (fine_weight_in, fine_weight),
        (coarse_weight_in, coarse_weight),
        (fine_rays.at[:, here, :], near.at[0]),
        (coarse_rays.at[:, here, :], near.at[1]),
        (fine_rays.at[:, tail, :], rest.at[0]),
        (coarse_rays.at[:, tail, :], rest.at[1]),
    )
    copies = [fetch(a, b, sems.at[i]) for i, (a, b) in enumerate(sources)]
    for copy in copies[:3]:
        copy.wait()

    views, _, det = fine_axial.shape
    total = views * ray_weight.shape[2]
    span = views * det
    own = ray_weight.shape[0]
    coarse_depth = hit_depths(coarse_axial, hits)
    fine_depth = hit_depths(fine_axial, hits)
    for v in range(views):
        rows[:, v * det : (v + 1) * det] = coarse_depth[v].astype(BF16)
    wide = rows.shape[1] - span
    weight = jnp.concatenate([ray_weight[:, v, :] for v in range(views)], axis=1)
    fine_wide = jnp.concatenate(fine_depth, axis=1)
    if wide > total:
        weight = jnp.concatenate([weight, jnp.zeros((own, wide - total), F32)], axis=1)
    if wide > span:
        fine_wide = jnp.concatenate([fine_wide, jnp.zeros((fz, wide - span), F32)], axis=1)
    stack = [weight, fine_wide]
    if own + fz < PACK:
        stack.append(jnp.zeros((PACK - own - fz, wide), F32))
    rows[:, span:] = jnp.concatenate(stack, axis=0).astype(BF16)

    for copy in copies[3:5]:
        copy.wait()
    parts = PACK // fz
    empty = jnp.zeros((1, LANES), F32)
    for target, side in ((mine, core), (theirs, 1 - core)):
        column = 0
        begin = pl.multiple_of(side * half, half)
        for first, size in ((0, 2 * cut), (2 * cut, half - 2 * cut)):
            start = pl.multiple_of(begin + first, LANES)
            keep = keep_row(blocks, start, size)
            target[:, column : column + size] = (
                coarse_weight[:, pl.ds(start, size)] * keep
            ).astype(BF16)
            column += size
            fine = fine_weight[:, pl.ds(start, size)]
            for c in range(packed_tiles(size, fz)):
                pieces = []
                for i in range(fz):
                    for k in range(parts):
                        t = c * parts + k
                        inside = t * LANES < size
                        piece = fine[i : i + 1, t * LANES : (t + 1) * LANES] if inside else empty
                        pieces.append(piece)
                target[:, column : column + LANES] = jnp.concatenate(pieces, axis=0).astype(BF16)
                column += LANES
    for copy in copies[5:]:
        copy.wait()


def forward_kernel(
    fine_rays_in,
    coarse_rays_in,
    fine_in,
    coarse_in,
    fine_axial_in,
    coarse_axial_in,
    measured_in,
    blocks,
    hits,
    out,
    own_rays,
    fine_rays,
    coarse_rays,
    fine,
    coarse,
    fine_axial,
    coarse_axial,
    measured,
    sems,
    chunk_sems,
):
    core = lax.axis_index("slab") % 2
    fz, cells = fine.shape
    half = cells // 2
    steps = chunk_sems.shape[0]
    chunk = cells // steps
    copies = []
    for i in range(steps):
        part = pl.ds(i * chunk, chunk)
        copies.append(
            [
                fetch(fine_in.at[:, part], fine.at[:, part], chunk_sems.at[i, 0]),
                fetch(coarse_in.at[:, part], coarse.at[:, part], chunk_sems.at[i, 1]),
                fetch(fine_rays_in.at[:, part, :], fine_rays.at[:, part, :], chunk_sems.at[i, 2]),
                fetch(
                    coarse_rays_in.at[:, part, :], coarse_rays.at[:, part, :], chunk_sems.at[i, 3]
                ),
            ]
        )
    others = [
        fetch(fine_axial_in, fine_axial, sems.at[0]),
        fetch(coarse_axial_in, coarse_axial, sems.at[1]),
        fetch(measured_in, measured, sems.at[2]),
    ]
    views, _, columns = fine_rays.shape
    total = views * columns
    fine_sum = coarse_sum = None
    for i in range(steps):
        part = slice(i * chunk, (i + 1) * chunk)
        for copy in copies[i]:
            copy.wait()
        keep = keep_row(blocks, i * chunk, chunk)
        fine_rows = fine[:, part].astype(BF16)
        coarse_rows = (coarse[:, part] * keep).astype(BF16)
        fine_wide = jnp.concatenate([fine_rays[v, part, :] for v in range(views)], axis=1)
        coarse_wide = jnp.concatenate([coarse_rays[v, part, :] for v in range(views)], axis=1)
        fine_part = dot(fine_rows, fine_wide, ((1,), (0,)))
        coarse_part = dot(coarse_rows, coarse_wide, ((1,), (0,)))
        fine_sum = fine_part if fine_sum is None else fine_sum + fine_part
        coarse_sum = coarse_part if coarse_sum is None else coarse_sum + coarse_part
    held = pl.ds(pl.multiple_of(core * half, half), half)
    outgoing = [
        fetch(fine_rays.at[:, held, :], own_rays.at[0], sems.at[3]),
        fetch(coarse_rays.at[:, held, :], own_rays.at[1], sems.at[4]),
    ]
    for copy in others:
        copy.wait()
    coarse_depth = hit_depths(coarse_axial, hits)
    fine_depth = hit_depths(fine_axial, hits)
    own = measured.shape[0]
    det = out.shape[0]
    pad = jnp.zeros((PACK - fz, total), F32)
    moment = jnp.concatenate([coarse_sum, fine_sum, pad], axis=0).astype(BF16)
    pad = jnp.zeros((PACK - fz, det), F32)
    row = lax.broadcasted_iota(jnp.int32, (det, columns), 0) - lax.axis_index("slab") * own
    for v in range(views):
        depth = jnp.concatenate([coarse_depth[v], fine_depth[v], pad], axis=0).astype(BF16)
        where = slice(v * columns, (v + 1) * columns)
        projection = dot(depth, moment[:, where], ((0,), (0,)))
        given = jnp.zeros((det, columns), F32)
        for i in range(own):
            given = jnp.where(row == i, measured[i : i + 1, v, :], given)
        out[:, where] = given - projection
    for copy in outgoing:
        copy.wait()


def slab_of(block, bits):
    me = lax.axis_index("slab")
    apart = jnp.zeros_like(block)
    for place, bit in enumerate(bits):
        apart = apart + ((block >> (place + 1)) & 1) * bit
    return ((me - me % 2) ^ apart) + (block & 1)


def rows_kernel(own, fz, total, bits, rows, coarse_out, fine_out, coarse_turned, fine_turned, out):
    core = lax.axis_index("slab") % 2
    _, half_groups, slabs, _, width = rows.shape
    groups = 2 * half_groups
    span = width // 2
    det = out.shape[1]
    count = slabs * PACK
    shape = (slabs * own, count)
    w = lax.broadcasted_iota(jnp.int32, shape, 0)
    column = lax.broadcasted_iota(jnp.int32, shape, 1)
    block, row = column // PACK, column % PACK
    match = (row < own) & (w == slab_of(block, bits) * own + row)
    to_weight = jnp.where(match, 1.0, 0.0).astype(BF16)
    shape = (slabs * fz, count)
    z = lax.broadcasted_iota(jnp.int32, shape, 0)
    column = lax.broadcasted_iota(jnp.int32, shape, 1)
    to_fine = jnp.where(column == (z // fz) * PACK + own + z % fz, 1.0, 0.0).astype(BF16)
    for g in range(groups):
        one = rows[(g // half_groups) ^ core, g % half_groups]
        coarse = one[:, :, :span].reshape(count, span)
        side = one[:, :, span:].reshape(count, span)
        fine = dot(to_fine, side, ((1,), (0,)))
        coarse_out[g] = coarse
        fine_out[g] = fine.astype(BF16)
        wide = coarse.astype(F32)
        for v in range(span // det):
            where = slice(v * det, (v + 1) * det)
            coarse_turned[g, v] = wide[:, where].T.astype(BF16)
            fine_turned[g, v] = fine[:, where].T.astype(BF16)
        out[g] = dot(to_weight, side, ((1,), (0,)))[:, :total]


def weights_kernel(fz, cut, order, first, second, fine_out):
    slabs = first.shape[0]
    count = slabs * PACK
    parts = PACK // fz
    shape = (slabs * fz, count)
    z = lax.broadcasted_iota(jnp.int32, shape, 0)
    column = lax.broadcasted_iota(jnp.int32, shape, 1)
    where = z // fz
    moved = jnp.zeros_like(where)
    for j, k in enumerate(order):
        moved = jnp.where(where == j, k, moved)
    done = 0
    half = fine_out.shape[1]
    for source, block, size in ((first, where, 2 * cut), (second, moved, half - 2 * cut)):
        tiles = packed_tiles(size, fz)
        packed = source[:, :, size : size + tiles * LANES].reshape(count, tiles * LANES)
        for k in range(parts):
            choose = column == block * PACK + (z % fz) * parts + k
            chosen = dot(jnp.where(choose, 1.0, 0.0).astype(BF16), packed, ((1,), (0,)))
            for c in range(tiles):
                t = c * parts + k
                if t * LANES < size:
                    fine_out[:, done + t * LANES : done + (t + 1) * LANES] = chosen[
                        :, c * LANES : (c + 1) * LANES
                    ].astype(BF16)
        done += size


def residuals(q, deltas, weights):
    groups = q.shape[0]
    current = [q[g] for g in range(groups)]
    results = [[weights[g] * current[g] for g in range(groups)]]
    for mine, theirs in deltas:
        current = [
            current[g] - (mine[g].astype(F32) + theirs[g].astype(F32)) for g in range(groups)
        ]
        results.append([weights[g] * current[g] for g in range(groups)])
    return results


def spread(depth, residual, views):
    det, columns = residual.shape[0], residual.shape[1] // views
    pieces = [
        dot(
            depth[:, v * det : (v + 1) * det],
            residual[:, v * columns : (v + 1) * columns],
            ((1,), (0,)),
        )
        for v in range(views)
    ]
    return jnp.concatenate(pieces, axis=1)


def spread_kernel(views, q, weights, fine_depth, coarse_depth, fine_out, coarse_out):
    for g in range(q.shape[0]):
        residual = (weights[g] * q[g]).astype(BF16)
        fine_out[g] = spread(fine_depth[g], residual, views).astype(BF16)
        coarse_out[g] = spread(coarse_depth[g], residual, views).astype(BF16)


def segments(cut, half, groups, own_rays, near, far, rest):
    across = (lax.axis_index("slab") // 2) % 2
    views = own_rays.shape[1]

    def reader(start, size, others):
        def read(part, g):
            if g == 0:
                pieces = [own_rays[part, v, pl.ds(start, size), :] for v in range(views)]
            else:
                pieces = [others[g - 1][part, v] for v in range(views)]
            return jnp.concatenate(pieces, axis=1)

        return read

    here = pl.multiple_of(across * cut, LANES)
    there = pl.multiple_of((1 - across) * cut, LANES)
    last = half - 2 * cut
    return (
        (here, cut, reader(here, cut, near)),
        (there, cut, reader(there, cut, far)),
        (2 * cut, last, reader(2 * cut, last, rest)),
    )


def step_kernel(cut, order, groups, views, ready, *refs):
    refs = list(refs)
    if ready:
        spreads = [refs.pop(0), refs.pop(0)]
    else:
        q, mine, theirs, weights, fine_depth, coarse_depth = refs[:6]
        refs = refs[6:]
        residual = residuals(q, [(mine, theirs)], weights)[-1]
        residual = [r.astype(BF16) for r in residual]
        spreads = [
            [spread(depth[g], residual[g], views).astype(BF16) for g in range(groups)]
            for depth in (fine_depth, coarse_depth)
        ]
    turned = refs[:2]
    first, second, fine_weights, own_rays = refs[2:6]
    out = refs[-1]
    others = refs[6:-1]
    n = groups - 1
    near, far, rest = others[:n], others[n : 2 * n], others[2 * n :]
    slabs = first.shape[0]
    count = slabs * PACK
    half = own_rays.shape[2]
    columns = own_rays.shape[3]
    runs = segments(cut, half, groups, own_rays, near, far, rest)
    results = [None] * groups
    for part in range(2):
        moments = [None] * groups
        for index, (start, size, read) in enumerate(runs):
            if part == 0:
                weight = fine_weights[:, pl.ds(start, size)]
            elif index < 2:
                weight = first[:, :, pl.ds(start, size)].reshape(count, size)
            else:
                weight = jnp.concatenate([second[k, :, :size] for k in order], axis=0)
            rays = [read(part, g) for g in range(groups)]
            back = dot(spreads[part][0], rays[0], ((1,), (1,)))
            for g in range(1, groups):
                back = back + dot(spreads[part][g], rays[g], ((1,), (1,)))
            change = (weight.astype(F32) * back).astype(BF16)
            for g in range(groups):
                moment = dot(change, rays[g], ((1,), (0,)))
                moments[g] = moment if moments[g] is None else moments[g] + moment
        for g in range(groups):
            moment = moments[g].astype(BF16)
            pieces = [
                dot(turned[part][g, v], moment[:, v * columns : (v + 1) * columns], ((1,), (0,)))
                for v in range(views)
            ]
            value = jnp.concatenate(pieces, axis=1)
            results[g] = value if results[g] is None else results[g] + value
    for g in range(groups):
        out[g] = results[g].astype(BF16)


def tail_kernel(cut, groups, views, q, *refs):
    deltas = [(refs[0], refs[1]), (refs[2], refs[3])]
    weights, fine_depth, coarse_depth, own_rays = refs[4:8]
    mine, theirs = refs[-2:]
    others = refs[8:-2]
    n = groups - 1
    near, far, rest = others[:n], others[n : 2 * n], others[2 * n :]
    core = lax.axis_index("slab") % 2
    half = own_rays.shape[2]
    fz = mine.shape[0] - PACK
    history = residuals(q, deltas, weights)
    spreads = ([], [])
    for g in range(groups):
        value = history[0][g]
        for other in history[1:]:
            value = value + other[g]
        high, low = in_two(value)
        for part, depth in ((0, fine_depth[g, : 2 * fz]), (1, coarse_depth[g, : 2 * PACK])):
            pair = in_two(spread(depth, high, views) + spread(depth, low, views))
            spreads[part].append(jnp.concatenate(pair, axis=0))
    for part, size in ((0, fz), (1, PACK)):
        place = slice(PACK, PACK + fz) if part == 0 else slice(0, PACK)
        for start, width, read in segments(cut, half, groups, own_rays, near, far, rest):
            back = None
            for g in range(groups):
                value = dot(spreads[part][g], read(part, g), ((1,), (1,)))
                back = value if back is None else back + value
            back = back[: 2 * size] + back[2 * size :]
            lower, upper = back[:size], back[size:]
            where = pl.ds(start, width)
            mine[place, where] = jnp.where(core == 0, lower, upper)
            theirs[place, where] = jnp.where(core == 0, upper, lower)


def final_kernel(mine, received, fine, coarse, fw, cw, blocks, fine_out, coarse_out):
    core = lax.axis_index("slab") % 2
    half = mine.shape[1]
    for source, side in ((mine, core), (received, 1 - core)):
        start = pl.multiple_of(side * half, half)
        where = pl.ds(start, half)
        keep = keep_row(blocks, start, half)
        fine_out[:, where] = fine[:, where] + fw[:, where] * source[PACK:, :]
        coarse_out[:, where] = (coarse[:, where] + cw[:, where] * source[:PACK, :]) * keep


def make_body(slabs, groups):
    far_bits = [1 << k for k in range(slabs.bit_length() - 2, 1, -1)]
    view_bits = [1 << k for k in range(groups.bit_length() - 1)]

    def along_slab(value, bit):
        return swap(value, "slab", slabs, bit)

    def body(
        fine_volume,
        coarse_volume,
        fine_rays,
        coarse_rays,
        fine_axial,
        coarse_axial,
        measured,
        ray_weight,
        fine_cell_weight,
        coarse_cell_weight,
        margin_blocks,
        ray_hits,
    ):
        views, cells, columns = fine_rays.shape
        det = fine_axial.shape[2]
        fz, cz = fine_volume.shape[0], coarse_volume.shape[0]
        own = measured.shape[0]
        total = views * columns
        span = max(views * det, total)
        half = cells // 2
        cut = half * 5 // 16 // LANES * LANES
        last = half - 2 * cut
        core = lax.axis_index("slab") % 2
        lead = core == 0
        width = 2 * cut + packed_tiles(2 * cut, fz) * LANES
        width_two = last + packed_tiles(last, fz) * LANES

        small = in_hbm(
            fine_cell_weight, coarse_cell_weight, fine_axial, coarse_axial, ray_weight
        )
        near, rest, mine, theirs, rows = call(
            functools.partial(prepare_kernel, cut),
            "prepare",
            (
                shaped((2, views, cut, columns), BF16),
                shaped((2, views, last, columns), BF16),
                shaped((PACK, width + width_two), BF16),
                shaped((PACK, width + width_two), BF16),
                shaped((PACK, views * det + span), BF16),
            ),
            [HBM] * 7 + [SMEM] * 2,
            scratch_like(*small) + [pltpu.SemaphoreType.DMA((9,))],
        )(*in_hbm(fine_rays, coarse_rays), *small, *in_hbm(margin_blocks, ray_hits))

        near_list, rest_list, row_list = [near], [rest], [rows]
        for bit in view_bits:
            for held in (near_list, rest_list, row_list):
                held += [swap(value, "view", groups, bit) for value in held]
        near_list, rest_list = near_list[1:], rest_list[1:]
        far_list = [along_slab(value, 2) for value in near_list]

        def pair(a, b):
            return jnp.where(lead, jnp.stack([a, b]), jnp.stack([b, a]))

        both = pair(mine, along_slab(theirs, 1))
        first, second = both[:, :, :width], both[:, :, width:]
        half_groups = groups // 2
        low, high = jnp.stack(row_list[:half_groups]), jnp.stack(row_list[half_groups:])
        kept = jnp.where(lead, low, high)
        given = along_slab(jnp.where(lead, high, low), 1)
        shares = pair(kept, given)
        shares = shares.transpose(0, 2, 1, 3).reshape(2, PACK, -1)
        first = jnp.concatenate([first, shares], axis=2)
        second = jnp.concatenate([second, along_slab(second, 2)])
        for bit in far_bits:
            first = jnp.concatenate([first, along_slab(first, bit)])
            second = jnp.concatenate([second, along_slab(second, bit)])
        first = jnp.concatenate([first, along_slab(first, 2)])
        shares = first[:, :, width:]
        shares = jnp.stack([shares, along_slab(shares, 1)])
        shares = shares.reshape(2, slabs, PACK, half_groups, -1).transpose(0, 3, 1, 2, 4)
        count = len(far_bits)
        order = tuple(
            (j & 1) + 2 * (j >> (count + 1)) + 4 * ((j >> 1) & ((1 << count) - 1))
            for j in range(slabs)
        )

        coarse_depth, fine_depth, coarse_turned, fine_turned, weights = call(
            functools.partial(rows_kernel, own, fz, total, far_bits + [2]),
            "unpack_rows",
            (
                shaped((groups, slabs * PACK, span), BF16),
                shaped((groups, slabs * fz, span), BF16),
                shaped((groups, views, det, slabs * PACK), BF16),
                shaped((groups, views, det, slabs * fz), BF16),
                shaped((groups, det, total), F32),
            ),
            [VMEM],
        )(shares)
        fine_weights = call(
            functools.partial(weights_kernel, fz, cut, order),
            "unpack_weights",
            shaped((slabs * fz, half), BF16),
            [VMEM] * 2,
        )(first, second)

        taken = in_hbm(
            fine_rays,
            coarse_rays,
            fine_volume,
            coarse_volume,
            fine_axial,
            coarse_axial,
            measured,
        )
        q, own_rays = call(
            forward_kernel,
            "forward",
            (shaped((det, total), F32), shaped((2, views, half, columns), BF16)),
            [HBM] * 7 + [SMEM] * 2,
            scratch_like(*taken)
            + [pltpu.SemaphoreType.DMA((5,)), pltpu.SemaphoreType.DMA((4, 4))],
        )(*taken, *in_hbm(margin_blocks, ray_hits))
        for bit in [1, 2] + far_bits:
            q = q + along_slab(q.astype(BF16), bit).astype(F32)
        q = q[None]
        for bit in view_bits:
            q = jnp.concatenate([q, swap(q, "view", groups, bit)])

        spreads = call(
            functools.partial(spread_kernel, views),
            "spread",
            (
                shaped((groups, slabs * fz, total), BF16),
                shaped((groups, slabs * PACK, total), BF16),
            ),
            [VMEM] * 4,
        )(q, weights, fine_depth, coarse_depth)
        others = near_list + far_list + rest_list
        held = (fine_turned, coarse_turned, first, second, fine_weights, own_rays, *others)
        deltas = []
        for ready, inputs in ((True, spreads), (False, None)):
            if not ready:
                inputs = (q, *deltas, weights, fine_depth, coarse_depth)
            delta = call(
                functools.partial(step_kernel, cut, order, groups, views, ready),
                "ray_space_step",
                shaped((groups, det, total), BF16),
                [VMEM] * (len(inputs) + len(held)),
            )(*inputs, *held)
            deltas += [delta, along_slab(delta, 1)]
        result = shaped((PACK + fz, half), F32)
        inputs = (q, *deltas, weights, fine_depth, coarse_depth, own_rays, *others)
        ours, theirs = call(
            functools.partial(tail_kernel, cut, groups, views),
            "back_projection",
            (result, result),
            [VMEM] * len(inputs),
        )(*inputs)
        received = along_slab(theirs, 1)
        return call(
            final_kernel,
            "update",
            (shaped(fine_volume.shape, F32), shaped(coarse_volume.shape, F32)),
            [VMEM] * 6 + [SMEM],
        )(
            ours,
            received,
            fine_volume,
            coarse_volume,
            fine_cell_weight,
            coarse_cell_weight,
            margin_blocks,
        )

    return body


def solution(mesh):
    return jax.shard_map(
        make_body(mesh.shape["slab"], mesh.shape["view"]),
        mesh=mesh,
        in_specs=(
            P("slab", None),
            P("slab", None),
            P("view", None, None),
            P("view", None, None),
            P("view", "slab", None),
            P("view", "slab", None),
            P("slab", "view", None),
            P("slab", "view", None),
            P("slab", None),
            P("slab", None),
            P("slab", None),
            P("view", "slab", None),
        ),
        out_specs=(P("slab", None), P("slab", None)),
        check_vma=False,
    )
```

```python
import functools
import jax
import jax.numpy as jnp
from jax import lax
from jax.experimental import pallas as pl
from jax.experimental.pallas import tpu as pltpu
from jax.sharding import PartitionSpec as P

BLOCK = 128
LANES = 128
PACK = 16
F32 = jnp.float32
BF16 = jnp.bfloat16
PARAMS = pltpu.CompilerParams(vmem_limit_bytes=24 * 1024 * 1024)
VMEM = pl.BlockSpec(memory_space=pltpu.VMEM)
SMEM = pl.BlockSpec(memory_space=pltpu.SMEM)
ANY = pl.BlockSpec(memory_space=pl.ANY)
HBM = pl.BlockSpec(memory_space=pltpu.HBM)
SOURCE = {"rays": "start", "weights": "start"}
AWAITED = {"rays": "views"}
QUICK = pl.CostEstimate(flops=1, bytes_accessed=1, transcendentals=0)


def fetch(source, target, sem):
    copy = pltpu.make_async_copy(source, target, sem)
    copy.start()
    return copy


def in_hbm(*arrays):
    return [pltpu.with_memory_space_constraint(a, pltpu.HBM) for a in arrays]


def scratch_like(*arrays):
    return [pltpu.VMEM(a.shape, a.dtype) for a in arrays]


def shaped(shape, dtype):
    return jax.ShapeDtypeStruct(shape, dtype)


def call(kernel, name, out_shape, in_specs, scratch=()):
    many = isinstance(out_shape, tuple)
    return pl.pallas_call(
        kernel,
        out_shape=out_shape,
        in_specs=in_specs,
        out_specs=(VMEM,) * len(out_shape) if many else VMEM,
        scratch_shapes=list(scratch),
        compiler_params=PARAMS,
        cost_estimate=QUICK,
        name=name,
    )


def swap(value, axis, size, bits):
    return lax.ppermute(value, axis, [(i, i ^ bits) for i in range(size)])


def dot(a, b, dims):
    return lax.dot_general(a, b, (dims, ((), ())), preferred_element_type=F32)


def in_two(value):
    high = value.astype(BF16)
    return high, (value - high.astype(F32)).astype(BF16)


def keep_row(blocks_ref, start, width):
    ids = (lax.broadcasted_iota(jnp.int32, (1, width), 1) + start) // BLOCK
    keep = jnp.ones((1, width), F32)
    for k in range(blocks_ref.shape[1]):
        keep = jnp.where(ids == blocks_ref[0, k], 0.0, keep)
    return keep


def share_start(cells, groups, bits=0):
    core = lax.axis_index("slab") % 2
    share = cells // 2 // groups
    return pl.multiple_of(core * (cells // 2) + (lax.axis_index("view") ^ bits) * share, LANES)


def packed_tiles(cells, fz):
    parts = PACK // fz
    return -(-(cells // LANES) // parts)


def hit_depths(axial, hits):
    views, _, det = axial.shape
    tiles = hits.shape[2]
    tile = lax.broadcasted_iota(jnp.int32, (1, det), 1) // (det // tiles)
    result = []
    for v in range(views):
        hit = jnp.zeros((1, det), F32)
        for t in range(tiles):
            hit = jnp.where(tile == t, hits[v, 0, t].astype(F32), hit)
        result.append(axial[v].astype(F32) * hit)
    return result


def take_kernel(groups, bits, fine_rays, coarse_rays, *refs):
    out, sems = refs[-2:]
    cells = pl.ds(share_start(fine_rays.shape[1], groups, bits), out.shape[2])
    copies = [
        fetch(rays.at[:, cells, :], out.at[part], sems.at[part])
        for part, rays in enumerate((fine_rays, coarse_rays))
    ]
    for copy in copies:
        copy.wait()


def pair_kernel(mine, received, *refs):
    out = refs[-1]
    lead = lax.axis_index("slab") % 2 == 0
    own, other = mine[...].astype(F32), received[...].astype(F32)
    out[0] = jnp.where(lead, own, other).astype(BF16)
    out[1] = jnp.where(lead, other, own).astype(BF16)


def join_core_kernel(q, received, rows, *refs):
    total, out = refs[-2:]
    count = q.shape[0]
    value = q[...] + received[...].astype(F32)
    total[...] = value
    out[:count] = value.astype(BF16)
    out[count:] = rows[...]


def join_hop_kernel(last, q, mine, received, *refs):
    total, out = refs[-2:]
    count = q.shape[0]
    value = q[...] + received[:count].astype(F32)
    total[...] = value
    high, low = in_two(value)
    out[:count] = high
    base = count
    if last:
        out[count : 2 * count] = low
        base = 2 * count
    held = mine.shape[0] - count
    out[base : base + held] = mine[count:]
    out[base + held :] = received[count:]


def join_views_kernel(count, *refs):
    q, rows = refs[-2:]
    for g in range(q.shape[0]):
        part = refs[g]
        q[g] = part[:count].astype(F32) + part[count : 2 * count].astype(F32)
        rows[g] = part[2 * count :]


def start_kernel(
    fine_rays_in,
    coarse_rays_in,
    fine_in,
    coarse_in,
    fine_weight_in,
    coarse_weight_in,
    fine_axial_in,
    coarse_axial_in,
    measured_in,
    ray_weight_in,
    blocks,
    hits,
    mine,
    theirs,
    rows,
    out,
    short,
    own_rays,
    fine_rays,
    coarse_rays,
    fine,
    coarse,
    fine_weight,
    coarse_weight,
    fine_axial,
    coarse_axial,
    measured,
    ray_weight,
    scratch,
    sems,
    chunk_sems,
):
    me = lax.axis_index("slab")
    core = me % 2
    fz, cells = fine.shape
    half = cells // 2
    sources = (
        (fine_axial_in, fine_axial),
        (coarse_axial_in, coarse_axial),
        (ray_weight_in, ray_weight),
        (measured_in, measured),
        (fine_weight_in, fine_weight),
        (coarse_weight_in, coarse_weight),
    )
    others = [fetch(a, b, sems.at[i]) for i, (a, b) in enumerate(sources)]
    steps = chunk_sems.shape[0]
    chunk = cells // steps
    copies = []
    for i in range(steps):
        part = pl.ds(i * chunk, chunk)
        copies.append(
            [
                fetch(fine_in.at[:, part], fine.at[:, part], chunk_sems.at[i, 0]),
                fetch(coarse_in.at[:, part], coarse.at[:, part], chunk_sems.at[i, 1]),
                fetch(fine_rays_in.at[:, part, :], fine_rays.at[:, part, :], chunk_sems.at[i, 2]),
                fetch(
                    coarse_rays_in.at[:, part, :], coarse_rays.at[:, part, :], chunk_sems.at[i, 3]
                ),
            ]
        )
    for copy in others:
        copy.wait()

    views, _, det = fine_axial.shape
    columns = ray_weight.shape[2]
    total = views * columns
    span = views * det
    own = ray_weight.shape[0]
    coarse_depth = hit_depths(coarse_axial, hits)
    fine_depth = hit_depths(fine_axial, hits)
    wide = max(span, total)
    weight = jnp.concatenate([ray_weight[:, v, :] for v in range(views)], axis=1)
    fine_wide = jnp.concatenate(fine_depth, axis=1)
    if wide > total:
        weight = jnp.concatenate([weight, jnp.zeros((own, wide - total), F32)], axis=1)
    if wide > span:
        fine_wide = jnp.concatenate([fine_wide, jnp.zeros((fz, wide - span), F32)], axis=1)
    stack = [weight, fine_wide]
    if own + fz < PACK:
        stack.append(jnp.zeros((PACK - own - fz, wide), F32))
    packed = jnp.concatenate(coarse_depth + [jnp.concatenate(stack, axis=0)], axis=1).astype(BF16)
    for p in range((span + wide) // total):
        rows[p * PACK : (p + 1) * PACK] = packed[:, p * total : (p + 1) * total]

    parts = PACK // fz
    empty = jnp.zeros((1, LANES), F32)
    share = own_rays.shape[2]
    groups = half // share
    for target, side in ((mine, core), (theirs, 1 - core)):
        begin = pl.multiple_of(side * half + lax.axis_index("view") * share, LANES)
        keep = keep_row(blocks, begin, share)
        target[:, :share] = (coarse_weight[:, pl.ds(begin, share)] * keep).astype(BF16)
        weight = fine_weight[:, pl.ds(begin, share)]
        for c in range(packed_tiles(share, fz)):
            pieces = []
            for i in range(fz):
                for k in range(parts):
                    t = c * parts + k
                    inside = t * LANES < share
                    piece = weight[i : i + 1, t * LANES : (t + 1) * LANES] if inside else empty
                    pieces.append(piece)
            column = slice(share + c * LANES, share + (c + 1) * LANES)
            target[:, column] = jnp.concatenate(pieces, axis=0).astype(BF16)

    fine_sum = coarse_sum = None
    for i in range(steps):
        part = slice(i * chunk, (i + 1) * chunk)
        for copy in copies[i]:
            copy.wait()
        keep = keep_row(blocks, i * chunk, chunk)
        fine_rows = fine[:, part].astype(BF16)
        coarse_rows = (coarse[:, part] * keep).astype(BF16)
        fine_wide = jnp.concatenate([fine_rays[v, part, :] for v in range(views)], axis=1)
        coarse_wide = jnp.concatenate([coarse_rays[v, part, :] for v in range(views)], axis=1)
        fine_part = dot(fine_rows, fine_wide, ((1,), (0,)))
        coarse_part = dot(coarse_rows, coarse_wide, ((1,), (0,)))
        fine_sum = fine_part if fine_sum is None else fine_sum + fine_part
        coarse_sum = coarse_part if coarse_sum is None else coarse_sum + coarse_part
    held = pl.ds(share_start(cells, groups), share)
    outgoing = [
        fetch(fine_rays.at[:, held, :], own_rays.at[0], sems.at[6]),
        fetch(coarse_rays.at[:, held, :], own_rays.at[1], sems.at[7]),
    ]
    pad = jnp.zeros((PACK - fz, total), F32)
    moment = jnp.concatenate([coarse_sum, fine_sum, pad], axis=0).astype(BF16)
    pad = jnp.zeros((PACK - fz, det), F32)
    row = lax.broadcasted_iota(jnp.int32, (det, columns), 0) - me * own
    for v in range(views):
        depth = jnp.concatenate([coarse_depth[v], fine_depth[v], pad], axis=0).astype(BF16)
        where = slice(v * columns, (v + 1) * columns)
        projection = dot(depth, moment[:, where], ((0,), (0,)))
        given = jnp.zeros((det, columns), F32)
        for i in range(own):
            given = jnp.where(row == i, measured[i : i + 1, v, :], given)
        scratch[:, where] = given - projection
    kept = pl.ds(pl.multiple_of(core * (det // 2), PACK), det // 2)
    sent = pl.ds(pl.multiple_of((1 - core) * (det // 2), PACK), det // 2)
    out[...] = scratch[kept, :]
    short[...] = scratch[sent, :].astype(BF16)
    for copy in outgoing:
        copy.wait()


def slab_of(block, bits):
    me = lax.axis_index("slab")
    apart = jnp.zeros_like(block)
    for place, bit in enumerate(bits):
        apart = apart + ((block >> (place + 1)) & 1) * bit
    return ((me - me % 2) ^ apart) + (block & 1)


def rows_kernel(own, fz, bits, mine, theirs, q_mine, q_theirs, *refs):
    coarse_out, fine_out, coarse_turned, fine_turned, out, q_out = refs
    lead = lax.axis_index("slab") % 2 == 0
    kept = q_mine.shape[1]
    for g in range(q_mine.shape[0]):
        ours, others = q_mine[g], q_theirs[g]
        q_out[g, :kept] = jnp.where(lead, ours, others)
        q_out[g, kept:] = jnp.where(lead, others, ours)
    groups, held, total = mine.shape
    slabs = coarse_out.shape[1] // PACK
    height = 2 * held // slabs
    pieces = height // PACK
    det = out.shape[1]
    count = slabs * PACK
    shape = (slabs * own, count)
    w = lax.broadcasted_iota(jnp.int32, shape, 0)
    column = lax.broadcasted_iota(jnp.int32, shape, 1)
    block, row = column // PACK, column % PACK
    match = (row < own) & (w == slab_of(block, bits) * own + row)
    to_weight = jnp.where(match, 1.0, 0.0).astype(BF16)
    shape = (slabs * fz, count)
    z = lax.broadcasted_iota(jnp.int32, shape, 0)
    column = lax.broadcasted_iota(jnp.int32, shape, 1)
    to_fine = jnp.where(column == (z // fz) * PACK + own + z % fz, 1.0, 0.0).astype(BF16)
    for g in range(groups):
        own_rows, other_rows = mine[g].astype(F32), theirs[g].astype(F32)
        even = jnp.where(lead, own_rows, other_rows).astype(BF16)
        odd = jnp.where(lead, other_rows, own_rows).astype(BF16)
        cuts = []
        for p in range(pieces):
            blocks = [
                (even, odd)[j % 2][(j // 2) * height + p * PACK :][:PACK] for j in range(slabs)
            ]
            cuts.append(jnp.concatenate(blocks, axis=0))
        coarse = jnp.concatenate(cuts[: pieces // 2], axis=1)
        side = jnp.concatenate(cuts[pieces // 2 :], axis=1)
        fine = dot(to_fine, side, ((1,), (0,)))
        coarse_out[g] = coarse
        fine_out[g] = fine.astype(BF16)
        wide = coarse.astype(F32)
        for v in range(coarse.shape[1] // det):
            where = slice(v * det, (v + 1) * det)
            coarse_turned[g, v] = wide[:, where].T.astype(BF16)
            fine_turned[g, v] = fine[:, where].T.astype(BF16)
        out[g] = dot(to_weight, side, ((1,), (0,)))[:, :total]


def weights_kernel(fz, order, mine, received, coarse_out, fine_out):
    held = mine.shape[0]
    slabs = 2 * held
    count = slabs * PACK
    parts = PACK // fz
    size = fine_out.shape[1]
    tiles = packed_tiles(size, fz)
    blocks = [(mine, received)[k // held].at[k % held] for k in order]
    for j, block in enumerate(blocks):
        coarse_out[j * PACK : (j + 1) * PACK] = block[:, :size]
    source = jnp.concatenate([block[:, size : size + tiles * LANES] for block in blocks], axis=0)
    shape = (slabs * fz, count)
    z = lax.broadcasted_iota(jnp.int32, shape, 0)
    column = lax.broadcasted_iota(jnp.int32, shape, 1)
    for k in range(parts):
        choose = jnp.where(column == (z // fz) * PACK + (z % fz) * parts + k, 1.0, 0.0)
        chosen = dot(choose.astype(BF16), source, ((1,), (0,)))
        for c in range(tiles):
            t = c * parts + k
            if t * LANES < size:
                fine_out[:, t * LANES : (t + 1) * LANES] = chosen[
                    :, c * LANES : (c + 1) * LANES
                ].astype(BF16)


def residuals(q, deltas, weights):
    groups = q.shape[0]
    current = [q[g] for g in range(groups)]
    results = [[weights[g] * current[g] for g in range(groups)]]
    for delta in deltas:
        current = [current[g] - delta[g].astype(F32) for g in range(groups)]
        results.append([weights[g] * current[g] for g in range(groups)])
    return results


def spread(depth, residual, views):
    det, columns = residual.shape[0], residual.shape[1] // views
    pieces = [
        dot(
            depth[:, v * det : (v + 1) * det],
            residual[:, v * columns : (v + 1) * columns],
            ((1,), (0,)),
        )
        for v in range(views)
    ]
    return jnp.concatenate(pieces, axis=1)


def spread_kernel(views, q, weights, fine_depth, coarse_depth, fine_out, coarse_out):
    for g in range(q.shape[0]):
        residual = (weights[g] * q[g]).astype(BF16)
        fine_out[g] = spread(fine_depth[g], residual, views).astype(BF16)
        coarse_out[g] = spread(coarse_depth[g], residual, views).astype(BF16)


def group_rays(held, part, g, cut):
    return jnp.concatenate([held[g][part, v, cut, :] for v in range(held[g].shape[1])], axis=1)


def step_kernel(groups, views, ready, *refs):
    refs = list(refs)
    if ready:
        spreads = [refs.pop(0), refs.pop(0)]
    else:
        q, delta, weights, fine_depth, coarse_depth = refs[:5]
        refs = refs[5:]
        residual = residuals(q, [delta], weights)[-1]
        residual = [r.astype(BF16) for r in residual]
        spreads = [
            [spread(depth[g], residual[g], views).astype(BF16) for g in range(groups)]
            for depth in (fine_depth, coarse_depth)
        ]
    turned = refs[:2]
    coarse_weights, fine_weights = refs[2:4]
    held = refs[4:-1]
    out = refs[-1]
    size = fine_weights.shape[1]
    columns = held[0].shape[3]
    chunk = min(size, 512)
    results = [None] * groups
    for part in range(2):
        moments = [None] * groups
        for c in range(size // chunk):
            cut = slice(c * chunk, (c + 1) * chunk)
            if part == 0:
                weight = fine_weights[:, cut]
            else:
                weight = coarse_weights[:, cut]
            rays = [group_rays(held, part, g, cut) for g in range(groups)]
            back = dot(spreads[part][0], rays[0], ((1,), (1,)))
            for g in range(1, groups):
                back = back + dot(spreads[part][g], rays[g], ((1,), (1,)))
            change = (weight.astype(F32) * back).astype(BF16)
            for g in range(groups):
                moment = dot(change, rays[g], ((1,), (0,)))
                moments[g] = moment if moments[g] is None else moments[g] + moment
        for g in range(groups):
            moment = moments[g].astype(BF16)
            pieces = [
                dot(turned[part][g, v], moment[:, v * columns : (v + 1) * columns], ((1,), (0,)))
                for v in range(views)
            ]
            value = jnp.concatenate(pieces, axis=1)
            results[g] = value if results[g] is None else results[g] + value
    for g in range(groups):
        out[g] = results[g].astype(BF16)


def add_kernel(bit, mine, received, out):
    for g in range(mine.shape[0]):
        out[g] = (mine[g].astype(F32) + received[g ^ bit].astype(F32)).astype(BF16)


def tail_kernel(groups, views, q, *refs):
    deltas = refs[:2]
    weights, fine_depth, coarse_depth = refs[2:5]
    held = refs[5:-2]
    fine_out, coarse_out = refs[-2:]
    size = coarse_out.shape[1]
    chunk = min(size, 512)
    history = residuals(q, deltas, weights)
    rows = (fine_out.shape[0], coarse_out.shape[0])
    spreads = ([], [])
    for g in range(groups):
        value = history[0][g]
        for other in history[1:]:
            value = value + other[g]
        high, low = in_two(value)
        for part, depth in enumerate((fine_depth[g, : rows[0]], coarse_depth[g, : rows[1]])):
            pair = in_two(spread(depth, high, views) + spread(depth, low, views))
            spreads[part].append(jnp.concatenate(pair, axis=0))
    for part, out in enumerate((fine_out, coarse_out)):
        for c in range(size // chunk):
            cut = slice(c * chunk, (c + 1) * chunk)
            back = None
            for g in range(groups):
                value = dot(spreads[part][g], group_rays(held, part, g, cut), ((1,), (1,)))
                back = value if back is None else back + value
            out[:, cut] = (back[: rows[part]] + back[rows[part] :]).astype(BF16)


def sort_kernel(groups, *refs):
    pieces, outs = refs[:-4], refs[-4:]
    lead = lax.axis_index("slab") % 2 == 0
    view = lax.axis_index("view")
    for part in range(2):
        mine, theirs = outs[2 * part : 2 * part + 2]
        rows = mine.shape[0]
        size = pieces[part].shape[1]
        for g in range(groups):
            value = pieces[2 * g + part][...].astype(F32)
            lower, upper = value[:rows], value[rows:]
            where = pl.ds(pl.multiple_of((view ^ g) * size, LANES), size)
            mine[:, where] = jnp.where(lead, lower, upper).astype(BF16)
            theirs[:, where] = jnp.where(lead, upper, lower).astype(BF16)


def final_kernel(*refs):
    mine, received = refs[:2], refs[2:4]
    fine, coarse, fw, cw, blocks, fine_out, coarse_out = refs[4:]
    core = lax.axis_index("slab") % 2
    half = mine[0].shape[1]
    for source, side in ((mine, core), (received, 1 - core)):
        start = pl.multiple_of(side * half, half)
        where = pl.ds(start, half)
        keep = keep_row(blocks, start, half)
        fine_out[:, where] = fine[:, where] + fw[:, where] * source[0][...].astype(F32)
        coarse_out[:, where] = (
            coarse[:, where] + cw[:, where] * source[1][...].astype(F32)
        ) * keep


def make_body(slabs, groups):
    far_bits = [1 << k for k in range(slabs.bit_length() - 2, 1, -1)]
    view_bits = [1 << k for k in range(groups.bit_length() - 1)]

    def along_slab(value, bit):
        return swap(value, "slab", slabs, bit)

    def body(
        fine_volume,
        coarse_volume,
        fine_rays,
        coarse_rays,
        fine_axial,
        coarse_axial,
        measured,
        ray_weight,
        fine_cell_weight,
        coarse_cell_weight,
        margin_blocks,
        ray_hits,
    ):
        views, cells, columns = fine_rays.shape
        det = fine_axial.shape[2]
        fz, cz = fine_volume.shape[0], coarse_volume.shape[0]
        own = measured.shape[0]
        total = views * columns
        span = max(views * det, total)
        share = cells // 2 // groups
        lead = lax.axis_index("slab") % 2 == 0
        width = share + packed_tiles(share, fz) * LANES

        taken = in_hbm(
            fine_rays,
            coarse_rays,
            fine_volume,
            coarse_volume,
            fine_cell_weight,
            coarse_cell_weight,
            fine_axial,
            coarse_axial,
            measured,
            ray_weight,
        )
        height = PACK * ((views * det + span) // total)
        mine, theirs, rows, q, short, own_rays = call(
            start_kernel,
            "start",
            (
                shaped((PACK, width), BF16),
                shaped((PACK, width), BF16),
                shaped((height, total), BF16),
                shaped((det // 2, total), F32),
                shaped((det // 2, total), BF16),
                shaped((2, views, share, columns), BF16),
            ),
            [HBM] * len(taken) + [SMEM] * 2,
            scratch_like(*taken)
            + [
                pltpu.VMEM((det, total), F32),
                pltpu.SemaphoreType.DMA((8,)),
                pltpu.SemaphoreType.DMA((4, 4)),
            ],
        )(*taken, *in_hbm(margin_blocks, ray_hits))

        def to_views(value):
            values = [value]
            for bit in view_bits:
                values += [swap(one, "view", groups, bit) for one in values]
            return values

        rows_half = det // 2
        got = {}

        def begin(stage, token):
            waits = [] if token is None else [token]
            if SOURCE["rays"] == stage:
                got["rays"] = []
                for bits in range(1, groups):
                    value = call(
                        functools.partial(take_kernel, groups, bits),
                        "take_rays",
                        shaped((2, views, share, columns), BF16),
                        [HBM] * 2 + [ANY] * len(waits),
                        [pltpu.SemaphoreType.DMA((2,))],
                    )(*in_hbm(fine_rays, coarse_rays), *waits)
                    got["rays"].append(swap(value, "view", groups, bits))
            if SOURCE["weights"] == stage:
                packed = call(
                    pair_kernel,
                    "pair",
                    shaped((2, PACK, width), BF16),
                    [VMEM] * 2 + [ANY] * len(waits),
                )(mine, along_slab(theirs, 1), *waits)
                for index, bit in enumerate(far_bits + [2]):
                    hop = along_slab(packed, bit)
                    got["w%d" % index] = [hop]
                    if bit != 2:
                        packed = jnp.concatenate([packed, hop])
                got["weights"] = (packed, hop)

        def waits_of(stage):
            found = []
            for name, where in AWAITED.items():
                if where == stage:
                    found += got.get(name, [])
            return found

        begin("start", None)
        waits = waits_of("core")
        q, mixed = call(
            join_core_kernel,
            "join_core",
            (shaped((rows_half, total), F32), shaped((rows_half + height, total), BF16)),
            [VMEM] * 3 + [ANY] * len(waits),
        )(q, along_slab(short, 1), rows, *waits)
        begin("core", mixed)
        for index, bit in enumerate([2] + far_bits):
            last = index == len(far_bits)
            name = "last" if last else "hop%d" % index
            waits = waits_of(name)
            size = 2 * mixed.shape[0] - rows_half + (rows_half if last else 0)
            q, mixed = call(
                functools.partial(join_hop_kernel, last),
                "join_hop",
                (shaped(q.shape, F32), shaped((size, total), BF16)),
                [VMEM] * 3 + [ANY] * len(waits),
            )(q, mixed, along_slab(mixed, bit), *waits)
            begin(name, mixed)
        waits = waits_of("views")
        q, rows = call(
            functools.partial(join_views_kernel, rows_half),
            "join_views",
            (
                shaped((groups, rows_half, total), F32),
                shaped((groups, mixed.shape[0] - 2 * rows_half, total), BF16),
            ),
            [VMEM] * groups + [ANY] * len(waits),
        )(*to_views(mixed), *waits)
        count = len(far_bits)
        order = tuple(
            (j & 1) + 2 * (j >> 2) + (((j >> 1) & 1) << (count + 1)) for j in range(slabs)
        )
        coarse_depth, fine_depth, coarse_turned, fine_turned, weights, q = call(
            functools.partial(rows_kernel, own, fz, [2] + far_bits),
            "unpack_rows",
            (
                shaped((groups, slabs * PACK, span), BF16),
                shaped((groups, slabs * fz, span), BF16),
                shaped((groups, views, det, slabs * PACK), BF16),
                shaped((groups, views, det, slabs * fz), BF16),
                shaped((groups, det, total), F32),
                shaped((groups, det, total), F32),
            ),
            [VMEM] * 4,
        )(rows, along_slab(rows, 1), q, along_slab(q, 1))
        coarse_weights, fine_weights = call(
            functools.partial(weights_kernel, fz, order),
            "unpack_weights",
            (shaped((slabs * PACK, share), BF16), shaped((slabs * fz, share), BF16)),
            [VMEM] * 2,
        )(*got["weights"])
        spreads = call(
            functools.partial(spread_kernel, views),
            "spread",
            (
                shaped((groups, slabs * fz, total), BF16),
                shaped((groups, slabs * PACK, total), BF16),
            ),
            [VMEM] * 4,
        )(q, weights, fine_depth, coarse_depth)
        rays = [own_rays] + got["rays"]
        held = (fine_turned, coarse_turned, coarse_weights, fine_weights, *rays)
        def add(mine, received, bit):
            return call(
                functools.partial(add_kernel, bit),
                "add",
                shaped((groups, det, total), BF16),
                [VMEM] * 2,
            )(mine, received)

        deltas = []
        for ready, inputs in ((True, spreads), (False, None)):
            if not ready:
                inputs = (q, *deltas, weights, fine_depth, coarse_depth)
            delta = call(
                functools.partial(step_kernel, groups, views, ready),
                "ray_space_step",
                shaped((groups, det, total), BF16),
                [VMEM] * (len(inputs) + len(held)),
            )(*inputs, *held)
            delta = add(delta, along_slab(delta, 1), 0)
            for bit in view_bits:
                delta = add(delta, swap(delta, "view", groups, bit), bit)
            deltas.append(delta)
        inputs = (q, *deltas, weights, fine_depth, coarse_depth, *rays)
        pieces = call(
            functools.partial(tail_kernel, groups, views),
            "back_projection",
            (shaped((2 * fz, share), BF16), shaped((2 * PACK, share), BF16)),
            [VMEM] * len(inputs),
        )(*inputs)
        pieces = list(pieces)
        for bit in view_bits:
            pieces += [swap(value, "view", groups, bit) for value in pieces]
        fine_ours, fine_theirs, coarse_ours, coarse_theirs = call(
            functools.partial(sort_kernel, groups),
            "sort",
            (shaped((fz, cells // 2), BF16),) * 2 + (shaped((PACK, cells // 2), BF16),) * 2,
            [VMEM] * len(pieces),
        )(*pieces)
        return call(
            final_kernel,
            "update",
            (shaped(fine_volume.shape, F32), shaped(coarse_volume.shape, F32)),
            [VMEM] * 8 + [SMEM],
        )(
            fine_ours,
            coarse_ours,
            along_slab(fine_theirs, 1),
            along_slab(coarse_theirs, 1),
            fine_volume,
            coarse_volume,
            fine_cell_weight,
            coarse_cell_weight,
            margin_blocks,
        )

    return body


def solution(mesh):
    return jax.shard_map(
        make_body(mesh.shape["slab"], mesh.shape["view"]),
        mesh=mesh,
        in_specs=(
            P("slab", None),
            P("slab", None),
            P("view", None, None),
            P("view", None, None),
            P("view", "slab", None),
            P("view", "slab", None),
            P("slab", "view", None),
            P("slab", "view", None),
            P("slab", None),
            P("slab", None),
            P("slab", None),
            P("view", "slab", None),
        ),
        out_specs=(P("slab", None), P("slab", None)),
        check_vma=False,
    )
```

```python
import functools
import jax
import jax.numpy as jnp
from jax import lax
from jax.experimental import pallas as pl
from jax.experimental.pallas import tpu as pltpu
from jax.sharding import PartitionSpec as P

BLOCK = 128
LANES = 128
PACK = 16
F32 = jnp.float32
BF16 = jnp.bfloat16
PARAMS = pltpu.CompilerParams(vmem_limit_bytes=24 * 1024 * 1024)
VMEM = pl.BlockSpec(memory_space=pltpu.VMEM)
SMEM = pl.BlockSpec(memory_space=pltpu.SMEM)
ANY = pl.BlockSpec(memory_space=pl.ANY)
HBM = pl.BlockSpec(memory_space=pltpu.HBM)
SOURCE = {"rays": "start", "weights": "start"}
AWAITED = {"rays": "views"}
QUICK = pl.CostEstimate(flops=1, bytes_accessed=1, transcendentals=0)


def fetch(source, target, sem):
    copy = pltpu.make_async_copy(source, target, sem)
    copy.start()
    return copy


def in_hbm(*arrays):
    return [pltpu.with_memory_space_constraint(a, pltpu.HBM) for a in arrays]


def scratch_like(*arrays):
    return [pltpu.VMEM(a.shape, a.dtype) for a in arrays]


def shaped(shape, dtype):
    return jax.ShapeDtypeStruct(shape, dtype)


def call(kernel, name, out_shape, in_specs, scratch=()):
    many = isinstance(out_shape, tuple)
    return pl.pallas_call(
        kernel,
        out_shape=out_shape,
        in_specs=in_specs,
        out_specs=(VMEM,) * len(out_shape) if many else VMEM,
        scratch_shapes=list(scratch),
        compiler_params=PARAMS,
        cost_estimate=QUICK,
        name=name,
    )


def swap(value, axis, size, bits):
    return lax.ppermute(value, axis, [(i, i ^ bits) for i in range(size)])


def dot(a, b, dims):
    return lax.dot_general(a, b, (dims, ((), ())), preferred_element_type=F32)


def in_two(value):
    high = value.astype(BF16)
    return high, (value - high.astype(F32)).astype(BF16)


def keep_row(blocks_ref, start, width):
    ids = (lax.broadcasted_iota(jnp.int32, (1, width), 1) + start) // BLOCK
    keep = jnp.ones((1, width), F32)
    for k in range(blocks_ref.shape[1]):
        keep = jnp.where(ids == blocks_ref[0, k], 0.0, keep)
    return keep


def share_start(cells, groups, bits=0):
    core = lax.axis_index("slab") % 2
    share = cells // 2 // groups
    return pl.multiple_of(core * (cells // 2) + (lax.axis_index("view") ^ bits) * share, LANES)


def packed_tiles(cells, fz):
    parts = PACK // fz
    return -(-(cells // LANES) // parts)


def pack_fine(rows):
    fz, size = rows.shape
    parts = PACK // fz
    empty = jnp.zeros((1, LANES), rows.dtype)
    columns = []
    for c in range(packed_tiles(size, fz)):
        pieces = []
        for i in range(fz):
            for k in range(parts):
                t = c * parts + k
                inside = t * LANES < size
                pieces.append(rows[i : i + 1, t * LANES : (t + 1) * LANES] if inside else empty)
        columns.append(jnp.concatenate(pieces, axis=0))
    return jnp.concatenate(columns, axis=1)


def unpack_fine(packed, fz, size):
    parts = PACK // fz
    rows = []
    for i in range(fz):
        pieces = []
        for t in range(size // LANES):
            row, column = i * parts + t % parts, t // parts * LANES
            pieces.append(packed[row : row + 1, column : column + LANES])
        rows.append(jnp.concatenate(pieces, axis=1))
    return jnp.concatenate(rows, axis=0)


def hit_depths(axial, hits):
    views, _, det = axial.shape
    tiles = hits.shape[2]
    tile = lax.broadcasted_iota(jnp.int32, (1, det), 1) // (det // tiles)
    result = []
    for v in range(views):
        hit = jnp.zeros((1, det), F32)
        for t in range(tiles):
            hit = jnp.where(tile == t, hits[v, 0, t].astype(F32), hit)
        result.append(axial[v].astype(F32) * hit)
    return result


def take_kernel(groups, bits, fine_rays, coarse_rays, *refs):
    out, sems = refs[-2:]
    cells = pl.ds(share_start(fine_rays.shape[1], groups, bits), out.shape[2])
    copies = [
        fetch(rays.at[:, cells, :], out.at[part], sems.at[part])
        for part, rays in enumerate((fine_rays, coarse_rays))
    ]
    for copy in copies:
        copy.wait()


def pair_kernel(mine, received, *refs):
    out = refs[-1]
    lead = lax.axis_index("slab") % 2 == 0
    own, other = mine[...].astype(F32), received[...].astype(F32)
    out[0] = jnp.where(lead, own, other).astype(BF16)
    out[1] = jnp.where(lead, other, own).astype(BF16)


def join_core_kernel(q, received, rows, *refs):
    total, out = refs[-2:]
    count = q.shape[0]
    value = q[...] + received[...].astype(F32)
    total[...] = value
    out[:count] = value.astype(BF16)
    out[count:] = rows[...]


def join_hop_kernel(last, q, mine, received, *refs):
    total, out = refs[-2:]
    count = q.shape[0]
    value = q[...] + received[:count].astype(F32)
    total[...] = value
    high, low = in_two(value)
    out[:count] = high
    base = count
    if last:
        out[count : 2 * count] = low
        base = 2 * count
    held = mine.shape[0] - count
    out[base : base + held] = mine[count:]
    out[base + held :] = received[count:]


def join_views_kernel(count, *refs):
    q, rows = refs[-2:]
    for g in range(q.shape[0]):
        part = refs[g]
        q[g] = part[:count].astype(F32) + part[count : 2 * count].astype(F32)
        rows[g] = part[2 * count :]


def start_kernel(
    fine_rays_in,
    coarse_rays_in,
    fine_in,
    coarse_in,
    fine_weight_in,
    coarse_weight_in,
    fine_axial_in,
    coarse_axial_in,
    measured_in,
    ray_weight_in,
    blocks,
    hits,
    mine,
    theirs,
    rows,
    out,
    short,
    own_rays,
    fine_rays,
    coarse_rays,
    fine,
    coarse,
    fine_weight,
    coarse_weight,
    fine_axial,
    coarse_axial,
    measured,
    ray_weight,
    scratch,
    sems,
    chunk_sems,
):
    me = lax.axis_index("slab")
    core = me % 2
    fz, cells = fine.shape
    half = cells // 2
    sources = (
        (fine_axial_in, fine_axial),
        (coarse_axial_in, coarse_axial),
        (ray_weight_in, ray_weight),
        (measured_in, measured),
        (fine_weight_in, fine_weight),
        (coarse_weight_in, coarse_weight),
    )
    others = [fetch(a, b, sems.at[i]) for i, (a, b) in enumerate(sources)]
    steps = chunk_sems.shape[0]
    chunk = cells // steps
    copies = []
    for i in range(steps):
        part = pl.ds(i * chunk, chunk)
        copies.append(
            [
                fetch(fine_in.at[:, part], fine.at[:, part], chunk_sems.at[i, 0]),
                fetch(coarse_in.at[:, part], coarse.at[:, part], chunk_sems.at[i, 1]),
                fetch(fine_rays_in.at[:, part, :], fine_rays.at[:, part, :], chunk_sems.at[i, 2]),
                fetch(
                    coarse_rays_in.at[:, part, :], coarse_rays.at[:, part, :], chunk_sems.at[i, 3]
                ),
            ]
        )
    share = own_rays.shape[2]
    groups = half // share
    held = pl.ds(share_start(cells, groups), share)
    outgoing = [
        fetch(fine_rays_in.at[:, held, :], own_rays.at[0], sems.at[6]),
        fetch(coarse_rays_in.at[:, held, :], own_rays.at[1], sems.at[7]),
    ]
    for copy in others:
        copy.wait()

    views, _, det = fine_axial.shape
    columns = ray_weight.shape[2]
    total = views * columns
    span = views * det
    own = ray_weight.shape[0]
    coarse_depth = hit_depths(coarse_axial, hits)
    fine_depth = hit_depths(fine_axial, hits)
    wide = max(span, total)
    weight = jnp.concatenate([ray_weight[:, v, :] for v in range(views)], axis=1)
    fine_wide = jnp.concatenate(fine_depth, axis=1)
    if wide > total:
        weight = jnp.concatenate([weight, jnp.zeros((own, wide - total), F32)], axis=1)
    if wide > span:
        fine_wide = jnp.concatenate([fine_wide, jnp.zeros((fz, wide - span), F32)], axis=1)
    stack = [weight, fine_wide]
    if own + fz < PACK:
        stack.append(jnp.zeros((PACK - own - fz, wide), F32))
    packed = jnp.concatenate(coarse_depth + [jnp.concatenate(stack, axis=0)], axis=1).astype(BF16)
    for p in range((span + wide) // total):
        rows[p * PACK : (p + 1) * PACK] = packed[:, p * total : (p + 1) * total]

    for target, side in ((mine, core), (theirs, 1 - core)):
        begin = pl.multiple_of(side * half + lax.axis_index("view") * share, LANES)
        keep = keep_row(blocks, begin, share)
        target[:, :share] = (coarse_weight[:, pl.ds(begin, share)] * keep).astype(BF16)
        target[:, share:] = pack_fine(fine_weight[:, pl.ds(begin, share)]).astype(BF16)

    fine_sum = coarse_sum = None
    for i in range(steps):
        part = slice(i * chunk, (i + 1) * chunk)
        for copy in copies[i]:
            copy.wait()
        keep = keep_row(blocks, i * chunk, chunk)
        fine_rows = fine[:, part].astype(BF16)
        coarse_rows = (coarse[:, part] * keep).astype(BF16)
        fine_wide = jnp.concatenate([fine_rays[v, part, :] for v in range(views)], axis=1)
        coarse_wide = jnp.concatenate([coarse_rays[v, part, :] for v in range(views)], axis=1)
        fine_part = dot(fine_rows, fine_wide, ((1,), (0,)))
        coarse_part = dot(coarse_rows, coarse_wide, ((1,), (0,)))
        fine_sum = fine_part if fine_sum is None else fine_sum + fine_part
        coarse_sum = coarse_part if coarse_sum is None else coarse_sum + coarse_part
    pad = jnp.zeros((PACK - fz, total), F32)
    moment = jnp.concatenate([coarse_sum, fine_sum, pad], axis=0).astype(BF16)
    pad = jnp.zeros((PACK - fz, det), F32)
    row = lax.broadcasted_iota(jnp.int32, (det, columns), 0) - me * own
    for v in range(views):
        depth = jnp.concatenate([coarse_depth[v], fine_depth[v], pad], axis=0).astype(BF16)
        where = slice(v * columns, (v + 1) * columns)
        projection = dot(depth, moment[:, where], ((0,), (0,)))
        given = jnp.zeros((det, columns), F32)
        for i in range(own):
            given = jnp.where(row == i, measured[i : i + 1, v, :], given)
        scratch[:, where] = given - projection
    kept = pl.ds(pl.multiple_of(core * (det // 2), PACK), det // 2)
    sent = pl.ds(pl.multiple_of((1 - core) * (det // 2), PACK), det // 2)
    out[...] = scratch[kept, :]
    short[...] = scratch[sent, :].astype(BF16)
    for copy in outgoing:
        copy.wait()


def slab_of(block, bits):
    me = lax.axis_index("slab")
    apart = jnp.zeros_like(block)
    for place, bit in enumerate(bits):
        apart = apart + ((block >> (place + 1)) & 1) * bit
    return ((me - me % 2) ^ apart) + (block & 1)


def rows_kernel(own, fz, bits, mine, theirs, q_mine, q_theirs, *refs):
    coarse_out, fine_out, coarse_turned, fine_turned, out, q_out = refs
    lead = lax.axis_index("slab") % 2 == 0
    kept = q_mine.shape[1]
    for g in range(q_mine.shape[0]):
        ours, others = q_mine[g], q_theirs[g]
        q_out[g, :kept] = jnp.where(lead, ours, others)
        q_out[g, kept:] = jnp.where(lead, others, ours)
    groups, held, total = mine.shape
    slabs = coarse_out.shape[1] // PACK
    height = 2 * held // slabs
    pieces = height // PACK
    det = out.shape[1]
    count = slabs * PACK
    shape = (slabs * own, count)
    w = lax.broadcasted_iota(jnp.int32, shape, 0)
    column = lax.broadcasted_iota(jnp.int32, shape, 1)
    block, row = column // PACK, column % PACK
    match = (row < own) & (w == slab_of(block, bits) * own + row)
    to_weight = jnp.where(match, 1.0, 0.0).astype(BF16)
    shape = (slabs * fz, count)
    z = lax.broadcasted_iota(jnp.int32, shape, 0)
    column = lax.broadcasted_iota(jnp.int32, shape, 1)
    to_fine = jnp.where(column == (z // fz) * PACK + own + z % fz, 1.0, 0.0).astype(BF16)
    for g in range(groups):
        own_rows, other_rows = mine[g].astype(F32), theirs[g].astype(F32)
        even = jnp.where(lead, own_rows, other_rows).astype(BF16)
        odd = jnp.where(lead, other_rows, own_rows).astype(BF16)
        cuts = []
        for p in range(pieces):
            blocks = [
                (even, odd)[j % 2][(j // 2) * height + p * PACK :][:PACK] for j in range(slabs)
            ]
            cuts.append(jnp.concatenate(blocks, axis=0))
        coarse = jnp.concatenate(cuts[: pieces // 2], axis=1)
        side = jnp.concatenate(cuts[pieces // 2 :], axis=1)
        fine = dot(to_fine, side, ((1,), (0,)))
        coarse_out[g] = coarse
        fine_out[g] = fine.astype(BF16)
        wide = coarse.astype(F32)
        for v in range(coarse.shape[1] // det):
            where = slice(v * det, (v + 1) * det)
            coarse_turned[g, v] = wide[:, where].T.astype(BF16)
            fine_turned[g, v] = fine[:, where].T.astype(BF16)
        out[g] = dot(to_weight, side, ((1,), (0,)))[:, :total]


def weights_kernel(fz, order, mine, received, coarse_out, fine_out):
    held = mine.shape[0]
    slabs = 2 * held
    count = slabs * PACK
    parts = PACK // fz
    size = fine_out.shape[1]
    tiles = packed_tiles(size, fz)
    blocks = [(mine, received)[k // held].at[k % held] for k in order]
    for j, block in enumerate(blocks):
        coarse_out[j * PACK : (j + 1) * PACK] = block[:, :size]
    source = jnp.concatenate([block[:, size : size + tiles * LANES] for block in blocks], axis=0)
    shape = (slabs * fz, count)
    z = lax.broadcasted_iota(jnp.int32, shape, 0)
    column = lax.broadcasted_iota(jnp.int32, shape, 1)
    for k in range(parts):
        choose = jnp.where(column == (z // fz) * PACK + (z % fz) * parts + k, 1.0, 0.0)
        chosen = dot(choose.astype(BF16), source, ((1,), (0,)))
        for c in range(tiles):
            t = c * parts + k
            if t * LANES < size:
                fine_out[:, t * LANES : (t + 1) * LANES] = chosen[
                    :, c * LANES : (c + 1) * LANES
                ].astype(BF16)


def residuals(q, deltas, weights):
    groups = q.shape[0]
    current = [q[g] for g in range(groups)]
    results = [[weights[g] * current[g] for g in range(groups)]]
    for delta in deltas:
        current = [current[g] - delta[g].astype(F32) for g in range(groups)]
        results.append([weights[g] * current[g] for g in range(groups)])
    return results


def spread(depth, residual, views):
    det, columns = residual.shape[0], residual.shape[1] // views
    pieces = [
        dot(
            depth[:, v * det : (v + 1) * det],
            residual[:, v * columns : (v + 1) * columns],
            ((1,), (0,)),
        )
        for v in range(views)
    ]
    return jnp.concatenate(pieces, axis=1)


def spread_kernel(views, q, weights, fine_depth, coarse_depth, fine_out, coarse_out):
    for g in range(q.shape[0]):
        residual = (weights[g] * q[g]).astype(BF16)
        fine_out[g] = spread(fine_depth[g], residual, views).astype(BF16)
        coarse_out[g] = spread(coarse_depth[g], residual, views).astype(BF16)


def group_rays(held, part, g, cut):
    return jnp.concatenate([held[g][part, v, cut, :] for v in range(held[g].shape[1])], axis=1)


def step_kernel(groups, views, ready, *refs):
    refs = list(refs)
    if ready:
        spreads = [refs.pop(0), refs.pop(0)]
    else:
        q, delta, weights, fine_depth, coarse_depth = refs[:5]
        refs = refs[5:]
        residual = residuals(q, [delta], weights)[-1]
        residual = [r.astype(BF16) for r in residual]
        spreads = [
            [spread(depth[g], residual[g], views).astype(BF16) for g in range(groups)]
            for depth in (fine_depth, coarse_depth)
        ]
    turned = refs[:2]
    coarse_weights, fine_weights = refs[2:4]
    held = refs[4:-1]
    out = refs[-1]
    size = fine_weights.shape[1]
    columns = held[0].shape[3]
    chunk = min(size, 512)
    results = [None] * groups
    for part in range(2):
        moments = [None] * groups
        for c in range(size // chunk):
            cut = slice(c * chunk, (c + 1) * chunk)
            if part == 0:
                weight = fine_weights[:, cut]
            else:
                weight = coarse_weights[:, cut]
            rays = [group_rays(held, part, g, cut) for g in range(groups)]
            back = dot(spreads[part][0], rays[0], ((1,), (1,)))
            for g in range(1, groups):
                back = back + dot(spreads[part][g], rays[g], ((1,), (1,)))
            change = (weight.astype(F32) * back).astype(BF16)
            for g in range(groups):
                moment = dot(change, rays[g], ((1,), (0,)))
                moments[g] = moment if moments[g] is None else moments[g] + moment
        for g in range(groups):
            moment = moments[g].astype(BF16)
            pieces = [
                dot(turned[part][g, v], moment[:, v * columns : (v + 1) * columns], ((1,), (0,)))
                for v in range(views)
            ]
            value = jnp.concatenate(pieces, axis=1)
            results[g] = value if results[g] is None else results[g] + value
    for g in range(groups):
        out[g] = results[g].astype(BF16)


def add_kernel(bit, mine, received, out):
    for g in range(mine.shape[0]):
        out[g] = (mine[g].astype(F32) + received[g ^ bit].astype(F32)).astype(BF16)


def tail_kernel(fz, groups, views, q, *refs):
    deltas = refs[:2]
    weights, fine_depth, coarse_depth = refs[2:5]
    held = refs[5:-2]
    ours, theirs = refs[-2:]
    size = held[0].shape[2]
    chunk = min(size, 512)
    lead = lax.axis_index("slab") % 2 == 0
    history = residuals(q, deltas, weights)
    rows = (fz, PACK)
    spreads = ([], [])
    for g in range(groups):
        value = history[0][g]
        for other in history[1:]:
            value = value + other[g]
        high, low = in_two(value)
        for part, depth in enumerate((fine_depth[g, : 2 * fz], coarse_depth[g, : 2 * PACK])):
            pair = in_two(spread(depth, high, views) + spread(depth, low, views))
            spreads[part].append(jnp.concatenate(pair, axis=0))
    backs = ([], [])
    for part in range(2):
        for c in range(size // chunk):
            cut = slice(c * chunk, (c + 1) * chunk)
            back = None
            for g in range(groups):
                value = dot(spreads[part][g], group_rays(held, part, g, cut), ((1,), (1,)))
                back = value if back is None else back + value
            backs[part].append(back[: 2 * rows[part]] + back[2 * rows[part] :])
    for out, first in ((ours, lead), (theirs, jnp.logical_not(lead))):
        parts = []
        for part in range(2):
            back = jnp.concatenate(backs[part], axis=1)
            parts.append(jnp.where(first, back[: rows[part]], back[rows[part] :]))
        out[:, :size] = parts[1].astype(BF16)
        out[:, size:] = pack_fine(parts[0]).astype(BF16)


def final_kernel(groups, size, *refs):
    pieces = refs[: 2 * groups]
    fine, coarse, fw, cw, blocks, fine_out, coarse_out = refs[2 * groups :]
    core = lax.axis_index("slab") % 2
    view = lax.axis_index("view")
    fz, cells = fine.shape
    for index, piece in enumerate(pieces):
        side = core if index < groups else 1 - core
        start = side * (cells // 2) + (view ^ (index % groups)) * size
        start = pl.multiple_of(start, LANES)
        where = pl.ds(start, size)
        keep = keep_row(blocks, start, size)
        change = piece[:, :size].astype(F32)
        coarse_out[:, where] = (coarse[:, where] + cw[:, where] * change) * keep
        change = unpack_fine(piece[:, size:].astype(F32), fz, size)
        fine_out[:, where] = fine[:, where] + fw[:, where] * change


def make_body(slabs, groups):
    far_bits = [1 << k for k in range(slabs.bit_length() - 2, 1, -1)]
    view_bits = [1 << k for k in range(groups.bit_length() - 1)]

    def along_slab(value, bit):
        return swap(value, "slab", slabs, bit)

    def body(
        fine_volume,
        coarse_volume,
        fine_rays,
        coarse_rays,
        fine_axial,
        coarse_axial,
        measured,
        ray_weight,
        fine_cell_weight,
        coarse_cell_weight,
        margin_blocks,
        ray_hits,
    ):
        views, cells, columns = fine_rays.shape
        det = fine_axial.shape[2]
        fz, cz = fine_volume.shape[0], coarse_volume.shape[0]
        own = measured.shape[0]
        total = views * columns
        span = max(views * det, total)
        share = cells // 2 // groups
        lead = lax.axis_index("slab") % 2 == 0
        width = share + packed_tiles(share, fz) * LANES

        taken = in_hbm(
            fine_rays,
            coarse_rays,
            fine_volume,
            coarse_volume,
            fine_cell_weight,
            coarse_cell_weight,
            fine_axial,
            coarse_axial,
            measured,
            ray_weight,
        )
        height = PACK * ((views * det + span) // total)
        mine, theirs, rows, q, short, own_rays = call(
            start_kernel,
            "start",
            (
                shaped((PACK, width), BF16),
                shaped((PACK, width), BF16),
                shaped((height, total), BF16),
                shaped((det // 2, total), F32),
                shaped((det // 2, total), BF16),
                shaped((2, views, share, columns), BF16),
            ),
            [HBM] * len(taken) + [SMEM] * 2,
            scratch_like(*taken)
            + [
                pltpu.VMEM((det, total), F32),
                pltpu.SemaphoreType.DMA((8,)),
                pltpu.SemaphoreType.DMA((4, 4)),
            ],
        )(*taken, *in_hbm(margin_blocks, ray_hits))

        def to_views(value):
            values = [value]
            for bit in view_bits:
                values += [swap(one, "view", groups, bit) for one in values]
            return values

        rows_half = det // 2
        got = {}

        def begin(stage, token):
            waits = [] if token is None else [token]
            if SOURCE["rays"] == stage:
                got["rays"] = []
                for bits in range(1, groups):
                    value = call(
                        functools.partial(take_kernel, groups, bits),
                        "take_rays",
                        shaped((2, views, share, columns), BF16),
                        [HBM] * 2 + [ANY] * len(waits),
                        [pltpu.SemaphoreType.DMA((2,))],
                    )(*in_hbm(fine_rays, coarse_rays), *waits)
                    got["rays"].append(swap(value, "view", groups, bits))
            if SOURCE["weights"] == stage:
                packed = call(
                    pair_kernel,
                    "pair",
                    shaped((2, PACK, width), BF16),
                    [VMEM] * 2 + [ANY] * len(waits),
                )(mine, along_slab(theirs, 1), *waits)
                for index, bit in enumerate(far_bits + [2]):
                    hop = along_slab(packed, bit)
                    got["w%d" % index] = [hop]
                    if bit != 2:
                        packed = jnp.concatenate([packed, hop])
                got["weights"] = (packed, hop)

        def waits_of(stage):
            found = []
            for name, where in AWAITED.items():
                if where == stage:
                    found += got.get(name, [])
            return found

        begin("start", None)
        waits = waits_of("core")
        q, mixed = call(
            join_core_kernel,
            "join_core",
            (shaped((rows_half, total), F32), shaped((rows_half + height, total), BF16)),
            [VMEM] * 3 + [ANY] * len(waits),
        )(q, along_slab(short, 1), rows, *waits)
        begin("core", mixed)
        for index, bit in enumerate([2] + far_bits):
            last = index == len(far_bits)
            name = "last" if last else "hop%d" % index
            waits = waits_of(name)
            size = 2 * mixed.shape[0] - rows_half + (rows_half if last else 0)
            q, mixed = call(
                functools.partial(join_hop_kernel, last),
                "join_hop",
                (shaped(q.shape, F32), shaped((size, total), BF16)),
                [VMEM] * 3 + [ANY] * len(waits),
            )(q, mixed, along_slab(mixed, bit), *waits)
            begin(name, mixed)
        waits = waits_of("views")
        q, rows = call(
            functools.partial(join_views_kernel, rows_half),
            "join_views",
            (
                shaped((groups, rows_half, total), F32),
                shaped((groups, mixed.shape[0] - 2 * rows_half, total), BF16),
            ),
            [VMEM] * groups + [ANY] * len(waits),
        )(*to_views(mixed), *waits)
        count = len(far_bits)
        order = tuple(
            (j & 1) + 2 * (j >> 2) + (((j >> 1) & 1) << (count + 1)) for j in range(slabs)
        )
        coarse_depth, fine_depth, coarse_turned, fine_turned, weights, q = call(
            functools.partial(rows_kernel, own, fz, [2] + far_bits),
            "unpack_rows",
            (
                shaped((groups, slabs * PACK, span), BF16),
                shaped((groups, slabs * fz, span), BF16),
                shaped((groups, views, det, slabs * PACK), BF16),
                shaped((groups, views, det, slabs * fz), BF16),
                shaped((groups, det, total), F32),
                shaped((groups, det, total), F32),
            ),
            [VMEM] * 4,
        )(rows, along_slab(rows, 1), q, along_slab(q, 1))
        coarse_weights, fine_weights = call(
            functools.partial(weights_kernel, fz, order),
            "unpack_weights",
            (shaped((slabs * PACK, share), BF16), shaped((slabs * fz, share), BF16)),
            [VMEM] * 2,
        )(*got["weights"])
        spreads = call(
            functools.partial(spread_kernel, views),
            "spread",
            (
                shaped((groups, slabs * fz, total), BF16),
                shaped((groups, slabs * PACK, total), BF16),
            ),
            [VMEM] * 4,
        )(q, weights, fine_depth, coarse_depth)
        rays = [own_rays] + got["rays"]
        held = (fine_turned, coarse_turned, coarse_weights, fine_weights, *rays)
        def add(mine, received, bit):
            return call(
                functools.partial(add_kernel, bit),
                "add",
                shaped((groups, det, total), BF16),
                [VMEM] * 2,
            )(mine, received)

        deltas = []
        for ready, inputs in ((True, spreads), (False, None)):
            if not ready:
                inputs = (q, *deltas, weights, fine_depth, coarse_depth)
            delta = call(
                functools.partial(step_kernel, groups, views, ready),
                "ray_space_step",
                shaped((groups, det, total), BF16),
                [VMEM] * (len(inputs) + len(held)),
            )(*inputs, *held)
            delta = add(delta, along_slab(delta, 1), 0)
            for bit in view_bits:
                delta = add(delta, swap(delta, "view", groups, bit), bit)
            deltas.append(delta)
        inputs = (q, *deltas, weights, fine_depth, coarse_depth, *rays)
        ours, theirs = call(
            functools.partial(tail_kernel, fz, groups, views),
            "back_projection",
            (shaped((PACK, width), BF16),) * 2,
            [VMEM] * len(inputs),
        )(*inputs)
        both = ("slab", "view")
        pieces = [ours] + [swap(ours, "view", groups, bits) for bits in range(1, groups)]
        pieces += [swap(theirs, both, slabs * groups, groups | bits) for bits in range(groups)]
        return call(
            functools.partial(final_kernel, groups, share),
            "update",
            (shaped(fine_volume.shape, F32), shaped(coarse_volume.shape, F32)),
            [VMEM] * (2 * groups + 4) + [SMEM],
        )(
            *pieces,
            fine_volume,
            coarse_volume,
            fine_cell_weight,
            coarse_cell_weight,
            margin_blocks,
        )

    return body


def solution(mesh):
    return jax.shard_map(
        make_body(mesh.shape["slab"], mesh.shape["view"]),
        mesh=mesh,
        in_specs=(
            P("slab", None),
            P("slab", None),
            P("view", None, None),
            P("view", None, None),
            P("view", "slab", None),
            P("view", "slab", None),
            P("slab", "view", None),
            P("slab", "view", None),
            P("slab", None),
            P("slab", None),
            P("slab", None),
            P("view", "slab", None),
        ),
        out_specs=(P("slab", None), P("slab", None)),
        check_vma=False,
    )
```

```python
import functools
import jax
import jax.numpy as jnp
from jax import lax
from jax.experimental import pallas as pl
from jax.experimental.pallas import tpu as pltpu
from jax.sharding import PartitionSpec as P

BLOCK = 128
LANES = 128
PACK = 16
F32 = jnp.float32
BF16 = jnp.bfloat16
PARAMS = pltpu.CompilerParams(vmem_limit_bytes=24 * 1024 * 1024)
VMEM = pl.BlockSpec(memory_space=pltpu.VMEM)
SMEM = pl.BlockSpec(memory_space=pltpu.SMEM)
ANY = pl.BlockSpec(memory_space=pl.ANY)
HBM = pl.BlockSpec(memory_space=pltpu.HBM)
SOURCE = {"rays": "start", "weights": "start"}
AWAITED = {"rays": "views"}
QUICK = pl.CostEstimate(flops=1, bytes_accessed=1, transcendentals=0)


def fetch(source, target, sem):
    copy = pltpu.make_async_copy(source, target, sem)
    copy.start()
    return copy


def in_hbm(*arrays):
    return [pltpu.with_memory_space_constraint(a, pltpu.HBM) for a in arrays]


def scratch_like(*arrays):
    return [pltpu.VMEM(a.shape, a.dtype) for a in arrays]


def shaped(shape, dtype):
    return jax.ShapeDtypeStruct(shape, dtype)


def call(kernel, name, out_shape, in_specs, scratch=()):
    many = isinstance(out_shape, tuple)
    return pl.pallas_call(
        kernel,
        out_shape=out_shape,
        in_specs=in_specs,
        out_specs=(VMEM,) * len(out_shape) if many else VMEM,
        scratch_shapes=list(scratch),
        compiler_params=PARAMS,
        cost_estimate=QUICK,
        name=name,
    )


def swap(value, axis, size, bits):
    return lax.ppermute(value, axis, [(i, i ^ bits) for i in range(size)])


def dot(a, b, dims):
    return lax.dot_general(a, b, (dims, ((), ())), preferred_element_type=F32)


def in_two(value):
    high = value.astype(BF16)
    return high, (value - high.astype(F32)).astype(BF16)


def keep_row(blocks_ref, start, width):
    ids = (lax.broadcasted_iota(jnp.int32, (1, width), 1) + start) // BLOCK
    keep = jnp.ones((1, width), F32)
    for k in range(blocks_ref.shape[1]):
        keep = jnp.where(ids == blocks_ref[0, k], 0.0, keep)
    return keep


def share_start(cells, groups, bits=0):
    core = lax.axis_index("slab") % 2
    share = cells // 2 // groups
    return pl.multiple_of(core * (cells // 2) + (lax.axis_index("view") ^ bits) * share, LANES)


def packed_tiles(cells, fz):
    parts = PACK // fz
    return -(-(cells // LANES) // parts)


def pack_fine(rows):
    fz, size = rows.shape
    parts = PACK // fz
    empty = jnp.zeros((1, LANES), rows.dtype)
    columns = []
    for c in range(packed_tiles(size, fz)):
        pieces = []
        for i in range(fz):
            for k in range(parts):
                t = c * parts + k
                inside = t * LANES < size
                pieces.append(rows[i : i + 1, t * LANES : (t + 1) * LANES] if inside else empty)
        columns.append(jnp.concatenate(pieces, axis=0))
    return jnp.concatenate(columns, axis=1)


def unpack_fine(packed, fz, size):
    parts = PACK // fz
    rows = []
    for i in range(fz):
        pieces = []
        for t in range(size // LANES):
            row, column = i * parts + t % parts, t // parts * LANES
            pieces.append(packed[row : row + 1, column : column + LANES])
        rows.append(jnp.concatenate(pieces, axis=1))
    return jnp.concatenate(rows, axis=0)


def hit_depths(axial, hits):
    views, _, det = axial.shape
    tiles = hits.shape[2]
    tile = lax.broadcasted_iota(jnp.int32, (1, det), 1) // (det // tiles)
    result = []
    for v in range(views):
        hit = jnp.zeros((1, det), F32)
        for t in range(tiles):
            hit = jnp.where(tile == t, hits[v, 0, t].astype(F32), hit)
        result.append(axial[v].astype(F32) * hit)
    return result


def take_kernel(groups, bits, fine_rays, coarse_rays, *refs):
    out, sems = refs[-2:]
    cells = pl.ds(share_start(fine_rays.shape[1], groups, bits), out.shape[2])
    copies = [
        fetch(rays.at[:, cells, :], out.at[part], sems.at[part])
        for part, rays in enumerate((fine_rays, coarse_rays))
    ]
    for copy in copies:
        copy.wait()


def pair_kernel(mine, received, *refs):
    out = refs[-1]
    lead = lax.axis_index("slab") % 2 == 0
    own, other = mine[...].astype(F32), received[...].astype(F32)
    out[0] = jnp.where(lead, own, other).astype(BF16)
    out[1] = jnp.where(lead, other, own).astype(BF16)


def join_core_kernel(q, received, rows, *refs):
    total, out = refs[-2:]
    count = q.shape[0]
    value = q[...] + received[...].astype(F32)
    total[...] = value
    out[:count] = value.astype(BF16)
    out[count:] = rows[...]


def join_hop_kernel(last, q, mine, received, *refs):
    total, out = refs[-2:]
    count = q.shape[0]
    value = q[...] + received[:count].astype(F32)
    total[...] = value
    high, low = in_two(value)
    out[:count] = high
    base = count
    if last:
        out[count : 2 * count] = low
        base = 2 * count
    held = mine.shape[0] - count
    out[base : base + held] = mine[count:]
    out[base + held :] = received[count:]


def join_views_kernel(count, *refs):
    q, rows = refs[-2:]
    for g in range(q.shape[0]):
        part = refs[g]
        q[g] = part[:count].astype(F32) + part[count : 2 * count].astype(F32)
        rows[g] = part[2 * count :]


def start_kernel(
    fine_rays_in,
    coarse_rays_in,
    fine_in,
    coarse_in,
    fine_weight_in,
    coarse_weight_in,
    fine_axial_in,
    coarse_axial_in,
    measured_in,
    ray_weight_in,
    blocks_in,
    hits_in,
    mine,
    theirs,
    rows,
    out,
    short,
    own_rays,
    fine_rays,
    coarse_rays,
    fine,
    coarse,
    fine_weight,
    coarse_weight,
    fine_axial,
    coarse_axial,
    measured,
    ray_weight,
    blocks,
    hits,
    scratch,
    sems,
    chunk_sems,
):
    me = lax.axis_index("slab")
    core = me % 2
    fz, cells = fine.shape
    half = cells // 2
    sources = (
        (fine_axial_in, fine_axial),
        (coarse_axial_in, coarse_axial),
        (ray_weight_in, ray_weight),
        (measured_in, measured),
        (blocks_in, blocks),
        (hits_in, hits),
        (fine_weight_in, fine_weight),
        (coarse_weight_in, coarse_weight),
    )
    others = [fetch(a, b, sems.at[i]) for i, (a, b) in enumerate(sources)]
    steps = chunk_sems.shape[0]
    chunk = cells // steps
    copies = []
    for i in range(steps):
        part = pl.ds(i * chunk, chunk)
        copies.append(
            [
                fetch(fine_in.at[:, part], fine.at[:, part], chunk_sems.at[i, 0]),
                fetch(coarse_in.at[:, part], coarse.at[:, part], chunk_sems.at[i, 1]),
                fetch(fine_rays_in.at[:, part, :], fine_rays.at[:, part, :], chunk_sems.at[i, 2]),
                fetch(
                    coarse_rays_in.at[:, part, :], coarse_rays.at[:, part, :], chunk_sems.at[i, 3]
                ),
            ]
        )
    share = own_rays.shape[2]
    groups = half // share
    held = pl.ds(share_start(cells, groups), share)
    outgoing = [
        fetch(fine_rays_in.at[:, held, :], own_rays.at[0], sems.at[8]),
        fetch(coarse_rays_in.at[:, held, :], own_rays.at[1], sems.at[9]),
    ]
    for copy in others:
        copy.wait()

    views, _, det = fine_axial.shape
    columns = ray_weight.shape[2]
    total = views * columns
    span = views * det
    own = ray_weight.shape[0]
    coarse_depth = hit_depths(coarse_axial, hits)
    fine_depth = hit_depths(fine_axial, hits)
    wide = max(span, total)
    weight = jnp.concatenate([ray_weight[:, v, :] for v in range(views)], axis=1)
    fine_wide = jnp.concatenate(fine_depth, axis=1)
    if wide > total:
        weight = jnp.concatenate([weight, jnp.zeros((own, wide - total), F32)], axis=1)
    if wide > span:
        fine_wide = jnp.concatenate([fine_wide, jnp.zeros((fz, wide - span), F32)], axis=1)
    stack = [weight, fine_wide]
    if own + fz < PACK:
        stack.append(jnp.zeros((PACK - own - fz, wide), F32))
    packed = jnp.concatenate(coarse_depth + [jnp.concatenate(stack, axis=0)], axis=1).astype(BF16)
    for p in range((span + wide) // total):
        rows[p * PACK : (p + 1) * PACK] = packed[:, p * total : (p + 1) * total]

    for target, side in ((mine, core), (theirs, 1 - core)):
        begin = pl.multiple_of(side * half + lax.axis_index("view") * share, LANES)
        keep = keep_row(blocks, begin, share)
        target[:, :share] = (coarse_weight[:, pl.ds(begin, share)] * keep).astype(BF16)
        target[:, share:] = pack_fine(fine_weight[:, pl.ds(begin, share)]).astype(BF16)

    fine_sum = coarse_sum = None
    for i in range(steps):
        part = slice(i * chunk, (i + 1) * chunk)
        for copy in copies[i]:
            copy.wait()
        keep = keep_row(blocks, i * chunk, chunk)
        fine_rows = fine[:, part].astype(BF16)
        coarse_rows = (coarse[:, part] * keep).astype(BF16)
        fine_wide = jnp.concatenate([fine_rays[v, part, :] for v in range(views)], axis=1)
        coarse_wide = jnp.concatenate([coarse_rays[v, part, :] for v in range(views)], axis=1)
        fine_part = dot(fine_rows, fine_wide, ((1,), (0,)))
        coarse_part = dot(coarse_rows, coarse_wide, ((1,), (0,)))
        fine_sum = fine_part if fine_sum is None else fine_sum + fine_part
        coarse_sum = coarse_part if coarse_sum is None else coarse_sum + coarse_part
    pad = jnp.zeros((PACK - fz, total), F32)
    moment = jnp.concatenate([coarse_sum, fine_sum, pad], axis=0).astype(BF16)
    pad = jnp.zeros((PACK - fz, det), F32)
    row = lax.broadcasted_iota(jnp.int32, (det, columns), 0) - me * own
    for v in range(views):
        depth = jnp.concatenate([coarse_depth[v], fine_depth[v], pad], axis=0).astype(BF16)
        where = slice(v * columns, (v + 1) * columns)
        projection = dot(depth, moment[:, where], ((0,), (0,)))
        given = jnp.zeros((det, columns), F32)
        for i in range(own):
            given = jnp.where(row == i, measured[i : i + 1, v, :], given)
        scratch[:, where] = given - projection
    kept = pl.ds(pl.multiple_of(core * (det // 2), PACK), det // 2)
    sent = pl.ds(pl.multiple_of((1 - core) * (det // 2), PACK), det // 2)
    out[...] = scratch[kept, :]
    short[...] = scratch[sent, :].astype(BF16)
    for copy in outgoing:
        copy.wait()


def slab_of(block, bits):
    me = lax.axis_index("slab")
    apart = jnp.zeros_like(block)
    for place, bit in enumerate(bits):
        apart = apart + ((block >> (place + 1)) & 1) * bit
    return ((me - me % 2) ^ apart) + (block & 1)


def rows_kernel(own, fz, bits, mine, theirs, q_mine, q_theirs, *refs):
    coarse_out, fine_out, coarse_turned, fine_turned, out, q_out = refs
    lead = lax.axis_index("slab") % 2 == 0
    kept = q_mine.shape[1]
    for g in range(q_mine.shape[0]):
        ours, others = q_mine[g], q_theirs[g]
        q_out[g, :kept] = jnp.where(lead, ours, others)
        q_out[g, kept:] = jnp.where(lead, others, ours)
    groups, held, total = mine.shape
    slabs = coarse_out.shape[1] // PACK
    height = 2 * held // slabs
    pieces = height // PACK
    det = out.shape[1]
    count = slabs * PACK
    shape = (slabs * own, count)
    w = lax.broadcasted_iota(jnp.int32, shape, 0)
    column = lax.broadcasted_iota(jnp.int32, shape, 1)
    block, row = column // PACK, column % PACK
    match = (row < own) & (w == slab_of(block, bits) * own + row)
    to_weight = jnp.where(match, 1.0, 0.0).astype(BF16)
    shape = (slabs * fz, count)
    z = lax.broadcasted_iota(jnp.int32, shape, 0)
    column = lax.broadcasted_iota(jnp.int32, shape, 1)
    to_fine = jnp.where(column == (z // fz) * PACK + own + z % fz, 1.0, 0.0).astype(BF16)
    for g in range(groups):
        own_rows, other_rows = mine[g].astype(F32), theirs[g].astype(F32)
        even = jnp.where(lead, own_rows, other_rows).astype(BF16)
        odd = jnp.where(lead, other_rows, own_rows).astype(BF16)
        cuts = []
        for p in range(pieces):
            blocks = [
                (even, odd)[j % 2][(j // 2) * height + p * PACK :][:PACK] for j in range(slabs)
            ]
            cuts.append(jnp.concatenate(blocks, axis=0))
        coarse = jnp.concatenate(cuts[: pieces // 2], axis=1)
        side = jnp.concatenate(cuts[pieces // 2 :], axis=1)
        fine = dot(to_fine, side, ((1,), (0,)))
        coarse_out[g] = coarse
        fine_out[g] = fine.astype(BF16)
        wide = coarse.astype(F32)
        for v in range(coarse.shape[1] // det):
            where = slice(v * det, (v + 1) * det)
            coarse_turned[g, v] = wide[:, where].T.astype(BF16)
            fine_turned[g, v] = fine[:, where].T.astype(BF16)
        out[g] = dot(to_weight, side, ((1,), (0,)))[:, :total]


def weights_kernel(fz, order, mine, received, *refs):
    coarse_out, fine_out = refs[-2:]
    held = mine.shape[0]
    slabs = 2 * held
    count = slabs * PACK
    parts = PACK // fz
    size = fine_out.shape[1]
    tiles = packed_tiles(size, fz)
    blocks = [(mine, received)[k // held].at[k % held] for k in order]
    for j, block in enumerate(blocks):
        coarse_out[j * PACK : (j + 1) * PACK] = block[:, :size]
    source = jnp.concatenate([block[:, size : size + tiles * LANES] for block in blocks], axis=0)
    shape = (slabs * fz, count)
    z = lax.broadcasted_iota(jnp.int32, shape, 0)
    column = lax.broadcasted_iota(jnp.int32, shape, 1)
    for k in range(parts):
        choose = jnp.where(column == (z // fz) * PACK + (z % fz) * parts + k, 1.0, 0.0)
        chosen = dot(choose.astype(BF16), source, ((1,), (0,)))
        for c in range(tiles):
            t = c * parts + k
            if t * LANES < size:
                fine_out[:, t * LANES : (t + 1) * LANES] = chosen[
                    :, c * LANES : (c + 1) * LANES
                ].astype(BF16)


def whole_rows(mine, received):
    lead = lax.axis_index("slab") % 2 == 0
    ours, others = mine.astype(F32), received.astype(F32)
    return jnp.concatenate(
        [jnp.where(lead, ours, others), jnp.where(lead, others, ours)], axis=0
    )


def residuals(q, deltas, weights):
    groups = q.shape[0]
    current = [q[g] for g in range(groups)]
    results = [[weights[g] * current[g] for g in range(groups)]]
    for mine, received in deltas:
        current = [current[g] - whole_rows(mine[g], received[g]) for g in range(groups)]
        results.append([weights[g] * current[g] for g in range(groups)])
    return results


def spread(depth, residual, views):
    det, columns = residual.shape[0], residual.shape[1] // views
    pieces = [
        dot(
            depth[:, v * det : (v + 1) * det],
            residual[:, v * columns : (v + 1) * columns],
            ((1,), (0,)),
        )
        for v in range(views)
    ]
    return jnp.concatenate(pieces, axis=1)


def spread_kernel(views, q, weights, fine_depth, coarse_depth, fine_out, coarse_out):
    for g in range(q.shape[0]):
        residual = (weights[g] * q[g]).astype(BF16)
        fine_out[g] = spread(fine_depth[g], residual, views).astype(BF16)
        coarse_out[g] = spread(coarse_depth[g], residual, views).astype(BF16)


def group_rays(held, part, g, cut):
    return jnp.concatenate([held[g][part, v, cut, :] for v in range(held[g].shape[1])], axis=1)


def step_kernel(groups, views, ready, *refs):
    refs = list(refs)
    if ready:
        spreads = [refs.pop(0), refs.pop(0)]
    else:
        q, mine, received, weights, fine_depth, coarse_depth = refs[:6]
        refs = refs[6:]
        residual = residuals(q, [(mine, received)], weights)[-1]
        residual = [r.astype(BF16) for r in residual]
        spreads = [
            [spread(depth[g], residual[g], views).astype(BF16) for g in range(groups)]
            for depth in (fine_depth, coarse_depth)
        ]
    turned = refs[:2]
    coarse_weights, fine_weights = refs[2:4]
    held = refs[4:-3]
    kept, given, scratch = refs[-3:]
    size = fine_weights.shape[1]
    columns = held[0].shape[3]
    chunk = min(size, 1024)
    results = [None] * groups
    for part in range(2):
        moments = [None] * groups
        for c in range(size // chunk):
            cut = slice(c * chunk, (c + 1) * chunk)
            if part == 0:
                weight = fine_weights[:, cut]
            else:
                weight = coarse_weights[:, cut]
            rays = [group_rays(held, part, g, cut) for g in range(groups)]
            back = dot(spreads[part][0], rays[0], ((1,), (1,)))
            for g in range(1, groups):
                back = back + dot(spreads[part][g], rays[g], ((1,), (1,)))
            change = (weight.astype(F32) * back).astype(BF16)
            for g in range(groups):
                moment = dot(change, rays[g], ((1,), (0,)))
                moments[g] = moment if moments[g] is None else moments[g] + moment
        for g in range(groups):
            moment = moments[g].astype(BF16)
            pieces = [
                dot(turned[part][g, v], moment[:, v * columns : (v + 1) * columns], ((1,), (0,)))
                for v in range(views)
            ]
            value = jnp.concatenate(pieces, axis=1)
            results[g] = value if results[g] is None else results[g] + value
    core = lax.axis_index("slab") % 2
    rows = kept.shape[1]
    for g in range(groups):
        scratch[g] = results[g]
        kept[g] = scratch[g, pl.ds(pl.multiple_of(core * rows, PACK), rows), :].astype(BF16)
        given[g] = scratch[g, pl.ds(pl.multiple_of((1 - core) * rows, PACK), rows), :].astype(BF16)


def add_kernel(bit, mine, received, out):
    for g in range(mine.shape[0]):
        out[g] = (mine[g].astype(F32) + received[g ^ bit].astype(F32)).astype(BF16)


def tail_kernel(fz, groups, views, q, *refs):
    deltas = [refs[:2], refs[2:4]]
    weights, fine_depth, coarse_depth = refs[4:7]
    held = refs[7:-2]
    ours, theirs = refs[-2:]
    size = held[0].shape[2]
    chunk = min(size, 1024)
    lead = lax.axis_index("slab") % 2 == 0
    history = residuals(q, deltas, weights)
    rows = (fz, PACK)
    spreads = ([], [])
    for g in range(groups):
        value = history[0][g]
        for other in history[1:]:
            value = value + other[g]
        high, low = in_two(value)
        for part, depth in enumerate((fine_depth[g, : 2 * fz], coarse_depth[g, : 2 * PACK])):
            pair = in_two(spread(depth, high, views) + spread(depth, low, views))
            spreads[part].append(jnp.concatenate(pair, axis=0))
    backs = ([], [])
    for part in range(2):
        for c in range(size // chunk):
            cut = slice(c * chunk, (c + 1) * chunk)
            back = None
            for g in range(groups):
                value = dot(spreads[part][g], group_rays(held, part, g, cut), ((1,), (1,)))
                back = value if back is None else back + value
            backs[part].append(back[: 2 * rows[part]] + back[2 * rows[part] :])
    for out, first in ((ours, lead), (theirs, jnp.logical_not(lead))):
        parts = []
        for part in range(2):
            back = jnp.concatenate(backs[part], axis=1)
            parts.append(jnp.where(first, back[: rows[part]], back[rows[part] :]))
        out[:, :size] = parts[1].astype(BF16)
        out[:, size:] = pack_fine(parts[0]).astype(BF16)


def keep_kernel(blocks, out):
    out[...] = keep_row(blocks, 0, out.shape[1])


def final_kernel(groups, size, *refs):
    pieces = refs[: 2 * groups]
    fine, coarse, fw, cw, keep, fine_out, coarse_out = refs[2 * groups :]
    core = lax.axis_index("slab") % 2
    view = lax.axis_index("view")
    fz, cells = fine.shape
    for index, piece in enumerate(pieces):
        side = core if index < groups else 1 - core
        start = side * (cells // 2) + (view ^ (index % groups)) * size
        start = pl.multiple_of(start, LANES)
        where = pl.ds(start, size)
        change = piece[:, :size].astype(F32)
        coarse_out[:, where] = (coarse[:, where] + cw[:, where] * change) * keep[:, where]
        change = unpack_fine(piece[:, size:].astype(F32), fz, size)
        fine_out[:, where] = fine[:, where] + fw[:, where] * change


def make_body(slabs, groups):
    far_bits = [1 << k for k in range(slabs.bit_length() - 2, 1, -1)]
    view_bits = [1 << k for k in range(groups.bit_length() - 1)]

    def along_slab(value, bit):
        return swap(value, "slab", slabs, bit)

    def body(
        fine_volume,
        coarse_volume,
        fine_rays,
        coarse_rays,
        fine_axial,
        coarse_axial,
        measured,
        ray_weight,
        fine_cell_weight,
        coarse_cell_weight,
        margin_blocks,
        ray_hits,
    ):
        views, cells, columns = fine_rays.shape
        det = fine_axial.shape[2]
        fz, cz = fine_volume.shape[0], coarse_volume.shape[0]
        own = measured.shape[0]
        total = views * columns
        span = max(views * det, total)
        share = cells // 2 // groups
        lead = lax.axis_index("slab") % 2 == 0
        width = share + packed_tiles(share, fz) * LANES

        taken = in_hbm(
            fine_rays,
            coarse_rays,
            fine_volume,
            coarse_volume,
            fine_cell_weight,
            coarse_cell_weight,
            fine_axial,
            coarse_axial,
            measured,
            ray_weight,
        )
        height = PACK * ((views * det + span) // total)
        mine, theirs, rows, q, short, own_rays = call(
            start_kernel,
            "start",
            (
                shaped((PACK, width), BF16),
                shaped((PACK, width), BF16),
                shaped((height, total), BF16),
                shaped((det // 2, total), F32),
                shaped((det // 2, total), BF16),
                shaped((2, views, share, columns), BF16),
            ),
            [HBM] * (len(taken) + 2),
            scratch_like(*taken)
            + [
                pltpu.SMEM(margin_blocks.shape, jnp.int32),
                pltpu.SMEM(ray_hits.shape, jnp.int32),
                pltpu.VMEM((det, total), F32),
                pltpu.SemaphoreType.DMA((10,)),
                pltpu.SemaphoreType.DMA((4, 4)),
            ],
        )(*taken, *in_hbm(margin_blocks, ray_hits))

        def to_views(value):
            values = [value]
            for bit in view_bits:
                values += [swap(one, "view", groups, bit) for one in values]
            return values

        rows_half = det // 2
        got = {}

        def begin(stage, token):
            waits = [] if token is None else [token]
            if SOURCE["rays"] == stage:
                got["rays"] = []
                for bits in range(1, groups):
                    value = call(
                        functools.partial(take_kernel, groups, bits),
                        "take_rays",
                        shaped((2, views, share, columns), BF16),
                        [HBM] * 2 + [ANY] * len(waits),
                        [pltpu.SemaphoreType.DMA((2,))],
                    )(*in_hbm(fine_rays, coarse_rays), *waits)
                    got["rays"].append(swap(value, "view", groups, bits))
            if SOURCE["weights"] == stage:
                packed = call(
                    pair_kernel,
                    "pair",
                    shaped((2, PACK, width), BF16),
                    [VMEM] * 2 + [ANY] * len(waits),
                )(mine, along_slab(theirs, 1), *waits)
                for index, bit in enumerate(far_bits + [2]):
                    hop = along_slab(packed, bit)
                    got["w%d" % index] = [hop]
                    if bit != 2:
                        packed = jnp.concatenate([packed, hop])
                got["weights"] = (packed, hop)

        def waits_of(stage):
            found = []
            for name, where in AWAITED.items():
                if where == stage:
                    found += got.get(name, [])
            return found

        begin("start", None)
        waits = waits_of("core")
        q, mixed = call(
            join_core_kernel,
            "join_core",
            (shaped((rows_half, total), F32), shaped((rows_half + height, total), BF16)),
            [VMEM] * 3 + [ANY] * len(waits),
        )(q, along_slab(short, 1), rows, *waits)
        begin("core", mixed)
        for index, bit in enumerate([2] + far_bits):
            last = index == len(far_bits)
            name = "last" if last else "hop%d" % index
            waits = waits_of(name)
            size = 2 * mixed.shape[0] - rows_half + (rows_half if last else 0)
            q, mixed = call(
                functools.partial(join_hop_kernel, last),
                "join_hop",
                (shaped(q.shape, F32), shaped((size, total), BF16)),
                [VMEM] * 3 + [ANY] * len(waits),
            )(q, mixed, along_slab(mixed, bit), *waits)
            begin(name, mixed)
        waits = waits_of("views")
        q, rows = call(
            functools.partial(join_views_kernel, rows_half),
            "join_views",
            (
                shaped((groups, rows_half, total), F32),
                shaped((groups, mixed.shape[0] - 2 * rows_half, total), BF16),
            ),
            [VMEM] * groups + [ANY] * len(waits),
        )(*to_views(mixed), *waits)
        count = len(far_bits)
        order = tuple(
            (j & 1) + 2 * (j >> 2) + (((j >> 1) & 1) << (count + 1)) for j in range(slabs)
        )
        coarse_depth, fine_depth, coarse_turned, fine_turned, weights, q = call(
            functools.partial(rows_kernel, own, fz, [2] + far_bits),
            "unpack_rows",
            (
                shaped((groups, slabs * PACK, span), BF16),
                shaped((groups, slabs * fz, span), BF16),
                shaped((groups, views, det, slabs * PACK), BF16),
                shaped((groups, views, det, slabs * fz), BF16),
                shaped((groups, det, total), F32),
                shaped((groups, det, total), F32),
            ),
            [VMEM] * 4,
        )(rows, along_slab(rows, 1), q, along_slab(q, 1))
        spreads = call(
            functools.partial(spread_kernel, views),
            "spread",
            (
                shaped((groups, slabs * fz, total), BF16),
                shaped((groups, slabs * PACK, total), BF16),
            ),
            [VMEM] * 4,
        )(q, weights, fine_depth, coarse_depth)
        coarse_weights, fine_weights = call(
            functools.partial(weights_kernel, fz, order),
            "unpack_weights",
            (shaped((slabs * PACK, share), BF16), shaped((slabs * fz, share), BF16)),
            [VMEM] * 2 + [ANY] * len(spreads),
        )(*got["weights"], *spreads)
        rays = [own_rays] + got["rays"]
        held = (fine_turned, coarse_turned, coarse_weights, fine_weights, *rays)
        def add(mine, received, bit):
            return call(
                functools.partial(add_kernel, bit),
                "add",
                shaped((groups, rows_half, total), BF16),
                [VMEM] * 2,
            )(mine, received)

        deltas = []
        for ready, inputs in ((True, spreads), (False, None)):
            if not ready:
                inputs = (q, *deltas, weights, fine_depth, coarse_depth)
            delta, given = call(
                functools.partial(step_kernel, groups, views, ready),
                "ray_space_step",
                (shaped((groups, rows_half, total), BF16),) * 2,
                [VMEM] * (len(inputs) + len(held)),
                [pltpu.VMEM((groups, det, total), F32)],
            )(*inputs, *held)
            delta = add(delta, along_slab(given, 1), 0)
            for bit in view_bits:
                delta = add(delta, swap(delta, "view", groups, bit), bit)
            deltas += [delta, along_slab(delta, 1)]
        inputs = (q, *deltas, weights, fine_depth, coarse_depth, *rays)
        ours, theirs = call(
            functools.partial(tail_kernel, fz, groups, views),
            "back_projection",
            (shaped((PACK, width), BF16),) * 2,
            [VMEM] * len(inputs),
        )(*inputs)
        keep = call(keep_kernel, "keep", shaped((1, cells), F32), [SMEM])(margin_blocks)
        both = ("slab", "view")
        pieces = [ours] + [swap(ours, "view", groups, bits) for bits in range(1, groups)]
        pieces += [swap(theirs, both, slabs * groups, groups | bits) for bits in range(groups)]
        return call(
            functools.partial(final_kernel, groups, share),
            "update",
            (shaped(fine_volume.shape, F32), shaped(coarse_volume.shape, F32)),
            [VMEM] * (2 * groups + 5),
        )(
            *pieces,
            fine_volume,
            coarse_volume,
            fine_cell_weight,
            coarse_cell_weight,
            keep,
        )

    return body


def solution(mesh):
    return jax.shard_map(
        make_body(mesh.shape["slab"], mesh.shape["view"]),
        mesh=mesh,
        in_specs=(
            P("slab", None),
            P("slab", None),
            P("view", None, None),
            P("view", None, None),
            P("view", "slab", None),
            P("view", "slab", None),
            P("slab", "view", None),
            P("slab", "view", None),
            P("slab", None),
            P("slab", None),
            P("slab", None),
            P("view", "slab", None),
        ),
        out_specs=(P("slab", None), P("slab", None)),
        check_vma=False,
    )
```

```python
import functools
import jax
import jax.numpy as jnp
from jax import lax
from jax.experimental import pallas as pl
from jax.experimental.pallas import tpu as pltpu
from jax.sharding import PartitionSpec as P

BLOCK = 128
LANES = 128
PACK = 16
F32 = jnp.float32
BF16 = jnp.bfloat16
PARAMS = pltpu.CompilerParams(vmem_limit_bytes=24 * 1024 * 1024)
VMEM = pl.BlockSpec(memory_space=pltpu.VMEM)
SMEM = pl.BlockSpec(memory_space=pltpu.SMEM)
ANY = pl.BlockSpec(memory_space=pl.ANY)
HBM = pl.BlockSpec(memory_space=pltpu.HBM)
SOURCE = {'rays': 'start', 'weights': ("start", "core", "hop1")}
AWAITED = {"rays": "views", "w1": "last"}
QUICK = pl.CostEstimate(flops=1, bytes_accessed=1, transcendentals=0)


def fetch(source, target, sem):
    copy = pltpu.make_async_copy(source, target, sem)
    copy.start()
    return copy


def in_hbm(*arrays):
    return [pltpu.with_memory_space_constraint(a, pltpu.HBM) for a in arrays]


def scratch_like(*arrays):
    return [pltpu.VMEM(a.shape, a.dtype) for a in arrays]


def shaped(shape, dtype):
    return jax.ShapeDtypeStruct(shape, dtype)


def call(kernel, name, out_shape, in_specs, scratch=()):
    many = isinstance(out_shape, tuple)
    return pl.pallas_call(
        kernel,
        out_shape=out_shape,
        in_specs=in_specs,
        out_specs=(VMEM,) * len(out_shape) if many else VMEM,
        scratch_shapes=list(scratch),
        compiler_params=PARAMS,
        cost_estimate=QUICK,
        name=name,
    )


def swap(value, axis, size, bits):
    return lax.ppermute(value, axis, [(i, i ^ bits) for i in range(size)])


def dot(a, b, dims):
    return lax.dot_general(a, b, (dims, ((), ())), preferred_element_type=F32)


def in_two(value):
    high = value.astype(BF16)
    return high, (value - high.astype(F32)).astype(BF16)


def keep_row(blocks_ref, start, width):
    ids = (lax.broadcasted_iota(jnp.int32, (1, width), 1) + start) // BLOCK
    keep = jnp.ones((1, width), F32)
    for k in range(blocks_ref.shape[1]):
        keep = jnp.where(ids == blocks_ref[0, k], 0.0, keep)
    return keep


def share_start(cells, groups, bits=0):
    core = lax.axis_index("slab") % 2
    share = cells // 2 // groups
    return pl.multiple_of(core * (cells // 2) + (lax.axis_index("view") ^ bits) * share, LANES)


def packed_tiles(cells, fz):
    parts = PACK // fz
    return -(-(cells // LANES) // parts)


def pack_fine(rows):
    fz, size = rows.shape
    parts = PACK // fz
    empty = jnp.zeros((1, LANES), rows.dtype)
    columns = []
    for c in range(packed_tiles(size, fz)):
        pieces = []
        for i in range(fz):
            for k in range(parts):
                t = c * parts + k
                inside = t * LANES < size
                pieces.append(rows[i : i + 1, t * LANES : (t + 1) * LANES] if inside else empty)
        columns.append(jnp.concatenate(pieces, axis=0))
    return jnp.concatenate(columns, axis=1)


def unpack_fine(packed, fz, size):
    parts = PACK // fz
    rows = []
    for i in range(fz):
        pieces = []
        for t in range(size // LANES):
            row, column = i * parts + t % parts, t // parts * LANES
            pieces.append(packed[row : row + 1, column : column + LANES])
        rows.append(jnp.concatenate(pieces, axis=1))
    return jnp.concatenate(rows, axis=0)


def hit_depths(axial, hits):
    views, _, det = axial.shape
    tiles = hits.shape[2]
    tile = lax.broadcasted_iota(jnp.int32, (1, det), 1) // (det // tiles)
    result = []
    for v in range(views):
        hit = jnp.zeros((1, det), F32)
        for t in range(tiles):
            hit = jnp.where(tile == t, hits[v, 0, t].astype(F32), hit)
        result.append(axial[v].astype(F32) * hit)
    return result


def take_kernel(groups, bits, fine_rays, coarse_rays, *refs):
    out, sems = refs[-2:]
    cells = pl.ds(share_start(fine_rays.shape[1], groups, bits), out.shape[2])
    copies = [
        fetch(rays.at[:, cells, :], out.at[part], sems.at[part])
        for part, rays in enumerate((fine_rays, coarse_rays))
    ]
    for copy in copies:
        copy.wait()


def pair_kernel(mine, received, *refs):
    out = refs[-1]
    lead = lax.axis_index("slab") % 2 == 0
    own, other = mine[...].astype(F32), received[...].astype(F32)
    out[0] = jnp.where(lead, own, other).astype(BF16)
    out[1] = jnp.where(lead, other, own).astype(BF16)


def join_blocks_kernel(mine, received, *refs):
    out = refs[-1]
    out[: mine.shape[0]] = mine[...]
    out[mine.shape[0] :] = received[...]


def join_core_kernel(q, received, rows, *refs):
    total, out = refs[-2:]
    count = q.shape[0]
    value = q[...] + received[...].astype(F32)
    total[...] = value
    out[:count] = value.astype(BF16)
    out[count:] = rows[...]


def join_hop_kernel(q, mine, received, *refs):
    total, out = refs[-2:]
    count = q.shape[0]
    value = q[...] + received[:count].astype(F32)
    total[...] = value
    out[:count] = value.astype(BF16)
    held = mine.shape[0] - count
    out[count : count + held] = mine[count:]
    out[count + held :] = received[count:]


def join_last_kernel(q, mine, received, *refs):
    out = refs[-1]
    count = q.shape[0]
    out[:count], out[count : 2 * count] = in_two(q[...] + received[:count].astype(F32))
    held = mine.shape[0] - count
    out[2 * count : 2 * count + held] = mine[count:]
    out[2 * count + held :] = received[count:]


def join_views_kernel(count, *refs):
    q, rows = refs[-2:]
    for g in range(q.shape[0]):
        part = refs[g]
        q[g] = part[:count].astype(F32) + part[count : 2 * count].astype(F32)
        rows[g] = part[2 * count :]


def start_kernel(
    fine_rays_in,
    coarse_rays_in,
    fine_in,
    coarse_in,
    fine_weight_in,
    coarse_weight_in,
    fine_axial_in,
    coarse_axial_in,
    measured_in,
    ray_weight_in,
    blocks_in,
    hits_in,
    mine,
    theirs,
    rows,
    out,
    short,
    own_rays,
    fine_rays,
    coarse_rays,
    fine,
    coarse,
    fine_weight,
    coarse_weight,
    fine_axial,
    coarse_axial,
    measured,
    ray_weight,
    blocks,
    hits,
    scratch,
    sems,
    chunk_sems,
):
    me = lax.axis_index("slab")
    core = me % 2
    fz, cells = fine.shape
    half = cells // 2
    sources = (
        (fine_axial_in, fine_axial),
        (coarse_axial_in, coarse_axial),
        (ray_weight_in, ray_weight),
        (measured_in, measured),
        (blocks_in, blocks),
        (hits_in, hits),
        (fine_weight_in, fine_weight),
        (coarse_weight_in, coarse_weight),
    )
    others = [fetch(a, b, sems.at[i]) for i, (a, b) in enumerate(sources)]
    steps = chunk_sems.shape[0]
    chunk = cells // steps
    copies = []
    for i in range(steps):
        part = pl.ds(i * chunk, chunk)
        copies.append(
            [
                fetch(fine_in.at[:, part], fine.at[:, part], chunk_sems.at[i, 0]),
                fetch(coarse_in.at[:, part], coarse.at[:, part], chunk_sems.at[i, 1]),
                fetch(fine_rays_in.at[:, part, :], fine_rays.at[:, part, :], chunk_sems.at[i, 2]),
                fetch(
                    coarse_rays_in.at[:, part, :], coarse_rays.at[:, part, :], chunk_sems.at[i, 3]
                ),
            ]
        )
    share = own_rays.shape[2]
    groups = half // share
    held = pl.ds(share_start(cells, groups), share)
    outgoing = [
        fetch(fine_rays_in.at[:, held, :], own_rays.at[0], sems.at[8]),
        fetch(coarse_rays_in.at[:, held, :], own_rays.at[1], sems.at[9]),
    ]
    for copy in others:
        copy.wait()

    views, _, det = fine_axial.shape
    columns = ray_weight.shape[2]
    total = views * columns
    span = views * det
    own = ray_weight.shape[0]
    coarse_depth = hit_depths(coarse_axial, hits)
    fine_depth = hit_depths(fine_axial, hits)
    wide = max(span, total)
    weight = jnp.concatenate([ray_weight[:, v, :] for v in range(views)], axis=1)
    fine_wide = jnp.concatenate(fine_depth, axis=1)
    if wide > total:
        weight = jnp.concatenate([weight, jnp.zeros((own, wide - total), F32)], axis=1)
    if wide > span:
        fine_wide = jnp.concatenate([fine_wide, jnp.zeros((fz, wide - span), F32)], axis=1)
    stack = [weight, fine_wide]
    if own + fz < PACK:
        stack.append(jnp.zeros((PACK - own - fz, wide), F32))
    packed = jnp.concatenate(coarse_depth + [jnp.concatenate(stack, axis=0)], axis=1).astype(BF16)
    for p in range((span + wide) // total):
        rows[p * PACK : (p + 1) * PACK] = packed[:, p * total : (p + 1) * total]

    for target, side in ((mine, core), (theirs, 1 - core)):
        begin = pl.multiple_of(side * half + lax.axis_index("view") * share, LANES)
        keep = keep_row(blocks, begin, share)
        target[:, :share] = (coarse_weight[:, pl.ds(begin, share)] * keep).astype(BF16)
        target[:, share:] = pack_fine(fine_weight[:, pl.ds(begin, share)]).astype(BF16)

    fine_sum = coarse_sum = None
    for i in range(steps):
        part = slice(i * chunk, (i + 1) * chunk)
        for copy in copies[i]:
            copy.wait()
        keep = keep_row(blocks, i * chunk, chunk)
        fine_rows = fine[:, part].astype(BF16)
        coarse_rows = (coarse[:, part] * keep).astype(BF16)
        fine_wide = jnp.concatenate([fine_rays[v, part, :] for v in range(views)], axis=1)
        coarse_wide = jnp.concatenate([coarse_rays[v, part, :] for v in range(views)], axis=1)
        fine_part = dot(fine_rows, fine_wide, ((1,), (0,)))
        coarse_part = dot(coarse_rows, coarse_wide, ((1,), (0,)))
        fine_sum = fine_part if fine_sum is None else fine_sum + fine_part
        coarse_sum = coarse_part if coarse_sum is None else coarse_sum + coarse_part
    pad = jnp.zeros((PACK - fz, total), F32)
    moment = jnp.concatenate([coarse_sum, fine_sum, pad], axis=0).astype(BF16)
    pad = jnp.zeros((PACK - fz, det), F32)
    row = lax.broadcasted_iota(jnp.int32, (det, columns), 0) - me * own
    for v in range(views):
        depth = jnp.concatenate([coarse_depth[v], fine_depth[v], pad], axis=0).astype(BF16)
        where = slice(v * columns, (v + 1) * columns)
        projection = dot(depth, moment[:, where], ((0,), (0,)))
        given = jnp.zeros((det, columns), F32)
        for i in range(own):
            given = jnp.where(row == i, measured[i : i + 1, v, :], given)
        scratch[:, where] = given - projection
    kept = pl.ds(pl.multiple_of(core * (det // 2), PACK), det // 2)
    sent = pl.ds(pl.multiple_of((1 - core) * (det // 2), PACK), det // 2)
    out[...] = scratch[kept, :]
    short[...] = scratch[sent, :].astype(BF16)
    for copy in outgoing:
        copy.wait()


def slab_of(block, bits):
    me = lax.axis_index("slab")
    apart = jnp.zeros_like(block)
    for place, bit in enumerate(bits):
        apart = apart + ((block >> (place + 1)) & 1) * bit
    return ((me - me % 2) ^ apart) + (block & 1)


def rows_kernel(own, fz, bits, mine, theirs, q_mine, q_theirs, *refs):
    coarse_out, fine_out, coarse_turned, fine_turned, out, q_out = refs[-6:]
    lead = lax.axis_index("slab") % 2 == 0
    kept = q_mine.shape[1]
    for g in range(q_mine.shape[0]):
        ours, others = q_mine[g], q_theirs[g]
        q_out[g, :kept] = jnp.where(lead, ours, others)
        q_out[g, kept:] = jnp.where(lead, others, ours)
    groups, held, total = mine.shape
    slabs = coarse_out.shape[1] // PACK
    height = 2 * held // slabs
    pieces = height // PACK
    det = out.shape[1]
    count = slabs * PACK
    shape = (slabs * own, count)
    w = lax.broadcasted_iota(jnp.int32, shape, 0)
    column = lax.broadcasted_iota(jnp.int32, shape, 1)
    block, row = column // PACK, column % PACK
    match = (row < own) & (w == slab_of(block, bits) * own + row)
    to_weight = jnp.where(match, 1.0, 0.0).astype(BF16)
    shape = (slabs * fz, count)
    z = lax.broadcasted_iota(jnp.int32, shape, 0)
    column = lax.broadcasted_iota(jnp.int32, shape, 1)
    to_fine = jnp.where(column == (z // fz) * PACK + own + z % fz, 1.0, 0.0).astype(BF16)
    for g in range(groups):
        own_rows, other_rows = mine[g].astype(F32), theirs[g].astype(F32)
        even = jnp.where(lead, own_rows, other_rows).astype(BF16)
        odd = jnp.where(lead, other_rows, own_rows).astype(BF16)
        cuts = []
        for p in range(pieces):
            blocks = [
                (even, odd)[j % 2][(j // 2) * height + p * PACK :][:PACK] for j in range(slabs)
            ]
            cuts.append(jnp.concatenate(blocks, axis=0))
        coarse = jnp.concatenate(cuts[: pieces // 2], axis=1)
        side = jnp.concatenate(cuts[pieces // 2 :], axis=1)
        fine = dot(to_fine, side, ((1,), (0,)))
        coarse_out[g] = coarse
        fine_out[g] = fine.astype(BF16)
        wide = coarse.astype(F32)
        for v in range(coarse.shape[1] // det):
            where = slice(v * det, (v + 1) * det)
            coarse_turned[g, v] = wide[:, where].T.astype(BF16)
            fine_turned[g, v] = fine[:, where].T.astype(BF16)
        out[g] = dot(to_weight, side, ((1,), (0,)))[:, :total]


def weights_kernel(fz, order, mine, received, *refs):
    coarse_out, fine_out = refs[-2:]
    held = mine.shape[0]
    slabs = 2 * held
    count = slabs * PACK
    parts = PACK // fz
    size = fine_out.shape[1]
    tiles = packed_tiles(size, fz)
    blocks = [(mine, received)[k // held].at[k % held] for k in order]
    for j, block in enumerate(blocks):
        coarse_out[j * PACK : (j + 1) * PACK] = block[:, :size]
    source = jnp.concatenate([block[:, size : size + tiles * LANES] for block in blocks], axis=0)
    shape = (slabs * fz, count)
    z = lax.broadcasted_iota(jnp.int32, shape, 0)
    column = lax.broadcasted_iota(jnp.int32, shape, 1)
    for k in range(parts):
        choose = jnp.where(column == (z // fz) * PACK + (z % fz) * parts + k, 1.0, 0.0)
        chosen = dot(choose.astype(BF16), source, ((1,), (0,)))
        for c in range(tiles):
            t = c * parts + k
            if t * LANES < size:
                fine_out[:, t * LANES : (t + 1) * LANES] = chosen[
                    :, c * LANES : (c + 1) * LANES
                ].astype(BF16)


def whole_rows(mine, received):
    lead = lax.axis_index("slab") % 2 == 0
    ours, others = mine.astype(F32), received.astype(F32)
    return jnp.concatenate(
        [jnp.where(lead, ours, others), jnp.where(lead, others, ours)], axis=0
    )


def residuals(q, deltas, weights):
    groups = q.shape[0]
    current = [q[g] for g in range(groups)]
    results = [[weights[g] * current[g] for g in range(groups)]]
    for mine, received in deltas:
        current = [current[g] - whole_rows(mine[g], received[g]) for g in range(groups)]
        results.append([weights[g] * current[g] for g in range(groups)])
    return results


def spread(depth, residual, views):
    det, columns = residual.shape[0], residual.shape[1] // views
    pieces = [
        dot(
            depth[:, v * det : (v + 1) * det],
            residual[:, v * columns : (v + 1) * columns],
            ((1,), (0,)),
        )
        for v in range(views)
    ]
    return jnp.concatenate(pieces, axis=1)


def spread_kernel(views, q, weights, fine_depth, coarse_depth, fine_out, coarse_out):
    for g in range(q.shape[0]):
        residual = (weights[g] * q[g]).astype(BF16)
        fine_out[g] = spread(fine_depth[g], residual, views).astype(BF16)
        coarse_out[g] = spread(coarse_depth[g], residual, views).astype(BF16)


def group_rays(held, part, g, cut):
    return jnp.concatenate([held[g][part, v, cut, :] for v in range(held[g].shape[1])], axis=1)


def step_kernel(groups, views, ready, *refs):
    refs = list(refs)
    if ready:
        spreads = [refs.pop(0), refs.pop(0)]
    else:
        q, mine, received, weights, fine_depth, coarse_depth = refs[:6]
        refs = refs[6:]
        residual = residuals(q, [(mine, received)], weights)[-1]
        residual = [r.astype(BF16) for r in residual]
        spreads = [
            [spread(depth[g], residual[g], views).astype(BF16) for g in range(groups)]
            for depth in (fine_depth, coarse_depth)
        ]
    turned = refs[:2]
    coarse_weights, fine_weights = refs[2:4]
    held = refs[4:-3]
    kept, given, scratch = refs[-3:]
    size = fine_weights.shape[1]
    columns = held[0].shape[3]
    chunk = min(size, 1024)
    results = [None] * groups
    for part in range(2):
        moments = [None] * groups
        for c in range(size // chunk):
            cut = slice(c * chunk, (c + 1) * chunk)
            if part == 0:
                weight = fine_weights[:, cut]
            else:
                weight = coarse_weights[:, cut]
            rays = [group_rays(held, part, g, cut) for g in range(groups)]
            back = dot(spreads[part][0], rays[0], ((1,), (1,)))
            for g in range(1, groups):
                back = back + dot(spreads[part][g], rays[g], ((1,), (1,)))
            change = (weight.astype(F32) * back).astype(BF16)
            for g in range(groups):
                moment = dot(change, rays[g], ((1,), (0,)))
                moments[g] = moment if moments[g] is None else moments[g] + moment
        for g in range(groups):
            moment = moments[g].astype(BF16)
            pieces = [
                dot(turned[part][g, v], moment[:, v * columns : (v + 1) * columns], ((1,), (0,)))
                for v in range(views)
            ]
            value = jnp.concatenate(pieces, axis=1)
            results[g] = value if results[g] is None else results[g] + value
    core = lax.axis_index("slab") % 2
    rows = kept.shape[1]
    for g in range(groups):
        scratch[g] = results[g]
        kept[g] = scratch[g, pl.ds(pl.multiple_of(core * rows, PACK), rows), :].astype(BF16)
        given[g] = scratch[g, pl.ds(pl.multiple_of((1 - core) * rows, PACK), rows), :].astype(BF16)


def add_kernel(bit, mine, received, out):
    for g in range(mine.shape[0]):
        out[g] = (mine[g].astype(F32) + received[g ^ bit].astype(F32)).astype(BF16)


def tail_kernel(fz, groups, views, q, *refs):
    deltas = [refs[:2], refs[2:4]]
    weights, fine_depth, coarse_depth = refs[4:7]
    held = refs[7:-2]
    ours, theirs = refs[-2:]
    size = held[0].shape[2]
    chunk = min(size, 1024)
    lead = lax.axis_index("slab") % 2 == 0
    history = residuals(q, deltas, weights)
    rows = (fz, PACK)
    spreads = ([], [])
    for g in range(groups):
        value = history[0][g]
        for other in history[1:]:
            value = value + other[g]
        high, low = in_two(value)
        for part, depth in enumerate((fine_depth[g, : 2 * fz], coarse_depth[g, : 2 * PACK])):
            pair = in_two(spread(depth, high, views) + spread(depth, low, views))
            spreads[part].append(jnp.concatenate(pair, axis=0))
    backs = ([], [])
    for part in range(2):
        for c in range(size // chunk):
            cut = slice(c * chunk, (c + 1) * chunk)
            back = None
            for g in range(groups):
                value = dot(spreads[part][g], group_rays(held, part, g, cut), ((1,), (1,)))
                back = value if back is None else back + value
            backs[part].append(back[: 2 * rows[part]] + back[2 * rows[part] :])
    for out, first in ((ours, lead), (theirs, jnp.logical_not(lead))):
        parts = []
        for part in range(2):
            back = jnp.concatenate(backs[part], axis=1)
            parts.append(jnp.where(first, back[: rows[part]], back[rows[part] :]))
        out[:, :size] = parts[1].astype(BF16)
        out[:, size:] = pack_fine(parts[0]).astype(BF16)


def keep_kernel(blocks, out):
    out[...] = keep_row(blocks, 0, out.shape[1])


def final_kernel(groups, size, *refs):
    pieces = refs[: 2 * groups]
    fine, coarse, fw, cw, keep, fine_out, coarse_out = refs[2 * groups :]
    core = lax.axis_index("slab") % 2
    view = lax.axis_index("view")
    fz, cells = fine.shape
    for index, piece in enumerate(pieces):
        side = core if index < groups else 1 - core
        start = side * (cells // 2) + (view ^ (index % groups)) * size
        start = pl.multiple_of(start, LANES)
        where = pl.ds(start, size)
        change = piece[:, :size].astype(F32)
        coarse_out[:, where] = (coarse[:, where] + cw[:, where] * change) * keep[:, where]
        change = unpack_fine(piece[:, size:].astype(F32), fz, size)
        fine_out[:, where] = fine[:, where] + fw[:, where] * change


def make_body(slabs, groups):
    far_bits = [1 << k for k in range(slabs.bit_length() - 2, 1, -1)]
    view_bits = [1 << k for k in range(groups.bit_length() - 1)]

    def along_slab(value, bit):
        return swap(value, "slab", slabs, bit)

    def body(
        fine_volume,
        coarse_volume,
        fine_rays,
        coarse_rays,
        fine_axial,
        coarse_axial,
        measured,
        ray_weight,
        fine_cell_weight,
        coarse_cell_weight,
        margin_blocks,
        ray_hits,
    ):
        views, cells, columns = fine_rays.shape
        det = fine_axial.shape[2]
        fz, cz = fine_volume.shape[0], coarse_volume.shape[0]
        own = measured.shape[0]
        total = views * columns
        span = max(views * det, total)
        share = cells // 2 // groups
        lead = lax.axis_index("slab") % 2 == 0
        width = share + packed_tiles(share, fz) * LANES

        taken = in_hbm(
            fine_rays,
            coarse_rays,
            fine_volume,
            coarse_volume,
            fine_cell_weight,
            coarse_cell_weight,
            fine_axial,
            coarse_axial,
            measured,
            ray_weight,
        )
        height = PACK * ((views * det + span) // total)
        mine, theirs, rows, q, short, own_rays = call(
            start_kernel,
            "start",
            (
                shaped((PACK, width), BF16),
                shaped((PACK, width), BF16),
                shaped((height, total), BF16),
                shaped((det // 2, total), F32),
                shaped((det // 2, total), BF16),
                shaped((2, views, share, columns), BF16),
            ),
            [HBM] * (len(taken) + 2),
            scratch_like(*taken)
            + [
                pltpu.SMEM(margin_blocks.shape, jnp.int32),
                pltpu.SMEM(ray_hits.shape, jnp.int32),
                pltpu.VMEM((det, total), F32),
                pltpu.SemaphoreType.DMA((10,)),
                pltpu.SemaphoreType.DMA((4, 4)),
            ],
        )(*taken, *in_hbm(margin_blocks, ray_hits))

        def to_views(value):
            values = [value]
            for bit in view_bits:
                values += [swap(one, "view", groups, bit) for one in values]
            return values

        rows_half = det // 2
        got = {}

        def begin(stage, token):
            waits = [] if token is None else [token]
            if SOURCE["rays"] == stage:
                got["rays"] = []
                for bits in range(1, groups):
                    value = call(
                        functools.partial(take_kernel, groups, bits),
                        "take_rays",
                        shaped((2, views, share, columns), BF16),
                        [HBM] * 2 + [ANY] * len(waits),
                        [pltpu.SemaphoreType.DMA((2,))],
                    )(*in_hbm(fine_rays, coarse_rays), *waits)
                    got["rays"].append(swap(value, "view", groups, bits))
            for index, bit in enumerate(far_bits + [2]):
                if SOURCE["weights"][min(index, 2)] != stage:
                    continue
                if index == 0:
                    packed = call(
                        pair_kernel,
                        "pair",
                        shaped((2, PACK, width), BF16),
                        [VMEM] * 2 + [ANY] * len(waits),
                    )(mine, along_slab(theirs, 1), *waits)
                else:
                    packed, hop = got["weights"]
                    packed = call(
                        join_blocks_kernel,
                        "join_blocks",
                        shaped((2 * packed.shape[0], PACK, width), BF16),
                        [VMEM] * 2 + [ANY] * len(waits),
                    )(packed, hop, *waits)
                got["w%d" % index] = [along_slab(packed, bit)]
                got["weights"] = (packed, got["w%d" % index][0])

        def waits_of(stage):
            found = []
            for name, where in AWAITED.items():
                if where == stage:
                    found += got.get(name, [])
            return found

        begin("start", None)
        waits = waits_of("core")
        q, mixed = call(
            join_core_kernel,
            "join_core",
            (shaped((rows_half, total), F32), shaped((rows_half + height, total), BF16)),
            [VMEM] * 3 + [ANY] * len(waits),
        )(q, along_slab(short, 1), rows, *waits)
        begin("core", mixed)
        for index, bit in enumerate([2] + far_bits):
            last = index == len(far_bits)
            name = "last" if last else "hop%d" % index
            waits = waits_of(name)
            inputs = (q, mixed, along_slab(mixed, bit), *waits)
            specs = [VMEM] * 3 + [ANY] * len(waits)
            size = 2 * mixed.shape[0]
            if last:
                mixed = call(join_last_kernel, "join_last", shaped((size, total), BF16), specs)(
                    *inputs
                )
            else:
                q, mixed = call(
                    join_hop_kernel,
                    "join_hop",
                    (shaped(q.shape, F32), shaped((size - rows_half, total), BF16)),
                    specs,
                )(*inputs)
            begin(name, mixed)
        waits = waits_of("views")
        q, rows = call(
            functools.partial(join_views_kernel, rows_half),
            "join_views",
            (
                shaped((groups, rows_half, total), F32),
                shaped((groups, mixed.shape[0] - 2 * rows_half, total), BF16),
            ),
            [VMEM] * groups + [ANY] * len(waits),
        )(*to_views(mixed), *waits)
        count = len(far_bits)
        order = tuple(
            (j & 1) + 2 * (j >> 2) + (((j >> 1) & 1) << (count + 1)) for j in range(slabs)
        )
        waits = waits_of("rows")
        coarse_depth, fine_depth, coarse_turned, fine_turned, weights, q = call(
            functools.partial(rows_kernel, own, fz, [2] + far_bits),
            "unpack_rows",
            (
                shaped((groups, slabs * PACK, span), BF16),
                shaped((groups, slabs * fz, span), BF16),
                shaped((groups, views, det, slabs * PACK), BF16),
                shaped((groups, views, det, slabs * fz), BF16),
                shaped((groups, det, total), F32),
                shaped((groups, det, total), F32),
            ),
            [VMEM] * 4 + [ANY] * len(waits),
        )(rows, along_slab(rows, 1), q, along_slab(q, 1), *waits)
        spreads = call(
            functools.partial(spread_kernel, views),
            "spread",
            (
                shaped((groups, slabs * fz, total), BF16),
                shaped((groups, slabs * PACK, total), BF16),
            ),
            [VMEM] * 4,
        )(q, weights, fine_depth, coarse_depth)
        coarse_weights, fine_weights = call(
            functools.partial(weights_kernel, fz, order),
            "unpack_weights",
            (shaped((slabs * PACK, share), BF16), shaped((slabs * fz, share), BF16)),
            [VMEM] * 2 + [ANY] * len(spreads),
        )(*got["weights"], *spreads)
        rays = [own_rays] + got["rays"]
        held = (fine_turned, coarse_turned, coarse_weights, fine_weights, *rays)
        def add(mine, received, bit):
            return call(
                functools.partial(add_kernel, bit),
                "add",
                shaped((groups, rows_half, total), BF16),
                [VMEM] * 2,
            )(mine, received)

        deltas = []
        for ready, inputs in ((True, spreads), (False, None)):
            if not ready:
                inputs = (q, *deltas, weights, fine_depth, coarse_depth)
            delta, given = call(
                functools.partial(step_kernel, groups, views, ready),
                "ray_space_step",
                (shaped((groups, rows_half, total), BF16),) * 2,
                [VMEM] * (len(inputs) + len(held)),
                [pltpu.VMEM((groups, det, total), F32)],
            )(*inputs, *held)
            delta = add(delta, along_slab(given, 1), 0)
            for bit in view_bits:
                delta = add(delta, swap(delta, "view", groups, bit), bit)
            deltas += [delta, along_slab(delta, 1)]
        inputs = (q, *deltas, weights, fine_depth, coarse_depth, *rays)
        ours, theirs = call(
            functools.partial(tail_kernel, fz, groups, views),
            "back_projection",
            (shaped((PACK, width), BF16),) * 2,
            [VMEM] * len(inputs),
        )(*inputs)
        keep = call(keep_kernel, "keep", shaped((1, cells), F32), [SMEM])(margin_blocks)
        both = ("slab", "view")
        pieces = [ours] + [swap(ours, "view", groups, bits) for bits in range(1, groups)]
        pieces += [swap(theirs, both, slabs * groups, groups | bits) for bits in range(groups)]
        return call(
            functools.partial(final_kernel, groups, share),
            "update",
            (shaped(fine_volume.shape, F32), shaped(coarse_volume.shape, F32)),
            [VMEM] * (2 * groups + 5),
        )(
            *pieces,
            fine_volume,
            coarse_volume,
            fine_cell_weight,
            coarse_cell_weight,
            keep,
        )

    return body


def solution(mesh):
    return jax.shard_map(
        make_body(mesh.shape["slab"], mesh.shape["view"]),
        mesh=mesh,
        in_specs=(
            P("slab", None),
            P("slab", None),
            P("view", None, None),
            P("view", None, None),
            P("view", "slab", None),
            P("view", "slab", None),
            P("slab", "view", None),
            P("slab", "view", None),
            P("slab", None),
            P("slab", None),
            P("slab", None),
            P("view", "slab", None),
        ),
        out_specs=(P("slab", None), P("slab", None)),
        check_vma=False,
    )
```

```python
import functools
import jax
import jax.numpy as jnp
from jax import lax
from jax.experimental import pallas as pl
from jax.experimental.pallas import tpu as pltpu
from jax.sharding import PartitionSpec as P

BLOCK = 128
LANES = 128
PACK = 16
F32 = jnp.float32
BF16 = jnp.bfloat16
PARAMS = pltpu.CompilerParams(vmem_limit_bytes=24 * 1024 * 1024)
VMEM = pl.BlockSpec(memory_space=pltpu.VMEM)
SMEM = pl.BlockSpec(memory_space=pltpu.SMEM)
ANY = pl.BlockSpec(memory_space=pl.ANY)
HBM = pl.BlockSpec(memory_space=pltpu.HBM)
SOURCE = {'rays': 'start', 'weights': ("start", "core", "hop1")}
AWAITED = {"rays": "views", "w1": "last"}
QUICK = pl.CostEstimate(flops=1, bytes_accessed=1, transcendentals=0)


def fetch(source, target, sem):
    copy = pltpu.make_async_copy(source, target, sem)
    copy.start()
    return copy


def in_hbm(*arrays):
    return [pltpu.with_memory_space_constraint(a, pltpu.HBM) for a in arrays]


def scratch_like(*arrays):
    return [pltpu.VMEM(a.shape, a.dtype) for a in arrays]


def shaped(shape, dtype):
    return jax.ShapeDtypeStruct(shape, dtype)


def call(kernel, name, out_shape, in_specs, scratch=()):
    many = isinstance(out_shape, tuple)
    return pl.pallas_call(
        kernel,
        out_shape=out_shape,
        in_specs=in_specs,
        out_specs=(VMEM,) * len(out_shape) if many else VMEM,
        scratch_shapes=list(scratch),
        compiler_params=PARAMS,
        cost_estimate=QUICK,
        name=name,
    )


def swap(value, axis, size, bits):
    return lax.ppermute(value, axis, [(i, i ^ bits) for i in range(size)])


def dot(a, b, dims):
    return lax.dot_general(a, b, (dims, ((), ())), preferred_element_type=F32)


def in_two(value):
    high = value.astype(BF16)
    return high, (value - high.astype(F32)).astype(BF16)


def keep_row(blocks_ref, start, width):
    ids = (lax.broadcasted_iota(jnp.int32, (1, width), 1) + start) // BLOCK
    keep = jnp.ones((1, width), F32)
    for k in range(blocks_ref.shape[1]):
        keep = jnp.where(ids == blocks_ref[0, k], 0.0, keep)
    return keep


def share_start(cells, groups, bits=0):
    core = lax.axis_index("slab") % 2
    share = cells // 2 // groups
    return pl.multiple_of(core * (cells // 2) + (lax.axis_index("view") ^ bits) * share, LANES)


def packed_tiles(cells, fz):
    parts = PACK // fz
    return -(-(cells // LANES) // parts)


def pack_fine(rows):
    fz, size = rows.shape
    parts = PACK // fz
    empty = jnp.zeros((1, LANES), rows.dtype)
    columns = []
    for c in range(packed_tiles(size, fz)):
        pieces = []
        for i in range(fz):
            for k in range(parts):
                t = c * parts + k
                inside = t * LANES < size
                pieces.append(rows[i : i + 1, t * LANES : (t + 1) * LANES] if inside else empty)
        columns.append(jnp.concatenate(pieces, axis=0))
    return jnp.concatenate(columns, axis=1)


def unpack_fine(packed, fz, size):
    parts = PACK // fz
    rows = []
    for i in range(fz):
        pieces = []
        for t in range(size // LANES):
            row, column = i * parts + t % parts, t // parts * LANES
            pieces.append(packed[row : row + 1, column : column + LANES])
        rows.append(jnp.concatenate(pieces, axis=1))
    return jnp.concatenate(rows, axis=0)


def hit_depths(axial, hits):
    views, _, det = axial.shape
    tiles = hits.shape[2]
    tile = lax.broadcasted_iota(jnp.int32, (1, det), 1) // (det // tiles)
    result = []
    for v in range(views):
        hit = jnp.zeros((1, det), F32)
        for t in range(tiles):
            hit = jnp.where(tile == t, hits[v, 0, t].astype(F32), hit)
        result.append(axial[v].astype(F32) * hit)
    return result


def take_kernel(groups, bits, fine_rays, coarse_rays, *refs):
    out, sems = refs[-2:]
    cells = pl.ds(share_start(fine_rays.shape[1], groups, bits), out.shape[2])
    copies = [
        fetch(rays.at[:, cells, :], out.at[part], sems.at[part])
        for part, rays in enumerate((fine_rays, coarse_rays))
    ]
    for copy in copies:
        copy.wait()


def pair_kernel(mine, received, *refs):
    out = refs[-1]
    lead = lax.axis_index("slab") % 2 == 0
    own, other = mine[...].astype(F32), received[...].astype(F32)
    out[0] = jnp.where(lead, own, other).astype(BF16)
    out[1] = jnp.where(lead, other, own).astype(BF16)


def join_blocks_kernel(mine, received, *refs):
    out = refs[-1]
    out[: mine.shape[0]] = mine[...]
    out[mine.shape[0] :] = received[...]


def join_core_kernel(q, received, rows, *refs):
    total, out = refs[-2:]
    count = q.shape[0]
    value = q[...] + received[...].astype(F32)
    total[...] = value
    out[:count] = value.astype(BF16)
    out[count:] = rows[...]


def join_hop_kernel(q, mine, received, *refs):
    total, out = refs[-2:]
    count = q.shape[0]
    value = q[...] + received[:count].astype(F32)
    total[...] = value
    out[:count] = value.astype(BF16)
    held = mine.shape[0] - count
    out[count : count + held] = mine[count:]
    out[count + held :] = received[count:]


def join_last_kernel(q, mine, received, *refs):
    out = refs[-1]
    count = q.shape[0]
    out[:count], out[count : 2 * count] = in_two(q[...] + received[:count].astype(F32))
    held = mine.shape[0] - count
    out[2 * count : 2 * count + held] = mine[count:]
    out[2 * count + held :] = received[count:]


def join_views_kernel(count, *refs):
    q, rows = refs[-2:]
    for g in range(q.shape[0]):
        part = refs[g]
        q[g] = part[:count].astype(F32) + part[count : 2 * count].astype(F32)
        rows[g] = part[2 * count :]


def start_kernel(
    fine_rays_in,
    coarse_rays_in,
    fine_in,
    coarse_in,
    fine_weight_in,
    coarse_weight_in,
    fine_axial,
    coarse_axial_in,
    measured_in,
    ray_weight_in,
    blocks_in,
    hits_in,
    mine,
    theirs,
    rows,
    out,
    short,
    own_rays,
    fine_rays,
    coarse_rays,
    fine,
    coarse,
    fine_weight,
    coarse_weight,
    coarse_axial,
    measured,
    ray_weight,
    blocks,
    hits,
    scratch,
    sems,
    chunk_sems,
):
    me = lax.axis_index("slab")
    core = me % 2
    fz, cells = fine.shape
    half = cells // 2
    sources = (
        (coarse_axial_in, coarse_axial),
        (ray_weight_in, ray_weight),
        (measured_in, measured),
        (blocks_in, blocks),
        (hits_in, hits),
        (fine_weight_in, fine_weight),
        (coarse_weight_in, coarse_weight),
    )
    others = [fetch(a, b, sems.at[i]) for i, (a, b) in enumerate(sources)]
    steps = chunk_sems.shape[0]
    chunk = cells // steps
    copies = []
    for i in range(steps):
        part = pl.ds(i * chunk, chunk)
        copies.append(
            [
                fetch(fine_in.at[:, part], fine.at[:, part], chunk_sems.at[i, 0]),
                fetch(coarse_in.at[:, part], coarse.at[:, part], chunk_sems.at[i, 1]),
                fetch(fine_rays_in.at[:, part, :], fine_rays.at[:, part, :], chunk_sems.at[i, 2]),
                fetch(
                    coarse_rays_in.at[:, part, :], coarse_rays.at[:, part, :], chunk_sems.at[i, 3]
                ),
            ]
        )
    share = own_rays.shape[2]
    groups = half // share
    held = pl.ds(share_start(cells, groups), share)
    outgoing = [
        fetch(fine_rays_in.at[:, held, :], own_rays.at[0], sems.at[8]),
        fetch(coarse_rays_in.at[:, held, :], own_rays.at[1], sems.at[9]),
    ]
    for copy in others:
        copy.wait()

    views, _, det = fine_axial.shape
    columns = ray_weight.shape[2]
    total = views * columns
    span = views * det
    own = ray_weight.shape[0]
    coarse_depth = hit_depths(coarse_axial, hits)
    fine_depth = hit_depths(fine_axial, hits)
    wide = max(span, total)
    weight = jnp.concatenate([ray_weight[:, v, :] for v in range(views)], axis=1)
    fine_wide = jnp.concatenate(fine_depth, axis=1)
    if wide > total:
        weight = jnp.concatenate([weight, jnp.zeros((own, wide - total), F32)], axis=1)
    if wide > span:
        fine_wide = jnp.concatenate([fine_wide, jnp.zeros((fz, wide - span), F32)], axis=1)
    stack = [weight, fine_wide]
    if own + fz < PACK:
        stack.append(jnp.zeros((PACK - own - fz, wide), F32))
    packed = jnp.concatenate(coarse_depth + [jnp.concatenate(stack, axis=0)], axis=1).astype(BF16)
    for p in range((span + wide) // total):
        rows[p * PACK : (p + 1) * PACK] = packed[:, p * total : (p + 1) * total]

    for target, side in ((mine, core), (theirs, 1 - core)):
        begin = pl.multiple_of(side * half + lax.axis_index("view") * share, LANES)
        keep = keep_row(blocks, begin, share)
        target[:, :share] = (coarse_weight[:, pl.ds(begin, share)] * keep).astype(BF16)
        target[:, share:] = pack_fine(fine_weight[:, pl.ds(begin, share)]).astype(BF16)

    fine_sum = coarse_sum = None
    for i in range(steps):
        part = slice(i * chunk, (i + 1) * chunk)
        for copy in copies[i]:
            copy.wait()
        keep = keep_row(blocks, i * chunk, chunk)
        fine_rows = fine[:, part].astype(BF16)
        coarse_rows = (coarse[:, part] * keep).astype(BF16)
        fine_wide = jnp.concatenate([fine_rays[v, part, :] for v in range(views)], axis=1)
        coarse_wide = jnp.concatenate([coarse_rays[v, part, :] for v in range(views)], axis=1)
        fine_part = dot(fine_rows, fine_wide, ((1,), (0,)))
        coarse_part = dot(coarse_rows, coarse_wide, ((1,), (0,)))
        fine_sum = fine_part if fine_sum is None else fine_sum + fine_part
        coarse_sum = coarse_part if coarse_sum is None else coarse_sum + coarse_part
    pad = jnp.zeros((PACK - fz, total), F32)
    moment = jnp.concatenate([coarse_sum, fine_sum, pad], axis=0).astype(BF16)
    pad = jnp.zeros((PACK - fz, det), F32)
    row = lax.broadcasted_iota(jnp.int32, (det, columns), 0) - me * own
    for v in range(views):
        depth = jnp.concatenate([coarse_depth[v], fine_depth[v], pad], axis=0).astype(BF16)
        where = slice(v * columns, (v + 1) * columns)
        projection = dot(depth, moment[:, where], ((0,), (0,)))
        given = jnp.zeros((det, columns), F32)
        for i in range(own):
            given = jnp.where(row == i, measured[i : i + 1, v, :], given)
        scratch[:, where] = given - projection
    kept = pl.ds(pl.multiple_of(core * (det // 2), PACK), det // 2)
    sent = pl.ds(pl.multiple_of((1 - core) * (det // 2), PACK), det // 2)
    out[...] = scratch[kept, :]
    short[...] = scratch[sent, :].astype(BF16)
    for copy in outgoing:
        copy.wait()


def slab_of(block, bits):
    me = lax.axis_index("slab")
    apart = jnp.zeros_like(block)
    for place, bit in enumerate(bits):
        apart = apart + ((block >> (place + 1)) & 1) * bit
    return ((me - me % 2) ^ apart) + (block & 1)


def rows_kernel(own, fz, bits, mine, theirs, q_mine, q_theirs, *refs):
    coarse_out, fine_out, coarse_turned, fine_turned, out, q_out = refs[-6:]
    lead = lax.axis_index("slab") % 2 == 0
    kept = q_mine.shape[1]
    for g in range(q_mine.shape[0]):
        ours, others = q_mine[g], q_theirs[g]
        q_out[g, :kept] = jnp.where(lead, ours, others)
        q_out[g, kept:] = jnp.where(lead, others, ours)
    groups, held, total = mine.shape
    slabs = coarse_out.shape[1] // PACK
    height = 2 * held // slabs
    pieces = height // PACK
    det = out.shape[1]
    count = slabs * PACK
    shape = (slabs * own, count)
    w = lax.broadcasted_iota(jnp.int32, shape, 0)
    column = lax.broadcasted_iota(jnp.int32, shape, 1)
    block, row = column // PACK, column % PACK
    match = (row < own) & (w == slab_of(block, bits) * own + row)
    to_weight = jnp.where(match, 1.0, 0.0).astype(BF16)
    shape = (slabs * fz, count)
    z = lax.broadcasted_iota(jnp.int32, shape, 0)
    column = lax.broadcasted_iota(jnp.int32, shape, 1)
    to_fine = jnp.where(column == (z // fz) * PACK + own + z % fz, 1.0, 0.0).astype(BF16)
    for g in range(groups):
        own_rows, other_rows = mine[g].astype(F32), theirs[g].astype(F32)
        even = jnp.where(lead, own_rows, other_rows).astype(BF16)
        odd = jnp.where(lead, other_rows, own_rows).astype(BF16)
        cuts = []
        for p in range(pieces):
            blocks = [
                (even, odd)[j % 2][(j // 2) * height + p * PACK :][:PACK] for j in range(slabs)
            ]
            cuts.append(jnp.concatenate(blocks, axis=0))
        coarse = jnp.concatenate(cuts[: pieces // 2], axis=1)
        side = jnp.concatenate(cuts[pieces // 2 :], axis=1)
        fine = dot(to_fine, side, ((1,), (0,)))
        coarse_out[g] = coarse
        fine_out[g] = fine.astype(BF16)
        wide = coarse.astype(F32)
        for v in range(coarse.shape[1] // det):
            where = slice(v * det, (v + 1) * det)
            coarse_turned[g, v] = wide[:, where].T.astype(BF16)
            fine_turned[g, v] = fine[:, where].T.astype(BF16)
        out[g] = dot(to_weight, side, ((1,), (0,)))[:, :total]


def weights_kernel(fz, order, mine, received, *refs):
    coarse_out, fine_out = refs[-2:]
    held = mine.shape[0]
    slabs = 2 * held
    count = slabs * PACK
    parts = PACK // fz
    size = fine_out.shape[1]
    tiles = packed_tiles(size, fz)
    blocks = [(mine, received)[k // held].at[k % held] for k in order]
    for j, block in enumerate(blocks):
        coarse_out[j * PACK : (j + 1) * PACK] = block[:, :size]
    source = jnp.concatenate([block[:, size : size + tiles * LANES] for block in blocks], axis=0)
    shape = (slabs * fz, count)
    z = lax.broadcasted_iota(jnp.int32, shape, 0)
    column = lax.broadcasted_iota(jnp.int32, shape, 1)
    for k in range(parts):
        choose = jnp.where(column == (z // fz) * PACK + (z % fz) * parts + k, 1.0, 0.0)
        chosen = dot(choose.astype(BF16), source, ((1,), (0,)))
        for c in range(tiles):
            t = c * parts + k
            if t * LANES < size:
                fine_out[:, t * LANES : (t + 1) * LANES] = chosen[
                    :, c * LANES : (c + 1) * LANES
                ].astype(BF16)


def whole_rows(mine, received):
    lead = lax.axis_index("slab") % 2 == 0
    ours, others = mine.astype(F32), received.astype(F32)
    return jnp.concatenate(
        [jnp.where(lead, ours, others), jnp.where(lead, others, ours)], axis=0
    )


def residuals(q, deltas, weights):
    groups = q.shape[0]
    current = [q[g] for g in range(groups)]
    results = [[weights[g] * current[g] for g in range(groups)]]
    for mine, received in deltas:
        current = [current[g] - whole_rows(mine[g], received[g]) for g in range(groups)]
        results.append([weights[g] * current[g] for g in range(groups)])
    return results


def spread(depth, residual, views):
    det, columns = residual.shape[0], residual.shape[1] // views
    pieces = [
        dot(
            depth[:, v * det : (v + 1) * det],
            residual[:, v * columns : (v + 1) * columns],
            ((1,), (0,)),
        )
        for v in range(views)
    ]
    return jnp.concatenate(pieces, axis=1)


def spread_kernel(views, q, weights, fine_depth, coarse_depth, fine_out, coarse_out):
    for g in range(q.shape[0]):
        residual = (weights[g] * q[g]).astype(BF16)
        fine_out[g] = spread(fine_depth[g], residual, views).astype(BF16)
        coarse_out[g] = spread(coarse_depth[g], residual, views).astype(BF16)


def group_rays(held, part, g, cut):
    return jnp.concatenate([held[g][part, v, cut, :] for v in range(held[g].shape[1])], axis=1)


def step_kernel(groups, views, ready, *refs):
    refs = list(refs)
    if ready:
        spreads = [refs.pop(0), refs.pop(0)]
    else:
        q, mine, received, weights, fine_depth, coarse_depth = refs[:6]
        refs = refs[6:]
        residual = residuals(q, [(mine, received)], weights)[-1]
        residual = [r.astype(BF16) for r in residual]
        spreads = [
            [spread(depth[g], residual[g], views).astype(BF16) for g in range(groups)]
            for depth in (fine_depth, coarse_depth)
        ]
    turned = refs[:2]
    coarse_weights, fine_weights = refs[2:4]
    held = refs[4:-3]
    kept, given, scratch = refs[-3:]
    size = fine_weights.shape[1]
    columns = held[0].shape[3]
    chunk = min(size, 1024)
    results = [None] * groups
    for part in range(2):
        moments = [None] * groups
        for c in range(size // chunk):
            cut = slice(c * chunk, (c + 1) * chunk)
            if part == 0:
                weight = fine_weights[:, cut]
            else:
                weight = coarse_weights[:, cut]
            rays = [group_rays(held, part, g, cut) for g in range(groups)]
            back = dot(spreads[part][0], rays[0], ((1,), (1,)))
            for g in range(1, groups):
                back = back + dot(spreads[part][g], rays[g], ((1,), (1,)))
            change = (weight.astype(F32) * back).astype(BF16)
            for g in range(groups):
                moment = dot(change, rays[g], ((1,), (0,)))
                moments[g] = moment if moments[g] is None else moments[g] + moment
        for g in range(groups):
            moment = moments[g].astype(BF16)
            pieces = [
                dot(turned[part][g, v], moment[:, v * columns : (v + 1) * columns], ((1,), (0,)))
                for v in range(views)
            ]
            value = jnp.concatenate(pieces, axis=1)
            results[g] = value if results[g] is None else results[g] + value
    core = lax.axis_index("slab") % 2
    rows = kept.shape[1]
    for g in range(groups):
        scratch[g] = results[g]
        kept[g] = scratch[g, pl.ds(pl.multiple_of(core * rows, PACK), rows), :].astype(BF16)
        given[g] = scratch[g, pl.ds(pl.multiple_of((1 - core) * rows, PACK), rows), :].astype(BF16)


def add_kernel(bit, mine, received, out):
    for g in range(mine.shape[0]):
        out[g] = (mine[g].astype(F32) + received[g ^ bit].astype(F32)).astype(BF16)


def tail_kernel(fz, groups, views, q, *refs):
    deltas = [refs[:2], refs[2:4]]
    weights, fine_depth, coarse_depth = refs[4:7]
    held = refs[7:-2]
    ours, theirs = refs[-2:]
    size = held[0].shape[2]
    chunk = min(size, 1024)
    lead = lax.axis_index("slab") % 2 == 0
    history = residuals(q, deltas, weights)
    rows = (fz, PACK)
    spreads = ([], [])
    for g in range(groups):
        value = history[0][g]
        for other in history[1:]:
            value = value + other[g]
        high, low = in_two(value)
        fine_rows = fine_depth[g, : 2 * PACK].astype(F32)[: 2 * fz].astype(BF16)
        for part, depth in enumerate((fine_rows, coarse_depth[g, : 2 * PACK])):
            pair = in_two(spread(depth, high, views) + spread(depth, low, views))
            spreads[part].append(jnp.concatenate(pair, axis=0))
    backs = ([], [])
    for part in range(2):
        for c in range(size // chunk):
            cut = slice(c * chunk, (c + 1) * chunk)
            back = None
            for g in range(groups):
                value = dot(spreads[part][g], group_rays(held, part, g, cut), ((1,), (1,)))
                back = value if back is None else back + value
            backs[part].append(back[: 2 * rows[part]] + back[2 * rows[part] :])
    for out, first in ((ours, lead), (theirs, jnp.logical_not(lead))):
        parts = []
        for part in range(2):
            back = jnp.concatenate(backs[part], axis=1)
            parts.append(jnp.where(first, back[: rows[part]], back[rows[part] :]))
        out[:, :size] = parts[1].astype(BF16)
        out[:, size:] = pack_fine(parts[0]).astype(BF16)


def keep_kernel(blocks, out):
    out[...] = keep_row(blocks, 0, out.shape[1])


def final_kernel(groups, size, *refs):
    pieces = refs[: 2 * groups]
    fine, coarse, fw, cw, keep, fine_out, coarse_out = refs[2 * groups :]
    core = lax.axis_index("slab") % 2
    view = lax.axis_index("view")
    fz, cells = fine.shape
    for index, piece in enumerate(pieces):
        side = core if index < groups else 1 - core
        start = side * (cells // 2) + (view ^ (index % groups)) * size
        start = pl.multiple_of(start, LANES)
        where = pl.ds(start, size)
        change = piece[:, :size].astype(F32)
        coarse_out[:, where] = (coarse[:, where] + cw[:, where] * change) * keep[:, where]
        change = unpack_fine(piece[:, size:].astype(F32), fz, size)
        fine_out[:, where] = fine[:, where] + fw[:, where] * change


def make_body(slabs, groups):
    far_bits = [1 << k for k in range(slabs.bit_length() - 2, 1, -1)]
    view_bits = [1 << k for k in range(groups.bit_length() - 1)]

    def along_slab(value, bit):
        return swap(value, "slab", slabs, bit)

    def body(
        fine_volume,
        coarse_volume,
        fine_rays,
        coarse_rays,
        fine_axial,
        coarse_axial,
        measured,
        ray_weight,
        fine_cell_weight,
        coarse_cell_weight,
        margin_blocks,
        ray_hits,
    ):
        views, cells, columns = fine_rays.shape
        det = fine_axial.shape[2]
        fz, cz = fine_volume.shape[0], coarse_volume.shape[0]
        own = measured.shape[0]
        total = views * columns
        span = max(views * det, total)
        share = cells // 2 // groups
        lead = lax.axis_index("slab") % 2 == 0
        width = share + packed_tiles(share, fz) * LANES

        taken = in_hbm(
            fine_rays,
            coarse_rays,
            fine_volume,
            coarse_volume,
            fine_cell_weight,
            coarse_cell_weight,
            coarse_axial,
            measured,
            ray_weight,
        )
        height = PACK * ((views * det + span) // total)
        mine, theirs, rows, q, short, own_rays = call(
            start_kernel,
            "start",
            (
                shaped((PACK, width), BF16),
                shaped((PACK, width), BF16),
                shaped((height, total), BF16),
                shaped((det // 2, total), F32),
                shaped((det // 2, total), BF16),
                shaped((2, views, share, columns), BF16),
            ),
            [HBM] * 6 + [VMEM] + [HBM] * 5,
            scratch_like(*taken)
            + [
                pltpu.SMEM(margin_blocks.shape, jnp.int32),
                pltpu.SMEM(ray_hits.shape, jnp.int32),
                pltpu.VMEM((det, total), F32),
                pltpu.SemaphoreType.DMA((10,)),
                pltpu.SemaphoreType.DMA((4, 4)),
            ],
        )(*taken[:6], fine_axial, *taken[6:], *in_hbm(margin_blocks, ray_hits))

        def to_views(value):
            values = [value]
            for bit in view_bits:
                values += [swap(one, "view", groups, bit) for one in values]
            return values

        rows_half = det // 2
        got = {}

        def begin(stage, token):
            waits = [] if token is None else [token]
            if SOURCE["rays"] == stage:
                got["rays"] = []
                for bits in range(1, groups):
                    value = call(
                        functools.partial(take_kernel, groups, bits),
                        "take_rays",
                        shaped((2, views, share, columns), BF16),
                        [HBM] * 2 + [ANY] * len(waits),
                        [pltpu.SemaphoreType.DMA((2,))],
                    )(*in_hbm(fine_rays, coarse_rays), *waits)
                    got["rays"].append(swap(value, "view", groups, bits))
            for index, bit in enumerate(far_bits + [2]):
                if SOURCE["weights"][min(index, 2)] != stage:
                    continue
                if index == 0:
                    packed = call(
                        pair_kernel,
                        "pair",
                        shaped((2, PACK, width), BF16),
                        [VMEM] * 2 + [ANY] * len(waits),
                    )(mine, along_slab(theirs, 1), *waits)
                else:
                    packed, hop = got["weights"]
                    packed = call(
                        join_blocks_kernel,
                        "join_blocks",
                        shaped((2 * packed.shape[0], PACK, width), BF16),
                        [VMEM] * 2 + [ANY] * len(waits),
                    )(packed, hop, *waits)
                got["w%d" % index] = [along_slab(packed, bit)]
                got["weights"] = (packed, got["w%d" % index][0])

        def waits_of(stage):
            found = []
            for name, where in AWAITED.items():
                if where == stage:
                    found += got.get(name, [])
            return found

        begin("start", None)
        waits = waits_of("core")
        q, mixed = call(
            join_core_kernel,
            "join_core",
            (shaped((rows_half, total), F32), shaped((rows_half + height, total), BF16)),
            [VMEM] * 3 + [ANY] * len(waits),
        )(q, along_slab(short, 1), rows, *waits)
        begin("core", mixed)
        for index, bit in enumerate([2] + far_bits):
            last = index == len(far_bits)
            name = "last" if last else "hop%d" % index
            waits = waits_of(name)
            inputs = (q, mixed, along_slab(mixed, bit), *waits)
            specs = [VMEM] * 3 + [ANY] * len(waits)
            size = 2 * mixed.shape[0]
            if last:
                mixed = call(join_last_kernel, "join_last", shaped((size, total), BF16), specs)(
                    *inputs
                )
            else:
                q, mixed = call(
                    join_hop_kernel,
                    "join_hop",
                    (shaped(q.shape, F32), shaped((size - rows_half, total), BF16)),
                    specs,
                )(*inputs)
            begin(name, mixed)
        waits = waits_of("views")
        q, rows = call(
            functools.partial(join_views_kernel, rows_half),
            "join_views",
            (
                shaped((groups, rows_half, total), F32),
                shaped((groups, mixed.shape[0] - 2 * rows_half, total), BF16),
            ),
            [VMEM] * groups + [ANY] * len(waits),
        )(*to_views(mixed), *waits)
        count = len(far_bits)
        order = tuple(
            (j & 1) + 2 * (j >> 2) + (((j >> 1) & 1) << (count + 1)) for j in range(slabs)
        )
        waits = waits_of("rows")
        coarse_depth, fine_depth, coarse_turned, fine_turned, weights, q = call(
            functools.partial(rows_kernel, own, fz, [2] + far_bits),
            "unpack_rows",
            (
                shaped((groups, slabs * PACK, span), BF16),
                shaped((groups, slabs * fz, span), BF16),
                shaped((groups, views, det, slabs * PACK), BF16),
                shaped((groups, views, det, slabs * fz), BF16),
                shaped((groups, det, total), F32),
                shaped((groups, det, total), F32),
            ),
            [VMEM] * 4 + [ANY] * len(waits),
        )(rows, along_slab(rows, 1), q, along_slab(q, 1), *waits)
        spreads = call(
            functools.partial(spread_kernel, views),
            "spread",
            (
                shaped((groups, slabs * fz, total), BF16),
                shaped((groups, slabs * PACK, total), BF16),
            ),
            [VMEM] * 4,
        )(q, weights, fine_depth, coarse_depth)
        coarse_weights, fine_weights = call(
            functools.partial(weights_kernel, fz, order),
            "unpack_weights",
            (shaped((slabs * PACK, share), BF16), shaped((slabs * fz, share), BF16)),
            [VMEM] * 2 + [ANY] * len(spreads),
        )(*got["weights"], *spreads)
        rays = [own_rays] + got["rays"]
        held = (fine_turned, coarse_turned, coarse_weights, fine_weights, *rays)
        def add(mine, received, bit):
            return call(
                functools.partial(add_kernel, bit),
                "add",
                shaped((groups, rows_half, total), BF16),
                [VMEM] * 2,
            )(mine, received)

        deltas = []
        for ready, inputs in ((True, spreads), (False, None)):
            if not ready:
                inputs = (q, *deltas, weights, fine_depth, coarse_depth)
            delta, given = call(
                functools.partial(step_kernel, groups, views, ready),
                "ray_space_step",
                (shaped((groups, rows_half, total), BF16),) * 2,
                [VMEM] * (len(inputs) + len(held)),
                [pltpu.VMEM((groups, det, total), F32)],
            )(*inputs, *held)
            delta = add(delta, along_slab(given, 1), 0)
            for bit in view_bits:
                delta = add(delta, swap(delta, "view", groups, bit), bit)
            deltas += [delta, along_slab(delta, 1)]
        inputs = (q, *deltas, weights, fine_depth, coarse_depth, *rays)
        ours, theirs = call(
            functools.partial(tail_kernel, fz, groups, views),
            "back_projection",
            (shaped((PACK, width), BF16),) * 2,
            [VMEM] * len(inputs),
        )(*inputs)
        keep = call(keep_kernel, "keep", shaped((1, cells), F32), [SMEM])(margin_blocks)
        both = ("slab", "view")
        pieces = [ours] + [swap(ours, "view", groups, bits) for bits in range(1, groups)]
        pieces += [swap(theirs, both, slabs * groups, groups | bits) for bits in range(groups)]
        return call(
            functools.partial(final_kernel, groups, share),
            "update",
            (shaped(fine_volume.shape, F32), shaped(coarse_volume.shape, F32)),
            [VMEM] * (2 * groups + 5),
        )(
            *pieces,
            fine_volume,
            coarse_volume,
            fine_cell_weight,
            coarse_cell_weight,
            keep,
        )

    return body


def solution(mesh):
    return jax.shard_map(
        make_body(mesh.shape["slab"], mesh.shape["view"]),
        mesh=mesh,
        in_specs=(
            P("slab", None),
            P("slab", None),
            P("view", None, None),
            P("view", None, None),
            P("view", "slab", None),
            P("view", "slab", None),
            P("slab", "view", None),
            P("slab", "view", None),
            P("slab", None),
            P("slab", None),
            P("slab", None),
            P("view", "slab", None),
        ),
        out_specs=(P("slab", None), P("slab", None)),
        check_vma=False,
    )
```

```python
import functools
import jax
import jax.numpy as jnp
from jax import lax
from jax.experimental import pallas as pl
from jax.experimental.pallas import tpu as pltpu
from jax.sharding import PartitionSpec as P

BLOCK = 128
LANES = 128
PACK = 16
F32 = jnp.float32
BF16 = jnp.bfloat16
PARAMS = pltpu.CompilerParams(vmem_limit_bytes=24 * 1024 * 1024)
VMEM = pl.BlockSpec(memory_space=pltpu.VMEM)
SMEM = pl.BlockSpec(memory_space=pltpu.SMEM)
ANY = pl.BlockSpec(memory_space=pl.ANY)
HBM = pl.BlockSpec(memory_space=pltpu.HBM)
SOURCE = {'rays': 'start', 'weights': ("start", "core", "hop1")}
AWAITED = {"rays": "views", "w1": "last"}
QUICK = pl.CostEstimate(flops=1, bytes_accessed=1, transcendentals=0)


def fetch(source, target, sem):
    copy = pltpu.make_async_copy(source, target, sem)
    copy.start()
    return copy


def in_hbm(*arrays):
    return [pltpu.with_memory_space_constraint(a, pltpu.HBM) for a in arrays]


def scratch_like(*arrays):
    return [pltpu.VMEM(a.shape, a.dtype) for a in arrays]


def shaped(shape, dtype):
    return jax.ShapeDtypeStruct(shape, dtype)


def call(kernel, name, out_shape, in_specs, scratch=()):
    many = isinstance(out_shape, tuple)
    return pl.pallas_call(
        kernel,
        out_shape=out_shape,
        in_specs=in_specs,
        out_specs=(VMEM,) * len(out_shape) if many else VMEM,
        scratch_shapes=list(scratch),
        compiler_params=PARAMS,
        cost_estimate=QUICK,
        name=name,
    )


def swap(value, axis, size, bits):
    return lax.ppermute(value, axis, [(i, i ^ bits) for i in range(size)])


def dot(a, b, dims):
    return lax.dot_general(a, b, (dims, ((), ())), preferred_element_type=F32)


def in_two(value):
    high = value.astype(BF16)
    return high, (value - high.astype(F32)).astype(BF16)


def keep_row(blocks_ref, start, width):
    ids = (lax.broadcasted_iota(jnp.int32, (1, width), 1) + start) // BLOCK
    keep = jnp.ones((1, width), F32)
    for k in range(blocks_ref.shape[1]):
        keep = jnp.where(ids == blocks_ref[0, k], 0.0, keep)
    return keep


def share_start(cells, groups, bits=0):
    core = lax.axis_index("slab") % 2
    share = cells // 2 // groups
    return pl.multiple_of(core * (cells // 2) + (lax.axis_index("view") ^ bits) * share, LANES)


def packed_tiles(cells, fz):
    parts = PACK // fz
    return -(-(cells // LANES) // parts)


def pack_fine(rows):
    fz, size = rows.shape
    parts = PACK // fz
    empty = jnp.zeros((1, LANES), rows.dtype)
    columns = []
    for c in range(packed_tiles(size, fz)):
        pieces = []
        for i in range(fz):
            for k in range(parts):
                t = c * parts + k
                inside = t * LANES < size
                pieces.append(rows[i : i + 1, t * LANES : (t + 1) * LANES] if inside else empty)
        columns.append(jnp.concatenate(pieces, axis=0))
    return jnp.concatenate(columns, axis=1)


def unpack_fine(packed, fz, size):
    parts = PACK // fz
    rows = []
    for i in range(fz):
        pieces = []
        for t in range(size // LANES):
            row, column = i * parts + t % parts, t // parts * LANES
            pieces.append(packed[row : row + 1, column : column + LANES])
        rows.append(jnp.concatenate(pieces, axis=1))
    return jnp.concatenate(rows, axis=0)


def hit_depths(axial, hits):
    views, _, det = axial.shape
    tiles = hits.shape[2]
    tile = lax.broadcasted_iota(jnp.int32, (1, det), 1) // (det // tiles)
    result = []
    for v in range(views):
        hit = jnp.zeros((1, det), F32)
        for t in range(tiles):
            hit = jnp.where(tile == t, hits[v, 0, t].astype(F32), hit)
        result.append(axial[v].astype(F32) * hit)
    return result


def take_kernel(groups, bits, fine_rays, coarse_rays, *refs):
    out, sems = refs[-2:]
    cells = pl.ds(share_start(fine_rays.shape[1], groups, bits), out.shape[2])
    copies = [
        fetch(rays.at[:, cells, :], out.at[part], sems.at[part])
        for part, rays in enumerate((fine_rays, coarse_rays))
    ]
    for copy in copies:
        copy.wait()


def pair_kernel(mine, received, *refs):
    out = refs[-1]
    lead = lax.axis_index("slab") % 2 == 0
    own, other = mine[...].astype(F32), received[...].astype(F32)
    out[0] = jnp.where(lead, own, other).astype(BF16)
    out[1] = jnp.where(lead, other, own).astype(BF16)


def join_blocks_kernel(mine, received, *refs):
    out = refs[-1]
    out[: mine.shape[0]] = mine[...]
    out[mine.shape[0] :] = received[...]


def join_core_kernel(q, received, rows, *refs):
    total, out = refs[-2:]
    count = q.shape[0]
    value = q[...] + received[...].astype(F32)
    total[...] = value
    out[:count] = value.astype(BF16)
    out[count:] = rows[...]


def join_hop_kernel(q, mine, received, *refs):
    total, out = refs[-2:]
    count = q.shape[0]
    value = q[...] + received[:count].astype(F32)
    total[...] = value
    out[:count] = value.astype(BF16)
    held = mine.shape[0] - count
    out[count : count + held] = mine[count:]
    out[count + held :] = received[count:]


def join_last_kernel(q, mine, received, *refs):
    out = refs[-1]
    count = q.shape[0]
    out[:count], out[count : 2 * count] = in_two(q[...] + received[:count].astype(F32))
    held = mine.shape[0] - count
    out[2 * count : 2 * count + held] = mine[count:]
    out[2 * count + held :] = received[count:]


def join_views_kernel(count, *refs):
    q, rows = refs[-2:]
    for g in range(q.shape[0]):
        part = refs[g]
        q[g] = part[:count].astype(F32) + part[count : 2 * count].astype(F32)
        rows[g] = part[2 * count :]


def start_kernel(
    fine_rays,
    coarse_rays,
    fine_in,
    coarse_in,
    fine_weight_in,
    coarse_weight_in,
    fine_axial,
    coarse_axial_in,
    measured_in,
    ray_weight_in,
    blocks_in,
    hits_in,
    mine,
    theirs,
    rows,
    out,
    short,
    own_rays,
    fine,
    coarse,
    fine_weight,
    coarse_weight,
    coarse_axial,
    measured,
    ray_weight,
    blocks,
    hits,
    scratch,
    sems,
    chunk_sems,
):
    me = lax.axis_index("slab")
    core = me % 2
    fz, cells = fine.shape
    half = cells // 2
    sources = (
        (coarse_axial_in, coarse_axial),
        (ray_weight_in, ray_weight),
        (measured_in, measured),
        (blocks_in, blocks),
        (hits_in, hits),
        (fine_weight_in, fine_weight),
        (coarse_weight_in, coarse_weight),
    )
    others = [fetch(a, b, sems.at[i]) for i, (a, b) in enumerate(sources)]
    steps = chunk_sems.shape[0]
    chunk = cells // steps
    copies = []
    for i in range(steps):
        part = pl.ds(i * chunk, chunk)
        copies.append(
            [
                fetch(fine_in.at[:, part], fine.at[:, part], chunk_sems.at[i, 0]),
                fetch(coarse_in.at[:, part], coarse.at[:, part], chunk_sems.at[i, 1]),
            ]
        )
    share = own_rays.shape[2]
    groups = half // share
    held = pl.ds(share_start(cells, groups), share)
    outgoing = [
        fetch(fine_rays.at[:, held, :], own_rays.at[0], sems.at[8]),
        fetch(coarse_rays.at[:, held, :], own_rays.at[1], sems.at[9]),
    ]
    for copy in others:
        copy.wait()

    views, _, det = fine_axial.shape
    columns = ray_weight.shape[2]
    total = views * columns
    span = views * det
    own = ray_weight.shape[0]
    coarse_depth = hit_depths(coarse_axial, hits)
    fine_depth = hit_depths(fine_axial, hits)
    wide = max(span, total)
    weight = jnp.concatenate([ray_weight[:, v, :] for v in range(views)], axis=1)
    fine_wide = jnp.concatenate(fine_depth, axis=1)
    if wide > total:
        weight = jnp.concatenate([weight, jnp.zeros((own, wide - total), F32)], axis=1)
    if wide > span:
        fine_wide = jnp.concatenate([fine_wide, jnp.zeros((fz, wide - span), F32)], axis=1)
    stack = [weight, fine_wide]
    if own + fz < PACK:
        stack.append(jnp.zeros((PACK - own - fz, wide), F32))
    packed = jnp.concatenate(coarse_depth + [jnp.concatenate(stack, axis=0)], axis=1).astype(BF16)
    for p in range((span + wide) // total):
        rows[p * PACK : (p + 1) * PACK] = packed[:, p * total : (p + 1) * total]

    for target, side in ((mine, core), (theirs, 1 - core)):
        begin = pl.multiple_of(side * half + lax.axis_index("view") * share, LANES)
        keep = keep_row(blocks, begin, share)
        target[:, :share] = (coarse_weight[:, pl.ds(begin, share)] * keep).astype(BF16)
        target[:, share:] = pack_fine(fine_weight[:, pl.ds(begin, share)]).astype(BF16)

    fine_sum = coarse_sum = None
    for i in range(steps):
        part = slice(i * chunk, (i + 1) * chunk)
        for copy in copies[i]:
            copy.wait()
        keep = keep_row(blocks, i * chunk, chunk)
        fine_rows = fine[:, part].astype(BF16)
        coarse_rows = (coarse[:, part] * keep).astype(BF16)
        fine_wide = jnp.concatenate([fine_rays[v, part, :] for v in range(views)], axis=1)
        coarse_wide = jnp.concatenate([coarse_rays[v, part, :] for v in range(views)], axis=1)
        fine_part = dot(fine_rows, fine_wide, ((1,), (0,)))
        coarse_part = dot(coarse_rows, coarse_wide, ((1,), (0,)))
        fine_sum = fine_part if fine_sum is None else fine_sum + fine_part
        coarse_sum = coarse_part if coarse_sum is None else coarse_sum + coarse_part
    pad = jnp.zeros((PACK - fz, total), F32)
    moment = jnp.concatenate([coarse_sum, fine_sum, pad], axis=0).astype(BF16)
    pad = jnp.zeros((PACK - fz, det), F32)
    row = lax.broadcasted_iota(jnp.int32, (det, columns), 0) - me * own
    for v in range(views):
        depth = jnp.concatenate([coarse_depth[v], fine_depth[v], pad], axis=0).astype(BF16)
        where = slice(v * columns, (v + 1) * columns)
        projection = dot(depth, moment[:, where], ((0,), (0,)))
        given = jnp.zeros((det, columns), F32)
        for i in range(own):
            given = jnp.where(row == i, measured[i : i + 1, v, :], given)
        scratch[:, where] = given - projection
    kept = pl.ds(pl.multiple_of(core * (det // 2), PACK), det // 2)
    sent = pl.ds(pl.multiple_of((1 - core) * (det // 2), PACK), det // 2)
    out[...] = scratch[kept, :]
    short[...] = scratch[sent, :].astype(BF16)
    for copy in outgoing:
        copy.wait()


def slab_of(block, bits):
    me = lax.axis_index("slab")
    apart = jnp.zeros_like(block)
    for place, bit in enumerate(bits):
        apart = apart + ((block >> (place + 1)) & 1) * bit
    return ((me - me % 2) ^ apart) + (block & 1)


def turn_kernel(fine, coarse, fine_out, coarse_out):
    det = fine_out.shape[2]
    for source, out in ((fine, fine_out), (coarse, coarse_out)):
        for g in range(out.shape[0]):
            wide = source[g].astype(F32)
            for v in range(out.shape[1]):
                out[g, v] = wide[:, v * det : (v + 1) * det].T.astype(BF16)


def rows_kernel(own, fz, bits, mine, theirs, q_mine, q_theirs, *refs):
    coarse_out, fine_out, out, q_out = refs[-4:]
    lead = lax.axis_index("slab") % 2 == 0
    kept = q_mine.shape[1]
    for g in range(q_mine.shape[0]):
        ours, others = q_mine[g], q_theirs[g]
        q_out[g, :kept] = jnp.where(lead, ours, others)
        q_out[g, kept:] = jnp.where(lead, others, ours)
    groups, held, total = mine.shape
    slabs = coarse_out.shape[1] // PACK
    height = 2 * held // slabs
    pieces = height // PACK
    det = out.shape[1]
    count = slabs * PACK
    shape = (slabs * own, count)
    w = lax.broadcasted_iota(jnp.int32, shape, 0)
    column = lax.broadcasted_iota(jnp.int32, shape, 1)
    block, row = column // PACK, column % PACK
    match = (row < own) & (w == slab_of(block, bits) * own + row)
    to_weight = jnp.where(match, 1.0, 0.0).astype(BF16)
    shape = (slabs * fz, count)
    z = lax.broadcasted_iota(jnp.int32, shape, 0)
    column = lax.broadcasted_iota(jnp.int32, shape, 1)
    to_fine = jnp.where(column == (z // fz) * PACK + own + z % fz, 1.0, 0.0).astype(BF16)
    for g in range(groups):
        own_rows, other_rows = mine[g].astype(F32), theirs[g].astype(F32)
        even = jnp.where(lead, own_rows, other_rows).astype(BF16)
        odd = jnp.where(lead, other_rows, own_rows).astype(BF16)
        cuts = []
        for p in range(pieces):
            blocks = [
                (even, odd)[j % 2][(j // 2) * height + p * PACK :][:PACK] for j in range(slabs)
            ]
            cuts.append(jnp.concatenate(blocks, axis=0))
        coarse = jnp.concatenate(cuts[: pieces // 2], axis=1)
        side = jnp.concatenate(cuts[pieces // 2 :], axis=1)
        fine = dot(to_fine, side, ((1,), (0,)))
        coarse_out[g] = coarse
        fine_out[g] = fine.astype(BF16)
        out[g] = dot(to_weight, side, ((1,), (0,)))[:, :total]


def weights_kernel(fz, order, mine, received, *refs):
    coarse_out, fine_out = refs[-2:]
    held = mine.shape[0]
    slabs = 2 * held
    count = slabs * PACK
    parts = PACK // fz
    size = fine_out.shape[1]
    tiles = packed_tiles(size, fz)
    blocks = [(mine, received)[k // held].at[k % held] for k in order]
    for j, block in enumerate(blocks):
        coarse_out[j * PACK : (j + 1) * PACK] = block[:, :size]
    source = jnp.concatenate([block[:, size : size + tiles * LANES] for block in blocks], axis=0)
    shape = (slabs * fz, count)
    z = lax.broadcasted_iota(jnp.int32, shape, 0)
    column = lax.broadcasted_iota(jnp.int32, shape, 1)
    for k in range(parts):
        choose = jnp.where(column == (z // fz) * PACK + (z % fz) * parts + k, 1.0, 0.0)
        chosen = dot(choose.astype(BF16), source, ((1,), (0,)))
        for c in range(tiles):
            t = c * parts + k
            if t * LANES < size:
                fine_out[:, t * LANES : (t + 1) * LANES] = chosen[
                    :, c * LANES : (c + 1) * LANES
                ].astype(BF16)


def whole_rows(mine, received):
    lead = lax.axis_index("slab") % 2 == 0
    ours, others = mine.astype(F32), received.astype(F32)
    return jnp.concatenate(
        [jnp.where(lead, ours, others), jnp.where(lead, others, ours)], axis=0
    )


def residuals(q, deltas, weights):
    groups = q.shape[0]
    current = [q[g] for g in range(groups)]
    results = [[weights[g] * current[g] for g in range(groups)]]
    for mine, received in deltas:
        current = [current[g] - whole_rows(mine[g], received[g]) for g in range(groups)]
        results.append([weights[g] * current[g] for g in range(groups)])
    return results


def spread(depth, residual, views):
    det, columns = residual.shape[0], residual.shape[1] // views
    pieces = [
        dot(
            depth[:, v * det : (v + 1) * det],
            residual[:, v * columns : (v + 1) * columns],
            ((1,), (0,)),
        )
        for v in range(views)
    ]
    return jnp.concatenate(pieces, axis=1)


def spread_kernel(views, q, weights, fine_depth, coarse_depth, fine_out, coarse_out):
    for g in range(q.shape[0]):
        residual = (weights[g] * q[g]).astype(BF16)
        fine_out[g] = spread(fine_depth[g], residual, views).astype(BF16)
        coarse_out[g] = spread(coarse_depth[g], residual, views).astype(BF16)


def group_rays(held, part, g, cut):
    return jnp.concatenate([held[g][part, v, cut, :] for v in range(held[g].shape[1])], axis=1)


def step_kernel(groups, views, ready, *refs):
    refs = list(refs)
    if ready:
        spreads = [refs.pop(0), refs.pop(0)]
    else:
        q, mine, received, weights, fine_depth, coarse_depth = refs[:6]
        refs = refs[6:]
        residual = residuals(q, [(mine, received)], weights)[-1]
        residual = [r.astype(BF16) for r in residual]
        spreads = [
            [spread(depth[g], residual[g], views).astype(BF16) for g in range(groups)]
            for depth in (fine_depth, coarse_depth)
        ]
    turned = refs[:2]
    coarse_weights, fine_weights = refs[2:4]
    held = refs[4:-3]
    kept, given, scratch = refs[-3:]
    size = fine_weights.shape[1]
    columns = held[0].shape[3]
    chunk = min(size, 1024)
    results = [None] * groups
    for part in range(2):
        moments = [None] * groups
        for c in range(size // chunk):
            cut = slice(c * chunk, (c + 1) * chunk)
            if part == 0:
                weight = fine_weights[:, cut]
            else:
                weight = coarse_weights[:, cut]
            rays = [group_rays(held, part, g, cut) for g in range(groups)]
            back = dot(spreads[part][0], rays[0], ((1,), (1,)))
            for g in range(1, groups):
                back = back + dot(spreads[part][g], rays[g], ((1,), (1,)))
            change = (weight.astype(F32) * back).astype(BF16)
            for g in range(groups):
                moment = dot(change, rays[g], ((1,), (0,)))
                moments[g] = moment if moments[g] is None else moments[g] + moment
        for g in range(groups):
            moment = moments[g].astype(BF16)
            pieces = [
                dot(turned[part][g, v], moment[:, v * columns : (v + 1) * columns], ((1,), (0,)))
                for v in range(views)
            ]
            value = jnp.concatenate(pieces, axis=1)
            results[g] = value if results[g] is None else results[g] + value
    core = lax.axis_index("slab") % 2
    rows = kept.shape[1]
    for g in range(groups):
        scratch[g] = results[g]
        kept[g] = scratch[g, pl.ds(pl.multiple_of(core * rows, PACK), rows), :].astype(BF16)
        given[g] = scratch[g, pl.ds(pl.multiple_of((1 - core) * rows, PACK), rows), :].astype(BF16)


def add_kernel(bit, mine, received, out):
    for g in range(mine.shape[0]):
        out[g] = (mine[g].astype(F32) + received[g ^ bit].astype(F32)).astype(BF16)


def tail_kernel(fz, groups, views, q, *refs):
    deltas = [refs[:2], refs[2:4]]
    weights, fine_depth, coarse_depth = refs[4:7]
    held = refs[7:-2]
    ours, theirs = refs[-2:]
    size = held[0].shape[2]
    chunk = min(size, 1024)
    lead = lax.axis_index("slab") % 2 == 0
    history = residuals(q, deltas, weights)
    rows = (fz, PACK)
    spreads = ([], [])
    for g in range(groups):
        value = history[0][g]
        for other in history[1:]:
            value = value + other[g]
        high, low = in_two(value)
        fine_rows = fine_depth[g, : 2 * PACK].astype(F32)[: 2 * fz].astype(BF16)
        for part, depth in enumerate((fine_rows, coarse_depth[g, : 2 * PACK])):
            pair = in_two(spread(depth, high, views) + spread(depth, low, views))
            spreads[part].append(jnp.concatenate(pair, axis=0))
    backs = ([], [])
    for part in range(2):
        for c in range(size // chunk):
            cut = slice(c * chunk, (c + 1) * chunk)
            back = None
            for g in range(groups):
                value = dot(spreads[part][g], group_rays(held, part, g, cut), ((1,), (1,)))
                back = value if back is None else back + value
            backs[part].append(back[: 2 * rows[part]] + back[2 * rows[part] :])
    for out, first in ((ours, lead), (theirs, jnp.logical_not(lead))):
        parts = []
        for part in range(2):
            back = jnp.concatenate(backs[part], axis=1)
            parts.append(jnp.where(first, back[: rows[part]], back[rows[part] :]))
        out[:, :size] = parts[1].astype(BF16)
        out[:, size:] = pack_fine(parts[0]).astype(BF16)


def keep_kernel(blocks, out):
    out[...] = keep_row(blocks, 0, out.shape[1])


def final_kernel(groups, size, *refs):
    pieces = refs[: 2 * groups]
    fine, coarse, fw, cw, keep, fine_out, coarse_out = refs[2 * groups :]
    core = lax.axis_index("slab") % 2
    view = lax.axis_index("view")
    fz, cells = fine.shape
    for index, piece in enumerate(pieces):
        side = core if index < groups else 1 - core
        start = side * (cells // 2) + (view ^ (index % groups)) * size
        start = pl.multiple_of(start, LANES)
        where = pl.ds(start, size)
        change = piece[:, :size].astype(F32)
        coarse_out[:, where] = (coarse[:, where] + cw[:, where] * change) * keep[:, where]
        change = unpack_fine(piece[:, size:].astype(F32), fz, size)
        fine_out[:, where] = fine[:, where] + fw[:, where] * change


def make_body(slabs, groups):
    far_bits = [1 << k for k in range(slabs.bit_length() - 2, 1, -1)]
    view_bits = [1 << k for k in range(groups.bit_length() - 1)]

    def along_slab(value, bit):
        return swap(value, "slab", slabs, bit)

    def body(
        fine_volume,
        coarse_volume,
        fine_rays,
        coarse_rays,
        fine_axial,
        coarse_axial,
        measured,
        ray_weight,
        fine_cell_weight,
        coarse_cell_weight,
        margin_blocks,
        ray_hits,
    ):
        views, cells, columns = fine_rays.shape
        det = fine_axial.shape[2]
        fz, cz = fine_volume.shape[0], coarse_volume.shape[0]
        own = measured.shape[0]
        total = views * columns
        span = max(views * det, total)
        share = cells // 2 // groups
        lead = lax.axis_index("slab") % 2 == 0
        width = share + packed_tiles(share, fz) * LANES

        taken = in_hbm(
            fine_volume,
            coarse_volume,
            fine_cell_weight,
            coarse_cell_weight,
            coarse_axial,
            measured,
            ray_weight,
        )
        height = PACK * ((views * det + span) // total)
        mine, theirs, rows, q, short, own_rays = call(
            start_kernel,
            "start",
            (
                shaped((PACK, width), BF16),
                shaped((PACK, width), BF16),
                shaped((height, total), BF16),
                shaped((det // 2, total), F32),
                shaped((det // 2, total), BF16),
                shaped((2, views, share, columns), BF16),
            ),
            [VMEM] * 2 + [HBM] * 4 + [VMEM] + [HBM] * 5,
            scratch_like(*taken)
            + [
                pltpu.SMEM(margin_blocks.shape, jnp.int32),
                pltpu.SMEM(ray_hits.shape, jnp.int32),
                pltpu.VMEM((det, total), F32),
                pltpu.SemaphoreType.DMA((10,)),
                pltpu.SemaphoreType.DMA((4, 4)),
            ],
        )(
            fine_rays,
            coarse_rays,
            *taken[:4],
            fine_axial,
            *taken[4:],
            *in_hbm(margin_blocks, ray_hits),
        )

        def to_views(value):
            values = [value]
            for bit in view_bits:
                values += [swap(one, "view", groups, bit) for one in values]
            return values

        rows_half = det // 2
        got = {}

        def begin(stage, token):
            waits = [] if token is None else [token]
            if SOURCE["rays"] == stage:
                got["rays"] = []
                for bits in range(1, groups):
                    value = call(
                        functools.partial(take_kernel, groups, bits),
                        "take_rays",
                        shaped((2, views, share, columns), BF16),
                        [HBM] * 2 + [ANY] * len(waits),
                        [pltpu.SemaphoreType.DMA((2,))],
                    )(*in_hbm(fine_rays, coarse_rays), *waits)
                    got["rays"].append(swap(value, "view", groups, bits))
            for index, bit in enumerate(far_bits + [2]):
                if SOURCE["weights"][min(index, 2)] != stage:
                    continue
                if index == 0:
                    packed = call(
                        pair_kernel,
                        "pair",
                        shaped((2, PACK, width), BF16),
                        [VMEM] * 2 + [ANY] * len(waits),
                    )(mine, along_slab(theirs, 1), *waits)
                else:
                    packed, hop = got["weights"]
                    packed = call(
                        join_blocks_kernel,
                        "join_blocks",
                        shaped((2 * packed.shape[0], PACK, width), BF16),
                        [VMEM] * 2 + [ANY] * len(waits),
                    )(packed, hop, *waits)
                got["w%d" % index] = [along_slab(packed, bit)]
                got["weights"] = (packed, got["w%d" % index][0])

        def waits_of(stage):
            found = []
            for name, where in AWAITED.items():
                if where == stage:
                    found += got.get(name, [])
            return found

        begin("start", None)
        waits = waits_of("core")
        q, mixed = call(
            join_core_kernel,
            "join_core",
            (shaped((rows_half, total), F32), shaped((rows_half + height, total), BF16)),
            [VMEM] * 3 + [ANY] * len(waits),
        )(q, along_slab(short, 1), rows, *waits)
        begin("core", mixed)
        for index, bit in enumerate([2] + far_bits):
            last = index == len(far_bits)
            name = "last" if last else "hop%d" % index
            waits = waits_of(name)
            inputs = (q, mixed, along_slab(mixed, bit), *waits)
            specs = [VMEM] * 3 + [ANY] * len(waits)
            size = 2 * mixed.shape[0]
            if last:
                mixed = call(join_last_kernel, "join_last", shaped((size, total), BF16), specs)(
                    *inputs
                )
            else:
                q, mixed = call(
                    join_hop_kernel,
                    "join_hop",
                    (shaped(q.shape, F32), shaped((size - rows_half, total), BF16)),
                    specs,
                )(*inputs)
            begin(name, mixed)
        waits = waits_of("views")
        q, rows = call(
            functools.partial(join_views_kernel, rows_half),
            "join_views",
            (
                shaped((groups, rows_half, total), F32),
                shaped((groups, mixed.shape[0] - 2 * rows_half, total), BF16),
            ),
            [VMEM] * groups + [ANY] * len(waits),
        )(*to_views(mixed), *waits)
        count = len(far_bits)
        order = tuple(
            (j & 1) + 2 * (j >> 2) + (((j >> 1) & 1) << (count + 1)) for j in range(slabs)
        )
        waits = waits_of("rows")
        coarse_depth, fine_depth, weights, q = call(
            functools.partial(rows_kernel, own, fz, [2] + far_bits),
            "unpack_rows",
            (
                shaped((groups, slabs * PACK, span), BF16),
                shaped((groups, slabs * fz, span), BF16),
                shaped((groups, det, total), F32),
                shaped((groups, det, total), F32),
            ),
            [VMEM] * 4 + [ANY] * len(waits),
        )(rows, along_slab(rows, 1), q, along_slab(q, 1), *waits)
        spreads = call(
            functools.partial(spread_kernel, views),
            "spread",
            (
                shaped((groups, slabs * fz, total), BF16),
                shaped((groups, slabs * PACK, total), BF16),
            ),
            [VMEM] * 4,
        )(q, weights, fine_depth, coarse_depth)
        fine_turned, coarse_turned = call(
            turn_kernel,
            "turn",
            (
                shaped((groups, views, det, slabs * fz), BF16),
                shaped((groups, views, det, slabs * PACK), BF16),
            ),
            [VMEM] * 2,
        )(fine_depth, coarse_depth)
        coarse_weights, fine_weights = call(
            functools.partial(weights_kernel, fz, order),
            "unpack_weights",
            (shaped((slabs * PACK, share), BF16), shaped((slabs * fz, share), BF16)),
            [VMEM] * 2 + [ANY] * 2,
        )(*got["weights"], *spreads)
        rays = [own_rays] + got["rays"]
        held = (fine_turned, coarse_turned, coarse_weights, fine_weights, *rays)
        def add(mine, received, bit):
            return call(
                functools.partial(add_kernel, bit),
                "add",
                shaped((groups, rows_half, total), BF16),
                [VMEM] * 2,
            )(mine, received)

        deltas = []
        for ready, inputs in ((True, spreads), (False, None)):
            if not ready:
                inputs = (q, *deltas, weights, fine_depth, coarse_depth)
            delta, given = call(
                functools.partial(step_kernel, groups, views, ready),
                "ray_space_step",
                (shaped((groups, rows_half, total), BF16),) * 2,
                [VMEM] * (len(inputs) + len(held)),
                [pltpu.VMEM((groups, det, total), F32)],
            )(*inputs, *held)
            delta = add(delta, along_slab(given, 1), 0)
            for bit in view_bits:
                delta = add(delta, swap(delta, "view", groups, bit), bit)
            deltas += [delta, along_slab(delta, 1)]
        inputs = (q, *deltas, weights, fine_depth, coarse_depth, *rays)
        ours, theirs = call(
            functools.partial(tail_kernel, fz, groups, views),
            "back_projection",
            (shaped((PACK, width), BF16),) * 2,
            [VMEM] * len(inputs),
        )(*inputs)
        keep = call(keep_kernel, "keep", shaped((1, cells), F32), [SMEM])(margin_blocks)
        both = ("slab", "view")
        pieces = [ours] + [swap(ours, "view", groups, bits) for bits in range(1, groups)]
        pieces += [swap(theirs, both, slabs * groups, groups | bits) for bits in range(groups)]
        return call(
            functools.partial(final_kernel, groups, share),
            "update",
            (shaped(fine_volume.shape, F32), shaped(coarse_volume.shape, F32)),
            [VMEM] * (2 * groups + 5),
        )(
            *pieces,
            fine_volume,
            coarse_volume,
            fine_cell_weight,
            coarse_cell_weight,
            keep,
        )

    return body


def solution(mesh):
    return jax.shard_map(
        make_body(mesh.shape["slab"], mesh.shape["view"]),
        mesh=mesh,
        in_specs=(
            P("slab", None),
            P("slab", None),
            P("view", None, None),
            P("view", None, None),
            P("view", "slab", None),
            P("view", "slab", None),
            P("slab", "view", None),
            P("slab", "view", None),
            P("slab", None),
            P("slab", None),
            P("slab", None),
            P("view", "slab", None),
        ),
        out_specs=(P("slab", None), P("slab", None)),
        check_vma=False,
    )
```

```python
import functools
import jax
import jax.numpy as jnp
from jax import lax
from jax.experimental import pallas as pl
from jax.experimental.pallas import tpu as pltpu
from jax.sharding import PartitionSpec as P

BLOCK = 128
LANES = 128
PACK = 16
F32 = jnp.float32
BF16 = jnp.bfloat16
PARAMS = pltpu.CompilerParams(vmem_limit_bytes=24 * 1024 * 1024)
VMEM = pl.BlockSpec(memory_space=pltpu.VMEM)
SMEM = pl.BlockSpec(memory_space=pltpu.SMEM)
ANY = pl.BlockSpec(memory_space=pl.ANY)
HBM = pl.BlockSpec(memory_space=pltpu.HBM)
SOURCE = {'rays': 'start', 'weights': ("start", "core", "last")}
AWAITED = {"rays": "views", "w1": "last"}
QUICK = pl.CostEstimate(flops=1, bytes_accessed=1, transcendentals=0)


def fetch(source, target, sem):
    copy = pltpu.make_async_copy(source, target, sem)
    copy.start()
    return copy


def in_hbm(*arrays):
    return [pltpu.with_memory_space_constraint(a, pltpu.HBM) for a in arrays]


def scratch_like(*arrays):
    return [pltpu.VMEM(a.shape, a.dtype) for a in arrays]


def shaped(shape, dtype):
    return jax.ShapeDtypeStruct(shape, dtype)


def call(kernel, name, out_shape, in_specs, scratch=()):
    many = isinstance(out_shape, tuple)
    return pl.pallas_call(
        kernel,
        out_shape=out_shape,
        in_specs=in_specs,
        out_specs=(VMEM,) * len(out_shape) if many else VMEM,
        scratch_shapes=list(scratch),
        compiler_params=PARAMS,
        cost_estimate=QUICK,
        name=name,
    )


def swap(value, axis, size, bits):
    return lax.ppermute(value, axis, [(i, i ^ bits) for i in range(size)])


def dot(a, b, dims):
    return lax.dot_general(a, b, (dims, ((), ())), preferred_element_type=F32)


def in_two(value):
    high = value.astype(BF16)
    return high, (value - high.astype(F32)).astype(BF16)


def keep_row(blocks_ref, start, width):
    ids = (lax.broadcasted_iota(jnp.int32, (1, width), 1) + start) // BLOCK
    keep = jnp.ones((1, width), F32)
    for k in range(blocks_ref.shape[1]):
        keep = jnp.where(ids == blocks_ref[0, k], 0.0, keep)
    return keep


def share_start(cells, groups, bits=0):
    core = lax.axis_index("slab") % 2
    share = cells // 2 // groups
    return pl.multiple_of(core * (cells // 2) + (lax.axis_index("view") ^ bits) * share, LANES)


def packed_tiles(cells, fz):
    parts = PACK // fz
    return -(-(cells // LANES) // parts)


def pack_fine(rows):
    fz, size = rows.shape
    parts = PACK // fz
    empty = jnp.zeros((1, LANES), rows.dtype)
    columns = []
    for c in range(packed_tiles(size, fz)):
        pieces = []
        for i in range(fz):
            for k in range(parts):
                t = c * parts + k
                inside = t * LANES < size
                pieces.append(rows[i : i + 1, t * LANES : (t + 1) * LANES] if inside else empty)
        columns.append(jnp.concatenate(pieces, axis=0))
    return jnp.concatenate(columns, axis=1)


def unpack_fine(packed, fz, size):
    parts = PACK // fz
    rows = []
    for i in range(fz):
        pieces = []
        for t in range(size // LANES):
            row, column = i * parts + t % parts, t // parts * LANES
            pieces.append(packed[row : row + 1, column : column + LANES])
        rows.append(jnp.concatenate(pieces, axis=1))
    return jnp.concatenate(rows, axis=0)


def hit_depths(axial, hits):
    views, _, det = axial.shape
    tiles = hits.shape[2]
    tile = lax.broadcasted_iota(jnp.int32, (1, det), 1) // (det // tiles)
    result = []
    for v in range(views):
        hit = jnp.zeros((1, det), F32)
        for t in range(tiles):
            hit = jnp.where(tile == t, hits[v, 0, t].astype(F32), hit)
        result.append(axial[v].astype(F32) * hit)
    return result


def take_kernel(groups, bits, fine_rays, coarse_rays, *refs):
    out, sems = refs[-2:]
    cells = pl.ds(share_start(fine_rays.shape[1], groups, bits), out.shape[2])
    copies = [
        fetch(rays.at[:, cells, :], out.at[part], sems.at[part])
        for part, rays in enumerate((fine_rays, coarse_rays))
    ]
    for copy in copies:
        copy.wait()


def pair_kernel(mine, received, *refs):
    out = refs[-1]
    lead = lax.axis_index("slab") % 2 == 0
    own, other = mine[...].astype(F32), received[...].astype(F32)
    out[0] = jnp.where(lead, own, other).astype(BF16)
    out[1] = jnp.where(lead, other, own).astype(BF16)


def join_blocks_kernel(mine, received, *refs):
    out = refs[-1]
    out[: mine.shape[0]] = mine[...]
    out[mine.shape[0] :] = received[...]


def join_core_kernel(q, received, rows, *refs):
    total, out = refs[-2:]
    count = q.shape[0]
    value = q[...] + received[...].astype(F32)
    total[...] = value
    out[:count] = value.astype(BF16)
    out[count:] = rows[...]


def join_hop_kernel(q, mine, received, *refs):
    total, out = refs[-2:]
    count = q.shape[0]
    value = q[...] + received[:count].astype(F32)
    total[...] = value
    out[:count] = value.astype(BF16)
    held = mine.shape[0] - count
    out[count : count + held] = mine[count:]
    out[count + held :] = received[count:]


def join_last_kernel(q, mine, received, *refs):
    out = refs[-1]
    count = q.shape[0]
    out[:count], out[count : 2 * count] = in_two(q[...] + received[:count].astype(F32))
    held = mine.shape[0] - count
    out[2 * count : 2 * count + held] = mine[count:]
    out[2 * count + held :] = received[count:]


def join_views_kernel(count, *refs):
    q, rows = refs[-2:]
    for g in range(q.shape[0]):
        part = refs[g]
        q[g] = part[:count].astype(F32) + part[count : 2 * count].astype(F32)
        rows[g] = part[2 * count :]


def start_kernel(
    fine_rays_in,
    coarse_rays_in,
    fine_in,
    coarse_in,
    fine_weight_in,
    coarse_weight_in,
    fine_axial,
    coarse_axial_in,
    measured_in,
    ray_weight_in,
    blocks_in,
    hits_in,
    mine,
    theirs,
    rows,
    out,
    short,
    own_rays,
    fine_rays,
    coarse_rays,
    fine,
    coarse,
    fine_weight,
    coarse_weight,
    coarse_axial,
    measured,
    ray_weight,
    blocks,
    hits,
    scratch,
    sems,
    chunk_sems,
):
    me = lax.axis_index("slab")
    core = me % 2
    fz, cells = fine.shape
    half = cells // 2
    sources = (
        (coarse_axial_in, coarse_axial),
        (ray_weight_in, ray_weight),
        (measured_in, measured),
        (blocks_in, blocks),
        (hits_in, hits),
        (fine_weight_in, fine_weight),
        (coarse_weight_in, coarse_weight),
    )
    others = [fetch(a, b, sems.at[i]) for i, (a, b) in enumerate(sources)]
    steps = chunk_sems.shape[0]
    chunk = cells // steps
    copies = []
    for i in range(steps):
        part = pl.ds(i * chunk, chunk)
        copies.append(
            [
                fetch(fine_in.at[:, part], fine.at[:, part], chunk_sems.at[i, 0]),
                fetch(coarse_in.at[:, part], coarse.at[:, part], chunk_sems.at[i, 1]),
                fetch(fine_rays_in.at[:, part, :], fine_rays.at[:, part, :], chunk_sems.at[i, 2]),
                fetch(
                    coarse_rays_in.at[:, part, :], coarse_rays.at[:, part, :], chunk_sems.at[i, 3]
                ),
            ]
        )
    share = own_rays.shape[2]
    groups = half // share
    held = pl.ds(share_start(cells, groups), share)
    outgoing = [
        fetch(fine_rays_in.at[:, held, :], own_rays.at[0], sems.at[8]),
        fetch(coarse_rays_in.at[:, held, :], own_rays.at[1], sems.at[9]),
    ]
    for copy in others:
        copy.wait()

    views, _, det = fine_axial.shape
    columns = ray_weight.shape[2]
    total = views * columns
    span = views * det
    own = ray_weight.shape[0]
    coarse_depth = hit_depths(coarse_axial, hits)
    fine_depth = hit_depths(fine_axial, hits)
    wide = max(span, total)
    weight = jnp.concatenate([ray_weight[:, v, :] for v in range(views)], axis=1)
    fine_wide = jnp.concatenate(fine_depth, axis=1)
    if wide > total:
        weight = jnp.concatenate([weight, jnp.zeros((own, wide - total), F32)], axis=1)
    if wide > span:
        fine_wide = jnp.concatenate([fine_wide, jnp.zeros((fz, wide - span), F32)], axis=1)
    stack = [weight, fine_wide]
    if own + fz < PACK:
        stack.append(jnp.zeros((PACK - own - fz, wide), F32))
    packed = jnp.concatenate(coarse_depth + [jnp.concatenate(stack, axis=0)], axis=1).astype(BF16)
    for p in range((span + wide) // total):
        rows[p * PACK : (p + 1) * PACK] = packed[:, p * total : (p + 1) * total]

    for target, side in ((mine, core), (theirs, 1 - core)):
        begin = pl.multiple_of(side * half + lax.axis_index("view") * share, LANES)
        keep = keep_row(blocks, begin, share)
        target[:, :share] = (coarse_weight[:, pl.ds(begin, share)] * keep).astype(BF16)
        target[:, share:] = pack_fine(fine_weight[:, pl.ds(begin, share)]).astype(BF16)

    fine_sum = coarse_sum = None
    for i in range(steps):
        part = slice(i * chunk, (i + 1) * chunk)
        for copy in copies[i]:
            copy.wait()
        keep = keep_row(blocks, i * chunk, chunk)
        fine_rows = fine[:, part].astype(BF16)
        coarse_rows = (coarse[:, part] * keep).astype(BF16)
        fine_wide = jnp.concatenate([fine_rays[v, part, :] for v in range(views)], axis=1)
        coarse_wide = jnp.concatenate([coarse_rays[v, part, :] for v in range(views)], axis=1)
        fine_part = dot(fine_rows, fine_wide, ((1,), (0,)))
        coarse_part = dot(coarse_rows, coarse_wide, ((1,), (0,)))
        fine_sum = fine_part if fine_sum is None else fine_sum + fine_part
        coarse_sum = coarse_part if coarse_sum is None else coarse_sum + coarse_part
    pad = jnp.zeros((PACK - fz, total), F32)
    moment = jnp.concatenate([coarse_sum, fine_sum, pad], axis=0).astype(BF16)
    pad = jnp.zeros((PACK - fz, det), F32)
    row = lax.broadcasted_iota(jnp.int32, (det, columns), 0) - me * own
    for v in range(views):
        depth = jnp.concatenate([coarse_depth[v], fine_depth[v], pad], axis=0).astype(BF16)
        where = slice(v * columns, (v + 1) * columns)
        projection = dot(depth, moment[:, where], ((0,), (0,)))
        given = jnp.zeros((det, columns), F32)
        for i in range(own):
            given = jnp.where(row == i, measured[i : i + 1, v, :], given)
        scratch[:, where] = given - projection
    kept = pl.ds(pl.multiple_of(core * (det // 2), PACK), det // 2)
    sent = pl.ds(pl.multiple_of((1 - core) * (det // 2), PACK), det // 2)
    out[...] = scratch[kept, :]
    short[...] = scratch[sent, :].astype(BF16)
    for copy in outgoing:
        copy.wait()


def slab_of(block, bits):
    me = lax.axis_index("slab")
    apart = jnp.zeros_like(block)
    for place, bit in enumerate(bits):
        apart = apart + ((block >> (place + 1)) & 1) * bit
    return ((me - me % 2) ^ apart) + (block & 1)


def rows_kernel(own, fz, bits, mine, theirs, q_mine, q_theirs, *refs):
    coarse_out, fine_out, coarse_turned, fine_turned, out, q_out = refs[-6:]
    lead = lax.axis_index("slab") % 2 == 0
    kept = q_mine.shape[1]
    for g in range(q_mine.shape[0]):
        ours, others = q_mine[g], q_theirs[g]
        q_out[g, :kept] = jnp.where(lead, ours, others)
        q_out[g, kept:] = jnp.where(lead, others, ours)
    groups, held, total = mine.shape
    slabs = coarse_out.shape[1] // PACK
    height = 2 * held // slabs
    pieces = height // PACK
    det = out.shape[1]
    count = slabs * PACK
    shape = (slabs * own, count)
    w = lax.broadcasted_iota(jnp.int32, shape, 0)
    column = lax.broadcasted_iota(jnp.int32, shape, 1)
    block, row = column // PACK, column % PACK
    match = (row < own) & (w == slab_of(block, bits) * own + row)
    to_weight = jnp.where(match, 1.0, 0.0).astype(BF16)
    shape = (slabs * fz, count)
    z = lax.broadcasted_iota(jnp.int32, shape, 0)
    column = lax.broadcasted_iota(jnp.int32, shape, 1)
    to_fine = jnp.where(column == (z // fz) * PACK + own + z % fz, 1.0, 0.0).astype(BF16)
    for g in range(groups):
        own_rows, other_rows = mine[g].astype(F32), theirs[g].astype(F32)
        even = jnp.where(lead, own_rows, other_rows).astype(BF16)
        odd = jnp.where(lead, other_rows, own_rows).astype(BF16)
        cuts = []
        for p in range(pieces):
            blocks = [
                (even, odd)[j % 2][(j // 2) * height + p * PACK :][:PACK] for j in range(slabs)
            ]
            cuts.append(jnp.concatenate(blocks, axis=0))
        coarse = jnp.concatenate(cuts[: pieces // 2], axis=1)
        side = jnp.concatenate(cuts[pieces // 2 :], axis=1)
        fine = dot(to_fine, side, ((1,), (0,)))
        coarse_out[g] = coarse
        fine_out[g] = fine.astype(BF16)
        wide = coarse.astype(F32)
        for v in range(coarse.shape[1] // det):
            where = slice(v * det, (v + 1) * det)
            coarse_turned[g, v] = wide[:, where].T.astype(BF16)
            fine_turned[g, v] = fine[:, where].T.astype(BF16)
        out[g] = dot(to_weight, side, ((1,), (0,)))[:, :total]


def weights_kernel(fz, order, mine, received, *refs):
    coarse_out, fine_out = refs[-2:]
    held = mine.shape[0]
    slabs = 2 * held
    count = slabs * PACK
    parts = PACK // fz
    size = fine_out.shape[1]
    tiles = packed_tiles(size, fz)
    blocks = [(mine, received)[k // held].at[k % held] for k in order]
    for j, block in enumerate(blocks):
        coarse_out[j * PACK : (j + 1) * PACK] = block[:, :size]
    source = jnp.concatenate([block[:, size : size + tiles * LANES] for block in blocks], axis=0)
    shape = (slabs * fz, count)
    z = lax.broadcasted_iota(jnp.int32, shape, 0)
    column = lax.broadcasted_iota(jnp.int32, shape, 1)
    for k in range(parts):
        choose = jnp.where(column == (z // fz) * PACK + (z % fz) * parts + k, 1.0, 0.0)
        chosen = dot(choose.astype(BF16), source, ((1,), (0,)))
        for c in range(tiles):
            t = c * parts + k
            if t * LANES < size:
                fine_out[:, t * LANES : (t + 1) * LANES] = chosen[
                    :, c * LANES : (c + 1) * LANES
                ].astype(BF16)


def whole_rows(mine, received):
    lead = lax.axis_index("slab") % 2 == 0
    ours, others = mine.astype(F32), received.astype(F32)
    return jnp.concatenate(
        [jnp.where(lead, ours, others), jnp.where(lead, others, ours)], axis=0
    )


def residuals(q, deltas, weights):
    groups = q.shape[0]
    current = [q[g] for g in range(groups)]
    results = [[weights[g] * current[g] for g in range(groups)]]
    for mine, received in deltas:
        current = [current[g] - whole_rows(mine[g], received[g]) for g in range(groups)]
        results.append([weights[g] * current[g] for g in range(groups)])
    return results


def spread(depth, residual, views):
    det, columns = residual.shape[0], residual.shape[1] // views
    pieces = [
        dot(
            depth[:, v * det : (v + 1) * det],
            residual[:, v * columns : (v + 1) * columns],
            ((1,), (0,)),
        )
        for v in range(views)
    ]
    return jnp.concatenate(pieces, axis=1)


def spread_kernel(views, q, weights, fine_depth, coarse_depth, fine_out, coarse_out):
    for g in range(q.shape[0]):
        residual = (weights[g] * q[g]).astype(BF16)
        fine_out[g] = spread(fine_depth[g], residual, views).astype(BF16)
        coarse_out[g] = spread(coarse_depth[g], residual, views).astype(BF16)


def group_rays(held, part, g, cut):
    return jnp.concatenate([held[g][part, v, cut, :] for v in range(held[g].shape[1])], axis=1)


def step_kernel(groups, views, ready, *refs):
    refs = list(refs)
    if ready:
        spreads = [refs.pop(0), refs.pop(0)]
    else:
        q, mine, received, weights, fine_depth, coarse_depth = refs[:6]
        refs = refs[6:]
        residual = residuals(q, [(mine, received)], weights)[-1]
        residual = [r.astype(BF16) for r in residual]
        spreads = [
            [spread(depth[g], residual[g], views).astype(BF16) for g in range(groups)]
            for depth in (fine_depth, coarse_depth)
        ]
    turned = refs[:2]
    coarse_weights, fine_weights = refs[2:4]
    held = refs[4:-3]
    kept, given, scratch = refs[-3:]
    size = fine_weights.shape[1]
    columns = held[0].shape[3]
    chunk = min(size, 1024)
    results = [None] * groups
    for part in range(2):
        moments = [None] * groups
        for c in range(size // chunk):
            cut = slice(c * chunk, (c + 1) * chunk)
            if part == 0:
                weight = fine_weights[:, cut]
            else:
                weight = coarse_weights[:, cut]
            rays = [group_rays(held, part, g, cut) for g in range(groups)]
            back = dot(spreads[part][0], rays[0], ((1,), (1,)))
            for g in range(1, groups):
                back = back + dot(spreads[part][g], rays[g], ((1,), (1,)))
            change = (weight.astype(F32) * back).astype(BF16)
            for g in range(groups):
                moment = dot(change, rays[g], ((1,), (0,)))
                moments[g] = moment if moments[g] is None else moments[g] + moment
        for g in range(groups):
            moment = moments[g].astype(BF16)
            pieces = [
                dot(turned[part][g, v], moment[:, v * columns : (v + 1) * columns], ((1,), (0,)))
                for v in range(views)
            ]
            value = jnp.concatenate(pieces, axis=1)
            results[g] = value if results[g] is None else results[g] + value
    core = lax.axis_index("slab") % 2
    rows = kept.shape[1]
    for g in range(groups):
        scratch[g] = results[g]
        kept[g] = scratch[g, pl.ds(pl.multiple_of(core * rows, PACK), rows), :].astype(BF16)
        given[g] = scratch[g, pl.ds(pl.multiple_of((1 - core) * rows, PACK), rows), :].astype(BF16)


def add_kernel(bit, mine, received, out):
    for g in range(mine.shape[0]):
        out[g] = (mine[g].astype(F32) + received[g ^ bit].astype(F32)).astype(BF16)


def tail_kernel(fz, groups, views, q, *refs):
    deltas = [refs[:2], refs[2:4]]
    weights, fine_depth, coarse_depth = refs[4:7]
    held = refs[7:-2]
    ours, theirs = refs[-2:]
    size = held[0].shape[2]
    chunk = min(size, 1024)
    lead = lax.axis_index("slab") % 2 == 0
    history = residuals(q, deltas, weights)
    rows = (fz, PACK)
    spreads = ([], [])
    for g in range(groups):
        value = history[0][g]
        for other in history[1:]:
            value = value + other[g]
        high, low = in_two(value)
        fine_rows = fine_depth[g, : 2 * PACK].astype(F32)[: 2 * fz].astype(BF16)
        for part, depth in enumerate((fine_rows, coarse_depth[g, : 2 * PACK])):
            pair = in_two(spread(depth, high, views) + spread(depth, low, views))
            spreads[part].append(jnp.concatenate(pair, axis=0))
    backs = ([], [])
    for part in range(2):
        for c in range(size // chunk):
            cut = slice(c * chunk, (c + 1) * chunk)
            back = None
            for g in range(groups):
                value = dot(spreads[part][g], group_rays(held, part, g, cut), ((1,), (1,)))
                back = value if back is None else back + value
            backs[part].append(back[: 2 * rows[part]] + back[2 * rows[part] :])
    for out, first in ((ours, lead), (theirs, jnp.logical_not(lead))):
        parts = []
        for part in range(2):
            back = jnp.concatenate(backs[part], axis=1)
            parts.append(jnp.where(first, back[: rows[part]], back[rows[part] :]))
        out[:, :size] = parts[1].astype(BF16)
        out[:, size:] = pack_fine(parts[0]).astype(BF16)


def keep_kernel(blocks, out):
    out[...] = keep_row(blocks, 0, out.shape[1])


def final_kernel(groups, size, *refs):
    pieces = refs[: 2 * groups]
    fine, coarse, fw, cw, keep, fine_out, coarse_out = refs[2 * groups :]
    core = lax.axis_index("slab") % 2
    view = lax.axis_index("view")
    fz, cells = fine.shape
    for index, piece in enumerate(pieces):
        side = core if index < groups else 1 - core
        start = side * (cells // 2) + (view ^ (index % groups)) * size
        start = pl.multiple_of(start, LANES)
        where = pl.ds(start, size)
        change = piece[:, :size].astype(F32)
        coarse_out[:, where] = (coarse[:, where] + cw[:, where] * change) * keep[:, where]
        change = unpack_fine(piece[:, size:].astype(F32), fz, size)
        fine_out[:, where] = fine[:, where] + fw[:, where] * change


def make_body(slabs, groups):
    far_bits = [1 << k for k in range(slabs.bit_length() - 2, 1, -1)]
    view_bits = [1 << k for k in range(groups.bit_length() - 1)]

    def along_slab(value, bit):
        return swap(value, "slab", slabs, bit)

    def body(
        fine_volume,
        coarse_volume,
        fine_rays,
        coarse_rays,
        fine_axial,
        coarse_axial,
        measured,
        ray_weight,
        fine_cell_weight,
        coarse_cell_weight,
        margin_blocks,
        ray_hits,
    ):
        views, cells, columns = fine_rays.shape
        det = fine_axial.shape[2]
        fz, cz = fine_volume.shape[0], coarse_volume.shape[0]
        own = measured.shape[0]
        total = views * columns
        span = max(views * det, total)
        share = cells // 2 // groups
        lead = lax.axis_index("slab") % 2 == 0
        width = share + packed_tiles(share, fz) * LANES

        taken = in_hbm(
            fine_rays,
            coarse_rays,
            fine_volume,
            coarse_volume,
            fine_cell_weight,
            coarse_cell_weight,
            coarse_axial,
            measured,
            ray_weight,
        )
        height = PACK * ((views * det + span) // total)
        mine, theirs, rows, q, short, own_rays = call(
            start_kernel,
            "start",
            (
                shaped((PACK, width), BF16),
                shaped((PACK, width), BF16),
                shaped((height, total), BF16),
                shaped((det // 2, total), F32),
                shaped((det // 2, total), BF16),
                shaped((2, views, share, columns), BF16),
            ),
            [HBM] * 6 + [VMEM] + [HBM] * 5,
            scratch_like(*taken)
            + [
                pltpu.SMEM(margin_blocks.shape, jnp.int32),
                pltpu.SMEM(ray_hits.shape, jnp.int32),
                pltpu.VMEM((det, total), F32),
                pltpu.SemaphoreType.DMA((10,)),
                pltpu.SemaphoreType.DMA((4, 4)),
            ],
        )(*taken[:6], fine_axial, *taken[6:], *in_hbm(margin_blocks, ray_hits))

        def to_views(value):
            values = [value]
            for bit in view_bits:
                values += [swap(one, "view", groups, bit) for one in values]
            return values

        rows_half = det // 2
        got = {}

        def begin(stage, token):
            waits = [] if token is None else [token]
            if SOURCE["rays"] == stage:
                got["rays"] = []
                for bits in range(1, groups):
                    value = call(
                        functools.partial(take_kernel, groups, bits),
                        "take_rays",
                        shaped((2, views, share, columns), BF16),
                        [HBM] * 2 + [ANY] * len(waits),
                        [pltpu.SemaphoreType.DMA((2,))],
                    )(*in_hbm(fine_rays, coarse_rays), *waits)
                    got["rays"].append(swap(value, "view", groups, bits))
            for index, bit in enumerate(far_bits + [2]):
                if SOURCE["weights"][min(index, 2)] != stage:
                    continue
                if index == 0:
                    packed = call(
                        pair_kernel,
                        "pair",
                        shaped((2, PACK, width), BF16),
                        [VMEM] * 2 + [ANY] * len(waits),
                    )(mine, along_slab(theirs, 1), *waits)
                else:
                    packed, hop = got["weights"]
                    packed = call(
                        join_blocks_kernel,
                        "join_blocks",
                        shaped((2 * packed.shape[0], PACK, width), BF16),
                        [VMEM] * 2 + [ANY] * len(waits),
                    )(packed, hop, *waits)
                got["w%d" % index] = [along_slab(packed, bit)]
                got["weights"] = (packed, got["w%d" % index][0])

        def waits_of(stage):
            found = []
            for name, where in AWAITED.items():
                if where == stage:
                    found += got.get(name, [])
            return found

        begin("start", None)
        waits = waits_of("core")
        q, mixed = call(
            join_core_kernel,
            "join_core",
            (shaped((rows_half, total), F32), shaped((rows_half + height, total), BF16)),
            [VMEM] * 3 + [ANY] * len(waits),
        )(q, along_slab(short, 1), rows, *waits)
        begin("core", mixed)
        for index, bit in enumerate([2] + far_bits):
            last = index == len(far_bits)
            name = "last" if last else "hop%d" % index
            waits = waits_of(name)
            inputs = (q, mixed, along_slab(mixed, bit), *waits)
            specs = [VMEM] * 3 + [ANY] * len(waits)
            size = 2 * mixed.shape[0]
            if last:
                mixed = call(join_last_kernel, "join_last", shaped((size, total), BF16), specs)(
                    *inputs
                )
            else:
                q, mixed = call(
                    join_hop_kernel,
                    "join_hop",
                    (shaped(q.shape, F32), shaped((size - rows_half, total), BF16)),
                    specs,
                )(*inputs)
            begin(name, mixed)
        waits = waits_of("views")
        q, rows = call(
            functools.partial(join_views_kernel, rows_half),
            "join_views",
            (
                shaped((groups, rows_half, total), F32),
                shaped((groups, mixed.shape[0] - 2 * rows_half, total), BF16),
            ),
            [VMEM] * groups + [ANY] * len(waits),
        )(*to_views(mixed), *waits)
        count = len(far_bits)
        order = tuple(
            (j & 1) + 2 * (j >> 2) + (((j >> 1) & 1) << (count + 1)) for j in range(slabs)
        )
        waits = waits_of("rows")
        coarse_depth, fine_depth, coarse_turned, fine_turned, weights, q = call(
            functools.partial(rows_kernel, own, fz, [2] + far_bits),
            "unpack_rows",
            (
                shaped((groups, slabs * PACK, span), BF16),
                shaped((groups, slabs * fz, span), BF16),
                shaped((groups, views, det, slabs * PACK), BF16),
                shaped((groups, views, det, slabs * fz), BF16),
                shaped((groups, det, total), F32),
                shaped((groups, det, total), F32),
            ),
            [VMEM] * 4 + [ANY] * len(waits),
        )(rows, along_slab(rows, 1), q, along_slab(q, 1), *waits)
        spreads = call(
            functools.partial(spread_kernel, views),
            "spread",
            (
                shaped((groups, slabs * fz, total), BF16),
                shaped((groups, slabs * PACK, total), BF16),
            ),
            [VMEM] * 4,
        )(q, weights, fine_depth, coarse_depth)
        coarse_weights, fine_weights = call(
            functools.partial(weights_kernel, fz, order),
            "unpack_weights",
            (shaped((slabs * PACK, share), BF16), shaped((slabs * fz, share), BF16)),
            [VMEM] * 2 + [ANY] * len(spreads),
        )(*got["weights"], *spreads)
        rays = [own_rays] + got["rays"]
        held = (fine_turned, coarse_turned, coarse_weights, fine_weights, *rays)
        def add(mine, received, bit):
            return call(
                functools.partial(add_kernel, bit),
                "add",
                shaped((groups, rows_half, total), BF16),
                [VMEM] * 2,
            )(mine, received)

        deltas = []
        for ready, inputs in ((True, spreads), (False, None)):
            if not ready:
                inputs = (q, *deltas, weights, fine_depth, coarse_depth)
            delta, given = call(
                functools.partial(step_kernel, groups, views, ready),
                "ray_space_step",
                (shaped((groups, rows_half, total), BF16),) * 2,
                [VMEM] * (len(inputs) + len(held)),
                [pltpu.VMEM((groups, det, total), F32)],
            )(*inputs, *held)
            delta = add(delta, along_slab(given, 1), 0)
            for bit in view_bits:
                delta = add(delta, swap(delta, "view", groups, bit), bit)
            deltas += [delta, along_slab(delta, 1)]
        inputs = (q, *deltas, weights, fine_depth, coarse_depth, *rays)
        ours, theirs = call(
            functools.partial(tail_kernel, fz, groups, views),
            "back_projection",
            (shaped((PACK, width), BF16),) * 2,
            [VMEM] * len(inputs),
        )(*inputs)
        keep = call(keep_kernel, "keep", shaped((1, cells), F32), [SMEM])(margin_blocks)
        both = ("slab", "view")
        pieces = [ours] + [swap(ours, "view", groups, bits) for bits in range(1, groups)]
        pieces += [swap(theirs, both, slabs * groups, groups | bits) for bits in range(groups)]
        return call(
            functools.partial(final_kernel, groups, share),
            "update",
            (shaped(fine_volume.shape, F32), shaped(coarse_volume.shape, F32)),
            [VMEM] * (2 * groups + 5),
        )(
            *pieces,
            fine_volume,
            coarse_volume,
            fine_cell_weight,
            coarse_cell_weight,
            keep,
        )

    return body


def solution(mesh):
    return jax.shard_map(
        make_body(mesh.shape["slab"], mesh.shape["view"]),
        mesh=mesh,
        in_specs=(
            P("slab", None),
            P("slab", None),
            P("view", None, None),
            P("view", None, None),
            P("view", "slab", None),
            P("view", "slab", None),
            P("slab", "view", None),
            P("slab", "view", None),
            P("slab", None),
            P("slab", None),
            P("slab", None),
            P("view", "slab", None),
        ),
        out_specs=(P("slab", None), P("slab", None)),
        check_vma=False,
    )
```
